32 devices in a mesh: dp: 8 (over y, x, core), fsdp: 4 (over z).
Axes of the slice: x: 2, y: 2, z: 4, core: 2. Of those that a mesh axis runs over, the one named last changes fastest.
Arguments:
- source: bfloat16 [32768, 512], P(('dp', 'fsdp')), may hold values from -6 to 6
- target: bfloat16 [32768, 512], P(('dp', 'fsdp')), may hold values from -6 to 6
- source_segments: int32 [64, 512], P(('dp', 'fsdp')), may hold values from 0 to 7, never falling along the last dimension, each value on 1 to 256 neighbouring positions
- target_segments: int32 [64, 512], P(('dp', 'fsdp')), may hold values from 0 to 7, never falling along the last dimension, each value on 1 to 256 neighbouring positions
- target_language: int32 [64, 8], P(('dp', 'fsdp')), may hold values from 0 to 7
- cotangent: bfloat16 [32768, 512], P(('dp', 'fsdp')), may hold values from -6 to 6
- enc_qkv: bfloat16 [512, 1536], P(('dp', 'fsdp')), may hold values from -0.25 to 0.25
- enc_out: bfloat16 [512, 512], P(('dp', 'fsdp')), may hold values from -0.5 to 0.5
- enc_up: bfloat16 [512, 2048], P(('dp', 'fsdp')), may hold values from -0.25 to 0.25
- enc_down: bfloat16 [2048, 512], P(('dp', 'fsdp')), may hold values from -0.125 to 0.125
- enc_vecs: bfloat16 [512, 8], P(('dp', 'fsdp')), may hold values from -1.2 to 1.45, as said below
- enc_bias_up: bfloat16 [2048], P(('dp', 'fsdp')), may hold values from -2 to 2
- dec_qkv: bfloat16 [512, 1536], P(('dp', 'fsdp')), may hold values from -0.25 to 0.25
- dec_out: bfloat16 [512, 512], P(('dp', 'fsdp')), may hold values from -0.5 to 0.5
- cross_q: bfloat16 [512, 512], P(('dp', 'fsdp')), may hold values from -0.25 to 0.25
- cross_kv: bfloat16 [512, 1024], P(('dp', 'fsdp')), may hold values from -0.25 to 0.25
- cross_out: bfloat16 [512, 512], P(('dp', 'fsdp')), may hold values from -0.5 to 0.5
- dec_up: bfloat16 [512, 2048], P(('dp', 'fsdp')), may hold values from -0.25 to 0.25
- dec_down: bfloat16 [2048, 512], P(('dp', 'fsdp')), may hold values from -0.125 to 0.125
- dec_vecs: bfloat16 [512, 13], P(('dp', 'fsdp')), may hold values from -1.2 to 1.45, as said below
- dec_bias_up: bfloat16 [2048], P(('dp', 'fsdp')), may hold values from -2 to 2
- lang_table: bfloat16 [512, 8], P(('dp', 'fsdp')), may hold values from -4 to 4
Outputs:
- dec_output: bfloat16 [32768, 512], P(('dp', 'fsdp'))
- source_grad: bfloat16 [32768, 512], P(('dp', 'fsdp'))
- target_grad: bfloat16 [32768, 512], P(('dp', 'fsdp'))
- enc_qkv_grad: float32 [512, 1536], P(('dp', 'fsdp'))
- enc_out_grad: float32 [512, 512], P(('dp', 'fsdp'))
- enc_up_grad: float32 [512, 2048], P(('dp', 'fsdp'))
- enc_down_grad: float32 [2048, 512], P(('dp', 'fsdp'))
- enc_vecs_grad: float32 [512, 8], P(('dp', 'fsdp'))
- enc_bias_up_grad: float32 [2048], P(('dp', 'fsdp'))
- dec_qkv_grad: float32 [512, 1536], P(('dp', 'fsdp'))
- dec_out_grad: float32 [512, 512], P(('dp', 'fsdp'))
- cross_q_grad: float32 [512, 512], P(('dp', 'fsdp'))
- cross_kv_grad: float32 [512, 1024], P(('dp', 'fsdp'))
- cross_out_grad: float32 [512, 512], P(('dp', 'fsdp'))
- dec_up_grad: float32 [512, 2048], P(('dp', 'fsdp'))
- dec_down_grad: float32 [2048, 512], P(('dp', 'fsdp'))
- dec_vecs_grad: float32 [512, 13], P(('dp', 'fsdp'))
- dec_bias_up_grad: float32 [2048], P(('dp', 'fsdp'))
- lang_table_grad: float32 [512, 8], P(('dp', 'fsdp'))
The draws below stay inside these ranges and needn't reach their ends.
Inputs may be any that keep to these rules, and one draw needn't show every extreme that they name: `source_segments`: within each row the numbers never fall; each of the 8 sentences holds 1 to 256 positions, and one holds exactly 256. `target_segments`: within each row the numbers never fall; each of the 8 sentences holds 1 to 256 positions, and one holds exactly 256. `enc_vecs`: columns 3 and 6 are gains, the others biases. `dec_vecs`: columns 3, 8 and 11 are gains, the others biases.
All inputs are finite; a program needn't handle non-finite values.
Results may differ from the reference program's by a relative error of at most 0.023.
Values may be sent and summed in bfloat16 or wider, within the bound.
No kernel may reach another device: no remote copies, remote signals or barrier semaphores. Data moves between devices by JAX's collectives and lax.ppermute only.
A program may use at most 256 MiB of HBM per device.

```python
import math
import jax
import jax.numpy as jnp
import numpy as np
from jax import lax

D = 512
HDIM = 64
FF = 2048
LANGS = 8
LEN = 512
SEGS = 8
SEG_MOST = 256
ROWS = 64
TOKENS = 32768


def vector_columns(key, gain_list):
    gain_mask = jnp.asarray(np.array(gain_list, dtype=np.float32))
    normal = jnp.clip(jax.random.normal(key, (D, len(gain_list)), jnp.float32), -2.9, 2.9)
    return (gain_mask * (1.0 + 0.15 * normal) + (1.0 - gain_mask) * (0.4 * normal)).astype(jnp.bfloat16)


def draw_enc_vecs(key, part):
    return vector_columns(jax.random.fold_in(key, 11), [0, 0, 0, 1, 0, 0, 1, 0])


def draw_dec_vecs(key, part):
    return vector_columns(jax.random.fold_in(key, 23), [0, 0, 0, 1, 0, 0, 0, 0, 1, 0, 0, 1, 0])


def set_ends(values, own_key, smallest, high):
    longest = values.shape.index(max(values.shape))
    spots = []
    for shift in (0, 1):
        where = [jax.random.randint(jax.random.fold_in(own_key, axis), (), 0, length) for axis, length in enumerate(values.shape)]
        where[longest] = (where[longest] + shift) % values.shape[longest]
        spots.append(tuple(where))
    return values.at[spots[0]].set(smallest).at[spots[1]].set(high)


def block_levels(stream_key, extent, split, smallest, largest):
    level = 1.0
    for axis_at, parts in split:
        steps = jax.random.uniform(jax.random.fold_in(jax.random.fold_in(stream_key, 6), axis_at), (parts,), jnp.float32, smallest / len(split), largest / len(split))
        level = level * jnp.repeat(jnp.exp(steps), extent[axis_at] // parts).reshape((-1,) + (1,) * (len(extent) - 1 - axis_at))
    return level


def split_up(number_of, total, most, skew):
    weights = [(1 << 20) // math.isqrt(grade ** skew) + 1 for grade in range(2, number_of + 1)]
    spare, given = total - most - (number_of - 1), [1] * (number_of - 1)
    while spare > 0:
        candidates = [i for i in range(number_of - 1) if given[i] < most]
        whole, remaining = sum([weights[i] for i in candidates]), spare
        for i in candidates:
            addition = min(most - given[i], max(1, remaining * weights[i] // whole), spare)
            given[i] = given[i] + addition
            spare = spare - addition
    return np.array([most] + given)


def ragged(key, amount, total, reach, skew):
    if amount == 2:
        one = jax.random.randint(key, (), max(1, total - reach), min(reach, total - 1) + 1)
        return jnp.stack([one, total - one])
    tallies = jnp.asarray(split_up(amount, total, reach, skew), jnp.int32)
    couples = (amount - 1) // 2
    donor, sink = tallies[1:1 + 2 * couples:2], tallies[2:2 + 2 * couples:2]
    slack = jnp.minimum(donor - 1, reach - sink)
    passed = jax.random.randint(jax.random.fold_in(key, 1), (couples,), 0, 1 << 20) % (slack + 1)
    tallies = tallies.at[1:1 + 2 * couples:2].set(donor - passed).at[2:2 + 2 * couples:2].set(sink + passed)
    return tallies[jax.random.permutation(jax.random.fold_in(key, 2), amount)]


def noise(key, dims, deviation, limit, cuts=(), held_as=jnp.bfloat16):
    level = block_levels(key, dims, cuts, -0.22, 0.18) if cuts else 1.0
    values = jax.random.normal(key, dims, jnp.float32) * deviation * level
    return jnp.minimum(jnp.maximum(values, -limit), limit).astype(held_as)


def setup_inputs(seed: int = 0) -> dict:
    streams_of = jax.random.split(jax.random.key(seed), 23)
    return {
        "source": noise(streams_of[0], (TOKENS, D), 1.0, 6.0, ((0, 32),)),
        "target": noise(streams_of[1], (TOKENS, D), 1.0, 6.0, ((0, 32),)),
        "source_segments": jax.vmap(lambda own: jnp.searchsorted(jnp.cumsum(ragged(own, SEGS, LEN, SEG_MOST, 1)), jnp.arange(LEN), side="right"))(jax.random.split(streams_of[2], ROWS)).reshape((ROWS, LEN)).astype(jnp.int32),
        "target_segments": jax.vmap(lambda own: jnp.searchsorted(jnp.cumsum(ragged(own, SEGS, LEN, SEG_MOST, 1)), jnp.arange(LEN), side="right"))(jax.random.split(streams_of[3], ROWS)).reshape((ROWS, LEN)).astype(jnp.int32),
        "target_language": set_ends(jax.random.randint(streams_of[4], (ROWS, SEGS), 0, LANGS), jax.random.fold_in(streams_of[4], 1), 0, LANGS - 1).astype(jnp.int32),
        "cotangent": noise(streams_of[5], (TOKENS, D), 1.0, 6.0, ((0, 32),)),
        "enc_qkv": noise(streams_of[6], (D, 3 * D), D ** -0.5, 0.25, ((0, 32),)),
        "enc_out": noise(streams_of[7], (D, D), (D // 4) ** -0.5, 0.5, ((0, 32),)),
        "enc_up": noise(streams_of[8], (D, FF), D ** -0.5, 0.25, ((0, 32),)),
        "enc_down": noise(streams_of[9], (FF, D), FF ** -0.5, 0.125, ((0, 32),)),
        "enc_vecs": draw_enc_vecs(jax.random.fold_in(streams_of[22], 71), 0),
        "enc_bias_up": noise(streams_of[11], (FF,), 0.5, 2.0, ((0, 32),)),
        "dec_qkv": noise(streams_of[12], (D, 3 * D), D ** -0.5, 0.25, ((0, 32),)),
        "dec_out": noise(streams_of[13], (D, D), (D // 4) ** -0.5, 0.5, ((0, 32),)),
        "cross_q": noise(streams_of[14], (D, D), D ** -0.5, 0.25, ((0, 32),)),
        "cross_kv": noise(streams_of[15], (D, 2 * D), D ** -0.5, 0.25, ((0, 32),)),
        "cross_out": noise(streams_of[16], (D, D), (D // 4) ** -0.5, 0.5, ((0, 32),)),
        "dec_up": noise(streams_of[17], (D, FF), D ** -0.5, 0.25, ((0, 32),)),
        "dec_down": noise(streams_of[18], (FF, D), FF ** -0.5, 0.125, ((0, 32),)),
        "dec_vecs": draw_dec_vecs(jax.random.fold_in(streams_of[22], 71), 0),
        "dec_bias_up": noise(streams_of[20], (FF,), 0.5, 2.0, ((0, 32),)),
        "lang_table": noise(streams_of[21], (D, LANGS), 1.0, 4.0, ((0, 32),)),
    }


@jax.custom_vjp
def low(v):
    return lax.optimization_barrier(v.astype(jnp.bfloat16)).astype(jnp.float32)

@jax.custom_vjp
def low_back(v):
    return v

def low_keep(v):
    return (low(v), None)

def low_pass(kept, grad):
    return (grad,)

def back_keep(v):
    return (v, None)

def back_low(kept, grad):
    return (low(grad),)
low.defvjp(low_keep, low_pass)
low_back.defvjp(back_keep, back_low)
highest = lax.Precision.HIGHEST
scale_dot = 0.125
norm_eps = 1e-05
masked_score = -1000000000.0

def matmul(left_operand, right_operand):
    return jnp.dot(left_operand, right_operand, precision=highest, preferred_element_type=jnp.float32)

def layer_norm(summed, norm_gain, norm_shift):
    centred = summed - lax.optimization_barrier(jnp.mean(summed, axis=-1, keepdims=True))
    variance = lax.optimization_barrier(jnp.mean(centred * centred, axis=-1, keepdims=True))
    return centred * lax.rsqrt(variance + norm_eps) * norm_gain + norm_shift

def attention(queries, key_rows, value_rows, allowed):
    query_heads = queries.reshape(queries.shape[0], -1, HDIM)
    key_heads = key_rows.reshape(key_rows.shape[0], -1, HDIM)
    value_heads = value_rows.reshape(value_rows.shape[0], -1, HDIM)
    scores = jnp.einsum('qhd,khd->hqk', query_heads, key_heads, precision=highest) * scale_dot
    scores = low_back(jnp.where(allowed[None], scores, jnp.float32(masked_score)))
    weights = low(jax.nn.softmax(scores, axis=-1))
    mixed_rows = jnp.einsum('hqk,khd->qhd', weights, value_heads, precision=highest)
    return mixed_rows.reshape(queries.shape[0], -1)

def attend_block(residual, query_low, memory_low, query_weight, memory_weight, out_weight, query_bias, value_bias, out_bias, norm_gain, norm_shift, allowed):
    model_width = query_weight.shape[1]
    queries = low(low_back(matmul(query_low, query_weight) + query_bias))
    key_zeros = jnp.zeros(value_bias.shape, jnp.float32)
    memory = low(low_back(matmul(memory_low, memory_weight) + jnp.concatenate([key_zeros, value_bias])))
    mixed_rows = low(low_back(attention(queries, memory[:, :model_width], memory[:, model_width:], allowed)))
    branch = low_back(matmul(mixed_rows, out_weight) + out_bias)
    return layer_norm(residual + branch, norm_gain, norm_shift)

def feed_block(residual, up_weight, up_bias, down_weight, down_bias, norm_gain, norm_shift):
    hidden = low_back(matmul(low(residual), up_weight) + up_bias)
    active = low(jax.nn.gelu(hidden, approximate=True))
    branch = low_back(matmul(active, down_weight) + down_bias)
    return layer_norm(residual + branch, norm_gain, norm_shift)

def row_forward(weights, row_items):
    enc_qkv, enc_out, enc_up, enc_down, enc_vecs, enc_bias_up, dec_qkv, dec_out, cross_q, cross_kv, cross_out, dec_up, dec_down, dec_vecs, dec_bias_up, lang_table = weights
    source_row, target_row, source_seg, target_seg, language_row = row_items
    model_width = enc_qkv.shape[0]
    source_seg = source_seg.astype(jnp.int32)
    target_seg = target_seg.astype(jnp.int32)
    language_row = language_row.astype(jnp.int32)
    same_source = source_seg[:, None] == source_seg[None, :]
    same_target = target_seg[:, None] == target_seg[None, :]
    same_cross = target_seg[:, None] == source_seg[None, :]
    seg_hot = (target_seg[:, None] == jnp.arange(SEGS, dtype=jnp.int32)[None, :]).astype(jnp.float32)
    lang_hot = (language_row[:, None] == jnp.arange(LANGS, dtype=jnp.int32)[None, :]).astype(jnp.float32)
    token_language = matmul(seg_hot, lang_hot)
    target_in = target_row + matmul(token_language, lang_table.T)
    source_low = low(source_row)
    enc_first = attend_block(source_row, source_low, source_low, enc_qkv[:, :model_width], enc_qkv[:, model_width:], enc_out, enc_vecs[:, 0], enc_vecs[:, 1], enc_vecs[:, 2], enc_vecs[:, 3], enc_vecs[:, 4], same_source)
    encoded = feed_block(enc_first, enc_up, enc_bias_up, enc_down, enc_vecs[:, 5], enc_vecs[:, 6], enc_vecs[:, 7])
    target_low = low(target_in)
    first_out = attend_block(target_in, target_low, target_low, dec_qkv[:, :model_width], dec_qkv[:, model_width:], dec_out, dec_vecs[:, 0], dec_vecs[:, 1], dec_vecs[:, 2], dec_vecs[:, 3], dec_vecs[:, 4], same_target)
    second_out = attend_block(first_out, low(first_out), low(encoded), cross_q, cross_kv, cross_out, dec_vecs[:, 5], dec_vecs[:, 6], dec_vecs[:, 7], dec_vecs[:, 8], dec_vecs[:, 9], same_cross)
    return feed_block(second_out, dec_up, dec_bias_up, dec_down, dec_vecs[:, 10], dec_vecs[:, 11], dec_vecs[:, 12])

def reference(source, target, source_segments, target_segments, target_language, cotangent, enc_qkv, enc_out, enc_up, enc_down, enc_vecs, enc_bias_up, dec_qkv, dec_out, cross_q, cross_kv, cross_out, dec_up, dec_down, dec_vecs, dec_bias_up, lang_table):
    weights = tuple((weight_part.astype(jnp.float32) for weight_part in (enc_qkv, enc_out, enc_up, enc_down, enc_vecs, enc_bias_up, dec_qkv, dec_out, cross_q, cross_kv, cross_out, dec_up, dec_down, dec_vecs, dec_bias_up, lang_table)))
    source_rows = source.astype(jnp.float32).reshape(ROWS, LEN, D)
    target_rows = target.astype(jnp.float32).reshape(ROWS, LEN, D)

    def forward(weights_now, sources, targets):

        def one_row(row_items):
            return row_forward(weights_now, row_items)
        return lax.map(jax.checkpoint(one_row), (sources, targets, source_segments, target_segments, target_language))
    output, pullback = jax.vjp(forward, weights, source_rows, target_rows)
    grad_weights, grad_source, grad_target = pullback(cotangent.astype(jnp.float32).reshape(ROWS, LEN, D))
    grad_enc_qkv, grad_enc_out, grad_enc_up, grad_enc_down, grad_enc_vecs, grad_enc_bias_up, grad_dec_qkv, grad_dec_out, grad_cross_q, grad_cross_kv, grad_cross_out, grad_dec_up, grad_dec_down, grad_dec_vecs, grad_dec_bias_up, grad_lang = grad_weights
    return (output.reshape(TOKENS, D).astype(jnp.bfloat16), grad_source.reshape(TOKENS, D).astype(jnp.bfloat16), grad_target.reshape(TOKENS, D).astype(jnp.bfloat16), grad_enc_qkv, grad_enc_out, grad_enc_up, grad_enc_down, grad_enc_vecs, grad_enc_bias_up, grad_dec_qkv, grad_dec_out, grad_cross_q, grad_cross_kv, grad_cross_out, grad_dec_up, grad_dec_down, grad_dec_vecs, grad_dec_bias_up, grad_lang)
```

```python
import functools

import jax
import jax.numpy as jnp
from jax import lax
from jax.experimental import pallas as pl
from jax.experimental.pallas import tpu as pltpu
from jax.sharding import PartitionSpec as P

HDIM = 64
LANGS = 8


scale_dot = 0.125
norm_eps = 1e-05
masked_score = -1000000000.0
highest = lax.Precision.HIGHEST


def low_dot(left_operand, right_operand):
    return jnp.dot(left_operand, right_operand, preferred_element_type=jnp.float32)


def rows_inner(left_operand, right_operand):
    return lax.dot_general(
        left_operand, right_operand, (((0,), (0,)), ((), ())), preferred_element_type=jnp.float32
    )


def right_inner(left_operand, right_operand):
    return lax.dot_general(
        left_operand, right_operand, (((1,), (1,)), ((), ())), preferred_element_type=jnp.float32
    )


def column_sum(matrix_rows):
    return jnp.sum(matrix_rows, axis=0, dtype=jnp.float32)


def project(inputs_low, weight_part, bias_row):
    return (low_dot(inputs_low, weight_part) + bias_row).astype(jnp.bfloat16)


def smooth_gate(hidden):
    return jax.nn.gelu(hidden, approximate=True)


def norm_forward(summed, norm_gain, norm_shift):
    centred = summed - jnp.mean(summed, axis=-1, keepdims=True)
    inverse = lax.rsqrt(jnp.mean(centred * centred, axis=-1, keepdims=True) + norm_eps)
    normed = centred * inverse
    return (normed * norm_gain + norm_shift, (normed, inverse))


def norm_backward(grad_out, norm_gain, norm_saved):
    normed, inverse = norm_saved
    grad_gain = jnp.sum(grad_out * normed, axis=0)
    grad_shift = jnp.sum(grad_out, axis=0)
    scaled = grad_out * norm_gain
    grad_input = inverse * (
        scaled
        - jnp.mean(scaled, axis=-1, keepdims=True)
        - normed * jnp.mean(scaled * normed, axis=-1, keepdims=True)
    )
    return (grad_input, grad_gain, grad_shift)


def split_heads(matrix_rows):
    return matrix_rows.reshape(matrix_rows.shape[0], -1, HDIM)


def merge_heads(head_rows):
    return head_rows.reshape(head_rows.shape[0], -1)


def score_block(queries, key_rows, allowed):
    scores = (
        jnp.einsum(
            "qhd,khd->hqk",
            split_heads(queries),
            split_heads(key_rows),
            preferred_element_type=jnp.float32,
        )
        * scale_dot
    )
    return jnp.where(allowed[None], scores, masked_score)


def attend_forward(queries, key_rows, value_rows, allowed):
    scores = score_block(queries, key_rows, allowed)
    top_score = jnp.max(scores, axis=-1, keepdims=True)
    powers = jnp.exp(scores - top_score)
    totals = jnp.sum(powers, axis=-1, keepdims=True)
    weights = (powers / totals).astype(jnp.bfloat16)
    mixed_rows = jnp.einsum(
        "hqk,khd->qhd", weights, split_heads(value_rows), preferred_element_type=jnp.float32
    )
    return (merge_heads(mixed_rows).astype(jnp.bfloat16), top_score + jnp.log(totals))


def attend_backward(grad_mixed, queries, key_rows, value_rows, allowed, log_totals):
    probs_now = jnp.exp(score_block(queries, key_rows, allowed) - log_totals)
    grad_heads = split_heads(grad_mixed)
    grad_values = jnp.einsum(
        "hqk,qhd->khd",
        probs_now.astype(jnp.bfloat16),
        grad_heads,
        preferred_element_type=jnp.float32,
    )
    grad_probs = jnp.einsum(
        "qhd,khd->hqk", grad_heads, split_heads(value_rows), preferred_element_type=jnp.float32
    )
    weighted = jnp.sum(probs_now * grad_probs, axis=-1, keepdims=True)
    grad_scores = (probs_now * (grad_probs - weighted)).astype(jnp.bfloat16)
    grad_queries = (
        jnp.einsum(
            "hqk,khd->qhd", grad_scores, split_heads(key_rows), preferred_element_type=jnp.float32
        )
        * scale_dot
    )
    grad_keys = (
        jnp.einsum(
            "hqk,qhd->khd", grad_scores, split_heads(queries), preferred_element_type=jnp.float32
        )
        * scale_dot
    )
    return (
        merge_heads(grad_queries).astype(jnp.bfloat16),
        merge_heads(grad_keys).astype(jnp.bfloat16),
        merge_heads(grad_values).astype(jnp.bfloat16),
    )


def attend_sublayer(
    residual, queries, key_rows, value_rows, out_weight, out_bias, norm_gain, norm_shift, allowed
):
    mixed_rows, log_totals = attend_forward(queries, key_rows, value_rows, allowed)
    branch = low_dot(mixed_rows, out_weight) + out_bias
    normed_out, norm_saved = norm_forward(residual + branch, norm_gain, norm_shift)
    return (normed_out, (queries, key_rows, value_rows, log_totals, mixed_rows, norm_saved))


def attend_sublayer_back(grad_out, out_weight, norm_gain, allowed, stored):
    queries, key_rows, value_rows, log_totals, mixed_rows, norm_saved = stored
    grad_sum, grad_gain, grad_shift = norm_backward(grad_out, norm_gain, norm_saved)
    grad_branch = grad_sum.astype(jnp.bfloat16)
    grad_mixed = right_inner(grad_branch, out_weight).astype(jnp.bfloat16)
    grad_queries, grad_keys, grad_values = attend_backward(
        grad_mixed, queries, key_rows, value_rows, allowed, log_totals
    )
    extras = (rows_inner(mixed_rows, grad_branch), column_sum(grad_branch), grad_gain, grad_shift)
    return (grad_sum, grad_queries, grad_keys, grad_values, extras)


def feed_forward(residual, up_weight, up_bias, down_weight, down_bias, norm_gain, norm_shift):
    inputs_low = residual.astype(jnp.bfloat16)
    hidden = low_dot(inputs_low, up_weight) + up_bias
    active = smooth_gate(hidden).astype(jnp.bfloat16)
    branch = low_dot(active, down_weight) + down_bias
    normed_out, norm_saved = norm_forward(residual + branch, norm_gain, norm_shift)
    return (normed_out, (inputs_low, hidden, active, norm_saved))


def feed_back(grad_out, up_weight, down_weight, norm_gain, stored):
    inputs_low, hidden, active, norm_saved = stored
    grad_sum, grad_gain, grad_shift = norm_backward(grad_out, norm_gain, norm_saved)
    grad_branch = grad_sum.astype(jnp.bfloat16)
    grad_active = right_inner(grad_branch, down_weight)
    gate_value, gate_pull = jax.vjp(smooth_gate, hidden)
    grad_hidden = gate_pull(grad_active)[0].astype(jnp.bfloat16)
    grad_input = grad_sum + right_inner(grad_hidden, up_weight)
    grads = (
        rows_inner(inputs_low, grad_hidden),
        column_sum(grad_hidden),
        rows_inner(active, grad_branch),
        column_sum(grad_branch),
        grad_gain,
        grad_shift,
    )
    return (grad_input, grads)


def row_masks(source_seg, target_seg):
    same_source = source_seg[:, None] == source_seg[None, :]
    same_target = target_seg[:, None] == target_seg[None, :]
    same_cross = target_seg[:, None] == source_seg[None, :]
    return (same_source, same_target, same_cross)


def language_rows(target_seg, language_row):
    seg_hot = (
        target_seg[:, None] == jnp.arange(language_row.shape[0], dtype=jnp.int32)[None, :]
    ).astype(jnp.float32)
    lang_hot = (language_row[:, None] == jnp.arange(LANGS, dtype=jnp.int32)[None, :]).astype(
        jnp.float32
    )
    return jnp.dot(seg_hot, lang_hot, precision=highest, preferred_element_type=jnp.float32)


def encoder_forward(enc_whole, source_row, same_source):
    qkv_weight, out_weight, up_weight, down_weight, vectors, up_bias = enc_whole
    columns = vectors.astype(jnp.float32)
    model_width = qkv_weight.shape[0]
    qkv_bias = jnp.concatenate(
        [columns[:, 0], jnp.zeros((model_width,), jnp.float32), columns[:, 1]]
    )
    qkv_rows = project(source_row, qkv_weight, qkv_bias)
    first_out, attend_stored = attend_sublayer(
        source_row.astype(jnp.float32),
        qkv_rows[:, :model_width],
        qkv_rows[:, model_width : 2 * model_width],
        qkv_rows[:, 2 * model_width :],
        out_weight,
        columns[:, 2],
        columns[:, 3],
        columns[:, 4],
        same_source,
    )
    encoded, feed_stored = feed_forward(
        first_out,
        up_weight,
        up_bias.astype(jnp.float32),
        down_weight,
        columns[:, 5],
        columns[:, 6],
        columns[:, 7],
    )
    return (encoded, (source_row, attend_stored, feed_stored))


def encoder_backward(enc_whole, grad_encoded, same_source, stored):
    qkv_weight, out_weight, up_weight, down_weight, vectors, up_bias = enc_whole
    columns = vectors.astype(jnp.float32)
    source_low, attend_stored, feed_stored = stored
    grad_first, feed_grads = feed_back(
        grad_encoded, up_weight, down_weight, columns[:, 6], feed_stored
    )
    grad_sum, grad_queries, grad_keys, grad_values, extras = attend_sublayer_back(
        grad_first, out_weight, columns[:, 3], same_source, attend_stored
    )
    grad_qkv = jnp.concatenate([grad_queries, grad_keys, grad_values], axis=1)
    grad_source = grad_sum + right_inner(grad_qkv, qkv_weight)
    vector_grads = jnp.stack(
        [
            column_sum(grad_queries),
            column_sum(grad_values),
            extras[1],
            extras[2],
            extras[3],
            feed_grads[3],
            feed_grads[4],
            feed_grads[5],
        ],
        axis=1,
    )
    grads = (
        rows_inner(source_low, grad_qkv),
        extras[0],
        feed_grads[0],
        feed_grads[2],
        vector_grads,
        feed_grads[1],
    )
    return (grads, grad_source)


def decoder_forward(dec_whole, target_row, encoded_low, token_language, masks):
    (
        qkv_weight,
        out_weight,
        query_weight,
        memory_weight,
        cross_weight,
        up_weight,
        down_weight,
        vectors,
        up_bias,
        language_table,
    ) = dec_whole
    same_source, same_target, same_cross = masks
    columns = vectors.astype(jnp.float32)
    model_width = qkv_weight.shape[0]
    target_in = target_row.astype(jnp.float32) + right_inner(
        token_language.astype(jnp.bfloat16), language_table
    )
    target_low = target_in.astype(jnp.bfloat16)
    qkv_bias = jnp.concatenate(
        [columns[:, 0], jnp.zeros((model_width,), jnp.float32), columns[:, 1]]
    )
    qkv_rows = project(target_low, qkv_weight, qkv_bias)
    first_out, self_stored = attend_sublayer(
        target_in,
        qkv_rows[:, :model_width],
        qkv_rows[:, model_width : 2 * model_width],
        qkv_rows[:, 2 * model_width :],
        out_weight,
        columns[:, 2],
        columns[:, 3],
        columns[:, 4],
        same_target,
    )
    first_low = first_out.astype(jnp.bfloat16)
    queries = project(first_low, query_weight, columns[:, 5])
    memory = project(
        encoded_low,
        memory_weight,
        jnp.concatenate([jnp.zeros((model_width,), jnp.float32), columns[:, 6]]),
    )
    second_out, cross_stored = attend_sublayer(
        first_out,
        queries,
        memory[:, :model_width],
        memory[:, model_width:],
        cross_weight,
        columns[:, 7],
        columns[:, 8],
        columns[:, 9],
        same_cross,
    )
    output, feed_stored = feed_forward(
        second_out,
        up_weight,
        up_bias.astype(jnp.float32),
        down_weight,
        columns[:, 10],
        columns[:, 11],
        columns[:, 12],
    )
    return (output, (target_low, first_low, self_stored, cross_stored, feed_stored))


def decoder_backward(dec_whole, grad_output, encoded_low, token_language, masks, stored):
    (
        qkv_weight,
        out_weight,
        query_weight,
        memory_weight,
        cross_weight,
        up_weight,
        down_weight,
        vectors,
        up_bias,
        language_table,
    ) = dec_whole
    same_source, same_target, same_cross = masks
    columns = vectors.astype(jnp.float32)
    target_low, first_low, self_stored, cross_stored, feed_stored = stored
    grad_second, feed_grads = feed_back(
        grad_output, up_weight, down_weight, columns[:, 11], feed_stored
    )
    cross_sum, cross_queries, cross_keys, cross_values, cross_extras = attend_sublayer_back(
        grad_second, cross_weight, columns[:, 8], same_cross, cross_stored
    )
    grad_memory = jnp.concatenate([cross_keys, cross_values], axis=1)
    grad_first = cross_sum + right_inner(cross_queries, query_weight)
    grad_encoded = right_inner(grad_memory, memory_weight)
    self_sum, self_queries, self_keys, self_values, self_extras = attend_sublayer_back(
        grad_first, out_weight, columns[:, 3], same_target, self_stored
    )
    grad_qkv = jnp.concatenate([self_queries, self_keys, self_values], axis=1)
    grad_target_in = self_sum + right_inner(grad_qkv, qkv_weight)
    vector_grads = jnp.stack(
        [
            column_sum(self_queries),
            column_sum(self_values),
            self_extras[1],
            self_extras[2],
            self_extras[3],
            column_sum(cross_queries),
            column_sum(cross_values),
            cross_extras[1],
            cross_extras[2],
            cross_extras[3],
            feed_grads[3],
            feed_grads[4],
            feed_grads[5],
        ],
        axis=1,
    )
    grad_language = lax.dot_general(
        grad_target_in,
        token_language,
        (((0,), (0,)), ((), ())),
        precision=highest,
        preferred_element_type=jnp.float32,
    )
    grads = (
        rows_inner(target_low, grad_qkv),
        self_extras[0],
        rows_inner(first_low, cross_queries),
        rows_inner(encoded_low, grad_memory),
        cross_extras[0],
        feed_grads[0],
        feed_grads[2],
        vector_grads,
        feed_grads[1],
        grad_language,
    )
    return (grads, grad_target_in, grad_encoded)


AXES = ("dp", "fsdp")


class Grid:
    def __init__(self, mesh):
        self.nd = mesh.shape["dp"]
        self.nf = mesh.shape["fsdp"]
        self.n = self.nd * self.nf
        self.nh = self.nd // 2
        self.bits = [1 << b for b in range(1, self.nd.bit_length() - 1)]

    def me(self):
        return lax.axis_index("dp") * self.nf + lax.axis_index("fsdp")

    def swap_dp(self, value, flip):
        return lax.ppermute(value, "dp", [(i, i ^ flip) for i in range(self.nd)])

    def swap_fsdp(self, value, flip):
        return lax.ppermute(value, "fsdp", [(i, i ^ flip) for i in range(self.nf)])


def gather_relative(grid, shard, flipped):
    parts = [shard] + [grid.swap_fsdp(shard, m) for m in range(1, grid.nf)]
    held = jnp.stack(parts)[None]
    bits = list(reversed(grid.bits)) if flipped else grid.bits
    order = [0]
    for bit in bits:
        held = jnp.concatenate([held, grid.swap_dp(held, bit)], axis=0)
        order = order + [o | bit for o in order]
    held = held.reshape((-1,) + shard.shape)
    other = grid.swap_dp(held, 1)
    return held, other, [o >> 1 for o in order]


def scatter_relative(grid, keep, send, flipped):
    rows = keep.shape[1:]
    got = grid.swap_dp(send, 1)
    held = keep.astype(jnp.float32) + got.astype(jnp.float32)
    held = held.reshape((grid.nh, grid.nf) + rows)
    bits = list(reversed(grid.bits)) if flipped else grid.bits
    for bit in reversed(bits):
        half = held.shape[0] // 2
        held = held[:half] + grid.swap_dp(held[half:].astype(jnp.bfloat16), bit).astype(jnp.float32)
    held = held[0]
    total = held[0]
    for m in range(1, grid.nf):
        total = total + grid.swap_fsdp(held[m].astype(jnp.bfloat16), m).astype(jnp.float32)
    return total


def spread_order(grid, flipped):
    bits = list(reversed(grid.bits)) if flipped else grid.bits
    order = [0]
    for bit in bits:
        order = order + [o | bit for o in order]
    return [o >> 1 for o in order]


def add_grads(running, fresh):
    return tuple((left_part + right_part for left_part, right_part in zip(running, fresh)))


def place_kernel(order, nf, forms, me_ref, mine, other, *refs):
    outs, sem = refs[:-1], refs[-1]
    me = me_ref[0]
    copies = []
    for part, source in enumerate((mine, other)):
        for at in range(len(order) * nf):
            r = (order[at // nf] * 2 + part) * nf + at % nf
            i = jnp.bitwise_xor(me, r)
            row = 0
            for out, (blocks, wide) in zip(outs, forms):
                dst = out.at[:, i] if wide else out.at[i]
                copies.append(
                    pltpu.make_async_copy(source.at[at, pl.ds(row, blocks)], dst, sem)
                )
                row += blocks
    for copy in copies:
        copy.start()
    for copy in copies:
        copy.wait()


def place_weights(grid, gathered, forms):
    mine, other, order = gathered
    rows = mine.shape[1]
    unit = rows // sum(b for b, _ in forms)
    me = grid.me()
    if unit % 16:
        whole = jnp.concatenate([mine, other])
        table = [0] * grid.n
        for part in range(2):
            for at in range(mine.shape[0]):
                r = (order[at // grid.nf] * 2 + part) * grid.nf + at % grid.nf
                table[r] = part * mine.shape[0] + at
        index = jnp.array(table, jnp.int32)[jnp.arange(grid.n, dtype=jnp.int32) ^ me]
        whole = jnp.take(whole, index, axis=0)
        outs, row = [], 0
        for blocks, wide in forms:
            part = whole[:, row : row + blocks * unit]
            if wide:
                part = part.reshape(grid.n, blocks, unit, 512).transpose(1, 0, 2, 3)
            outs.append(part.reshape(blocks, 512, 512))
            row += blocks * unit
        return outs
    split = (mine.shape[0], rows // unit, unit, 512)
    outs = pl.pallas_call(
        functools.partial(place_kernel, order, grid.nf, forms),
        out_shape=[
            jax.ShapeDtypeStruct(
                (blocks, grid.n, unit, 512) if wide else (grid.n, blocks, unit, 512), jnp.bfloat16
            )
            for blocks, wide in forms
        ],
        in_specs=[pl.BlockSpec(memory_space=pltpu.SMEM)] + [pl.BlockSpec(memory_space=pl.ANY)] * 2,
        out_specs=[pl.BlockSpec(memory_space=pl.ANY)] * len(forms),
        scratch_shapes=[pltpu.SemaphoreType.DMA],
    )(me.reshape(1), mine.reshape(split), other.reshape(split))
    return [out.reshape(blocks, 512, 512) for out, (blocks, _) in zip(outs, forms)]


def spread_grads(grid, grads, forms, flipped):
    unit = 512 // grid.n
    order = spread_order(grid, flipped)
    me = grid.me()
    parts = []
    for grad, (blocks, wide) in zip(grads, forms):
        if wide:
            part = grad.reshape(blocks, grid.n, unit, 512).transpose(1, 0, 2, 3)
        else:
            part = grad.reshape(grid.n, blocks, unit, 512)
        parts.append(part.reshape(grid.n, blocks * unit, 512))
    whole = jnp.concatenate(parts, axis=1)
    sides = []
    for part in range(2):
        table = [
            (o * 2 + part) * grid.nf + z for o in order for z in range(grid.nf)
        ]
        sides.append(jnp.take(whole, jnp.array(table, jnp.int32) ^ me, axis=0))
    return scatter_relative(grid, sides[0], sides[1], flipped)


def to_rows(shard):
    unit = shard.shape[0]
    blocks = shard.shape[1] // 512
    return shard.reshape(unit, blocks, 512).transpose(1, 0, 2).reshape(blocks * unit, 512)


def from_rows(rows, blocks):
    unit = rows.shape[0] // blocks
    return rows.reshape(blocks, unit, 512).transpose(1, 0, 2).reshape(unit, blocks * 512)


def side_by_side(blocks):
    return jnp.concatenate(list(blocks), axis=1)


def to_blocks(grad):
    return grad.astype(jnp.bfloat16).reshape(512, -1, 512).transpose(1, 0, 2)


def shards(
    grid,
    source,
    target,
    source_segments,
    target_segments,
    target_language,
    cotangent,
    enc_qkv,
    enc_out,
    enc_up,
    enc_down,
    enc_vecs,
    enc_bias_up,
    dec_qkv,
    dec_out,
    cross_q,
    cross_kv,
    cross_out,
    dec_up,
    dec_down,
    dec_vecs,
    dec_bias_up,
    lang_table,
):
    unit = enc_qkv.shape[0]
    bias_unit = enc_bias_up.shape[0] // unit
    small = jnp.concatenate(
        [
            enc_vecs,
            dec_vecs,
            lang_table,
            enc_bias_up.reshape(unit, bias_unit),
            dec_bias_up.reshape(unit, bias_unit),
        ],
        axis=1,
    )
    small = jnp.pad(small, ((0, 0), (0, 512 - small.shape[1])))
    pieces = (
        ([to_rows(enc_qkv), small], ((3, True), (1, True))),
        ([to_rows(enc_out), to_rows(enc_up), enc_down], ((1, True), (4, True), (4, False))),
        ([to_rows(dec_qkv), to_rows(dec_out), to_rows(cross_q), to_rows(cross_kv), to_rows(cross_out)], ((3, True), (1, True), (1, True), (2, True), (1, True))),
        ([to_rows(dec_up), dec_down], ((4, True), (4, False))),
    )
    placed = []
    for number, (arrays, forms) in enumerate(pieces):
        gathered = gather_relative(grid, jnp.concatenate(arrays, axis=0), number % 2 == 1)
        placed.append(place_weights(grid, gathered, forms))
    vectors = placed[0][1][0]
    enc_whole = (
        side_by_side(placed[0][0]),
        placed[1][0][0],
        side_by_side(placed[1][1]),
        placed[1][2].reshape(-1, 512),
        vectors[:, :8],
        vectors[:, 29:33].reshape(-1),
    )
    dec_whole = (
        side_by_side(placed[2][0]),
        placed[2][1][0],
        placed[2][2][0],
        side_by_side(placed[2][3]),
        placed[2][4][0],
        side_by_side(placed[3][0]),
        placed[3][1].reshape(-1, 512),
        vectors[:, 8:21],
        vectors[:, 33:37].reshape(-1),
        vectors[:, 21:29],
    )
    enc_again, dec_again = enc_whole, dec_whole
    row_count, length = source_segments.shape
    model_width = source.shape[1]
    source_rows = source.reshape(row_count, length, model_width)
    target_rows = target.reshape(row_count, length, model_width)
    grad_rows = cotangent.reshape(row_count, length, model_width)
    stored_rows = []
    dec_outputs = []
    for row_index in range(row_count):
        masks = row_masks(source_segments[row_index], target_segments[row_index])
        token_language = language_rows(target_segments[row_index], target_language[row_index])
        encoded, enc_stored = encoder_forward(enc_whole, source_rows[row_index], masks[0])
        encoded_low = encoded.astype(jnp.bfloat16)
        output, dec_stored = decoder_forward(
            dec_whole, target_rows[row_index], encoded_low, token_language, masks
        )
        dec_outputs.append(output.astype(jnp.bfloat16))
        stored_rows.append((masks, token_language, encoded_low, enc_stored, dec_stored))
    target_grads = []
    encoded_grads = []
    dec_total = ()
    for row_index in range(row_count):
        masks, token_language, encoded_low, enc_stored, dec_stored = stored_rows[row_index]
        row_grads, grad_target_in, grad_encoded = decoder_backward(
            dec_again,
            grad_rows[row_index].astype(jnp.float32),
            encoded_low,
            token_language,
            masks,
            dec_stored,
        )
        dec_total = row_grads if row_index == 0 else add_grads(dec_total, row_grads)
        target_grads.append(grad_target_in.astype(jnp.bfloat16))
        encoded_grads.append(grad_encoded)
    (
        grad_dec_qkv,
        grad_dec_out,
        grad_cross_q,
        grad_cross_kv,
        grad_cross_out,
        grad_dec_up,
        grad_dec_down,
        grad_dec_vecs,
        grad_dec_bias_up,
        grad_lang,
    ) = dec_total
    dec_a = spread_grads(
        grid,
        [to_blocks(grad_dec_up), grad_dec_down.astype(jnp.bfloat16).reshape(4, 512, 512)],
        ((4, True), (4, False)),
        False,
    )
    dec_b = spread_grads(
        grid,
        [to_blocks(g) for g in (grad_dec_qkv, grad_dec_out, grad_cross_q, grad_cross_kv, grad_cross_out)],
        ((3, True), (1, True), (1, True), (2, True), (1, True)),
        True,
    )
    source_grads = []
    enc_total = ()
    for row_index in range(row_count):
        masks, token_language, encoded_low, enc_stored, dec_stored = stored_rows[row_index]
        row_grads, grad_source = encoder_backward(
            enc_again, encoded_grads[row_index], masks[0], enc_stored
        )
        enc_total = row_grads if row_index == 0 else add_grads(enc_total, row_grads)
        source_grads.append(grad_source.astype(jnp.bfloat16))
    grad_enc_qkv, grad_enc_out, grad_enc_up, grad_enc_down, grad_enc_vecs, grad_enc_bias_up = (
        enc_total
    )
    enc_a = spread_grads(
        grid,
        [to_blocks(grad_enc_up), grad_enc_down.astype(jnp.bfloat16).reshape(4, 512, 512)],
        ((4, True), (4, False)),
        False,
    )
    small_grads = jnp.concatenate(
        [
            grad_enc_vecs,
            grad_dec_vecs,
            grad_lang,
            grad_enc_bias_up.reshape(512, bias_unit),
            grad_dec_bias_up.reshape(512, bias_unit),
        ],
        axis=1,
    )
    small_grads = jnp.pad(small_grads, ((0, 0), (0, 512 - small_grads.shape[1])))
    enc_b = spread_grads(
        grid,
        [to_blocks(g) for g in (grad_enc_qkv, grad_enc_out, small_grads)],
        ((3, True), (1, True), (1, True)),
        True,
    )
    shard_dec_up = from_rows(dec_a[: 4 * unit], 4)
    shard_dec_down = dec_a[4 * unit :]
    shard_dec_qkv = from_rows(dec_b[: 3 * unit], 3)
    shard_dec_out = dec_b[3 * unit : 4 * unit]
    shard_cross_q = dec_b[4 * unit : 5 * unit]
    shard_cross_kv = from_rows(dec_b[5 * unit : 7 * unit], 2)
    shard_cross_out = dec_b[7 * unit :]
    shard_enc_up = from_rows(enc_a[: 4 * unit], 4)
    shard_enc_down = enc_a[4 * unit :]
    shard_enc_qkv = from_rows(enc_b[: 3 * unit], 3)
    shard_enc_out = enc_b[3 * unit : 4 * unit]
    rest = enc_b[4 * unit :]
    shard_enc_vecs = rest[:, :8]
    shard_dec_vecs = rest[:, 8:21]
    shard_lang = rest[:, 21:29]
    shard_enc_bias_up = rest[:, 29:33].reshape(-1)
    shard_dec_bias_up = rest[:, 33:37].reshape(-1)
    return (
        jnp.concatenate(dec_outputs, axis=0),
        jnp.concatenate(source_grads, axis=0),
        jnp.concatenate(target_grads, axis=0),
        shard_enc_qkv,
        shard_enc_out,
        shard_enc_up,
        shard_enc_down,
        shard_enc_vecs,
        shard_enc_bias_up,
        shard_dec_qkv,
        shard_dec_out,
        shard_cross_q,
        shard_cross_kv,
        shard_cross_out,
        shard_dec_up,
        shard_dec_down,
        shard_dec_vecs,
        shard_dec_bias_up,
        shard_lang,
    )


def solution(mesh):
    return jax.shard_map(
        functools.partial(shards, Grid(mesh)),
        mesh=mesh,
        in_specs=(
            P(("dp", "fsdp"), None),
            P(("dp", "fsdp"), None),
            P(("dp", "fsdp"), None),
            P(("dp", "fsdp"), None),
            P(("dp", "fsdp"), None),
            P(("dp", "fsdp"), None),
            P(("dp", "fsdp"), None),
            P(("dp", "fsdp"), None),
            P(("dp", "fsdp"), None),
            P(("dp", "fsdp"), None),
            P(("dp", "fsdp"), None),
            P(("dp", "fsdp")),
            P(("dp", "fsdp"), None),
            P(("dp", "fsdp"), None),
            P(("dp", "fsdp"), None),
            P(("dp", "fsdp"), None),
            P(("dp", "fsdp"), None),
            P(("dp", "fsdp"), None),
            P(("dp", "fsdp"), None),
            P(("dp", "fsdp"), None),
            P(("dp", "fsdp")),
            P(("dp", "fsdp"), None),
        ),
        out_specs=(
            P(("dp", "fsdp"), None),
            P(("dp", "fsdp"), None),
            P(("dp", "fsdp"), None),
            P(("dp", "fsdp"), None),
            P(("dp", "fsdp"), None),
            P(("dp", "fsdp"), None),
            P(("dp", "fsdp"), None),
            P(("dp", "fsdp"), None),
            P(("dp", "fsdp")),
            P(("dp", "fsdp"), None),
            P(("dp", "fsdp"), None),
            P(("dp", "fsdp"), None),
            P(("dp", "fsdp"), None),
            P(("dp", "fsdp"), None),
            P(("dp", "fsdp"), None),
            P(("dp", "fsdp"), None),
            P(("dp", "fsdp"), None),
            P(("dp", "fsdp")),
            P(("dp", "fsdp"), None),
        ),
        check_vma=False,
    )
```

```python
import functools

import jax
import jax.numpy as jnp
from jax import lax
from jax.experimental import pallas as pl
from jax.experimental.pallas import tpu as pltpu
from jax.sharding import PartitionSpec as P

AXES = ("dp", "fsdp")
LANGS = 8
ROW = 512
CHUNK = 512
scale_dot = 0.125
norm_eps = 1e-05
VMEM_LIMIT = 56 * 1024 * 1024

ENC = 8
DEC = 16
ENC_UP = 29
DEC_UP = 33
BF = jnp.bfloat16
F32 = jnp.float32


class Grid:
    def __init__(self, mesh):
        self.nd = mesh.shape["dp"]
        self.nf = mesh.shape["fsdp"]
        self.n = self.nd * self.nf
        self.nh = self.nd // 2
        self.hz = self.nh * self.nf
        self.unit = ROW // self.n
        self.tiled = self.unit % 16 == 0
        self.cut = (self.n, self.unit) if self.tiled else (32, 16)

    def me(self):
        return lax.axis_index("dp") * self.nf + lax.axis_index("fsdp")

    def swap_dp(self, value, flip):
        return lax.ppermute(value, "dp", [(i, i ^ flip) for i in range(self.nd)])

    def swap_fsdp(self, value, flip):
        return lax.ppermute(value, "fsdp", [(i, i ^ flip) for i in range(self.nf)])

    def relative(self, part, at):
        return (at // self.nf * 2 + part) * self.nf + at % self.nf

    def spot(self, me, part, at, across):
        if not across:
            return jnp.bitwise_xor(me, self.relative(part, at))
        flip = (at // self.nf * 2 + part) * self.nf
        return jnp.bitwise_xor(me - lax.rem(me, self.nf), flip) + at % self.nf


def after(value, token):
    if token is None:
        return value
    return lax.optimization_barrier((value, token))[0]


def z_copies(grid, shard):
    return lax.all_to_all(
        jnp.broadcast_to(shard[None], (grid.nf,) + shard.shape), "fsdp", 0, 0, tiled=False
    )


def z_gather(grid, shard):
    return [shard] + [grid.swap_fsdp(shard, m) for m in range(1, grid.nf)]


def z_gather_halves(grid, shard):
    order = [0]
    flips = [1 << b for b in range(grid.nf.bit_length() - 1)]
    held = shard[None]
    for flip in reversed(flips):
        held = jnp.concatenate([held, grid.swap_fsdp(held, flip)])
        order = order + [o | flip for o in order]
    return jnp.stack([held[order.index(z)] for z in range(grid.nf)])


def xy_gather(grid, held):
    return [held] + [grid.swap_dp(held, h << 1) for h in range(1, grid.nh)]


def xy_gather_early(grid, held):
    return [held] + [grid.swap_dp(held, h << 1) for h in range(1, grid.nh - 1)]


def xy_gather_rest(grid, held):
    return [grid.swap_dp(held, grid.nh - 1 << 1)]


def core_sum(grid, keep, got):
    shape = (grid.nh, grid.nf) + keep.shape[1:]
    keep, got = keep.reshape(shape), got.reshape(shape)
    kind = keep.dtype
    sends = [(keep[h].astype(F32) + got[h].astype(F32)).astype(kind) for h in range(1, grid.nh)]
    return [keep[0], got[0]], sends


def xy_scatter(grid, sends):
    return [grid.swap_dp(s, h << 1) for h, s in zip(range(1, grid.nh), sends)]


def xy_sum(grid, parts, z):
    out = parts[0][z].astype(F32)
    for part in parts[1:]:
        out = out + part[z].astype(F32)
    return out


class Piece:
    def __init__(self, grid, forms, plain=False, across=False):
        self.grid, self.forms, self.plain, self.across = grid, forms, plain, across
        self.starts = [sum(b for b, _ in forms[:k]) for k in range(len(forms))]
        self.blocks = sum(b for b, _ in forms)
        self.refs = 1 if plain or not grid.tiled else 2

    def cut(self, k):
        blocks, wide = self.forms[k]
        a, b = self.grid.cut
        return (blocks, a, b, 512) if wide else (a, blocks, b, 512)

    def arrive(self, *held):
        grid = self.grid
        if grid.tiled:
            shape = (-1, self.blocks, grid.unit, 512)
            self.arrays = [tuple(h.reshape(shape) for h in held)] * len(self.forms)
            return
        whole = jnp.concatenate(held)
        if not self.plain:
            spots = [
                grid.spot(grid.me(), part, at, self.across)
                for part in range(2)
                for at in range(grid.hz)
            ]
            index = jnp.zeros((grid.n,), jnp.int32).at[jnp.stack(spots)].set(
                jnp.arange(grid.n, dtype=jnp.int32)
            )
            whole = jnp.take(whole, index, axis=0)
        self.arrays = []
        for k, (blocks, wide) in enumerate(self.forms):
            row = self.starts[k] * grid.unit
            part = whole[:, row : row + blocks * grid.unit]
            if wide:
                part = part.reshape(grid.n, blocks, grid.unit, 512).transpose(1, 0, 2, 3)
            self.arrays.append((part.reshape(self.cut(k)),))

    def pairs(self, k, me, refs, held):
        grid = self.grid
        blocks, wide = self.forms[k]
        start = self.starts[k]
        if not grid.tiled:
            yield refs[0 if len(refs) == 1 else k], held
        elif self.plain and wide:
            for j in range(blocks):
                yield refs[0].at[:, start + j], held.at[j]
        elif self.plain:
            yield refs[0].at[:, pl.ds(start, blocks)], held
        else:
            for part, ref in enumerate(refs):
                for at in range(grid.hz):
                    i = grid.spot(me, part, at, self.across)
                    yield ref.at[at, pl.ds(start, blocks)], held.at[:, i] if wide else held.at[i]

    def fetch(self, k, me, refs, dst, sem):
        for there, here in self.pairs(k, me, refs, dst):
            pltpu.make_async_copy(there, here, sem).start()

    def store(self, k, me, src, refs, sem):
        for there, here in self.pairs(k, me, refs, src):
            pltpu.make_async_copy(here, there, sem).start()

    def out_shapes(self):
        grid = self.grid
        if not grid.tiled:
            return [jax.ShapeDtypeStruct(self.cut(k), BF) for k in range(len(self.forms))]
        if self.plain:
            return [jax.ShapeDtypeStruct((grid.n, self.blocks, grid.unit, 512), BF)]
        return [jax.ShapeDtypeStruct((grid.hz, self.blocks, grid.unit, 512), BF)] * 2

    def ready(self, outs):
        grid = self.grid
        rows = self.blocks * grid.unit
        if grid.tiled:
            return [out.reshape(-1, rows, 512) for out in outs]
        parts = []
        for k, (blocks, wide) in enumerate(self.forms):
            part = outs[k]
            if wide:
                part = part.reshape(blocks, grid.n, grid.unit, 512).transpose(1, 0, 2, 3)
            parts.append(part.reshape(grid.n, blocks * grid.unit, 512))
        whole = jnp.concatenate(parts, axis=1)
        return [whole] if self.plain else spread_blocks(grid, whole)


def scatter_plain(grid, whole):
    rows = whole.shape[1]
    part = lax.psum_scatter(
        whole.reshape(grid.nd, grid.nf * rows, 512), "dp", scatter_dimension=0, tiled=False
    )
    return lax.psum_scatter(
        part.reshape(grid.nf, rows, 512), "fsdp", scatter_dimension=0, tiled=False
    )


def spread_blocks(grid, whole):
    sides = []
    for part in range(2):
        table = [grid.relative(part, at) for at in range(grid.hz)]
        sides.append(jnp.take(whole, jnp.array(table, jnp.int32) ^ grid.me(), axis=0))
    return sides


def finish(ref, sem):
    pltpu.make_async_copy(ref, ref, sem).wait()


def to_rows(shard):
    unit = shard.shape[0]
    blocks = shard.shape[1] // 512
    return shard.reshape(unit, blocks, 512).transpose(1, 0, 2).reshape(blocks * unit, 512)


def pack_kernel(*refs):
    out, at = refs[-1], 0
    for ref in refs[:-1]:
        rows = ref.shape[0]
        for j in range(ref.shape[1] // 512):
            out[at : at + rows] = ref[:, 512 * j : 512 * (j + 1)]
            at += rows


def pack(grid, arrays):
    if not grid.tiled:
        return jnp.concatenate([to_rows(a) if a.shape[0] == grid.unit else a for a in arrays], axis=0)
    rows = sum(a.size for a in arrays) // 512
    return pl.pallas_call(pack_kernel, out_shape=jax.ShapeDtypeStruct((rows, 512), BF), name="pack")(*arrays)


def shards_kernel(pieces, counts, *refs):
    refs = list(refs)
    own = [[refs.pop(0) for _ in range(count)] for count in counts[:-1]]
    lasts = [refs.pop(0) for _ in range(counts[-1])]
    at = 0
    for piece, parts in zip(pieces, own):
        rows = piece.blocks * piece.grid.unit
        total = None
        for part in parts:
            total = part[0].astype(F32) if total is None else total + part[0].astype(F32)
        for last in lasts:
            total = total + last[at : at + rows].astype(F32)
        at += rows
        row, unit = 0, piece.grid.unit
        for blocks, wide in piece.forms:
            out = refs.pop(0)
            for j in range(blocks):
                value = total[row : row + unit]
                if wide:
                    out[:, 512 * j : 512 * (j + 1)] = value
                else:
                    out[unit * j : unit * (j + 1)] = value
                row += unit


def shards(grid, pieces, own, lasts):
    if not grid.tiled:
        total = jnp.concatenate(
            [functools.reduce(lambda a, b: a + b, [p[0].astype(F32) for p in parts]) for parts in own]
        )
        for last in lasts:
            total = total + last.astype(F32)
        outs, row = [], 0
        for piece in pieces:
            for blocks, wide in piece.forms:
                part = total[row : row + blocks * grid.unit]
                outs.append(from_rows(part, blocks) if wide else part)
                row += blocks * grid.unit
        return outs
    first = lambda a: pl.BlockSpec((1,) + a.shape[1:], lambda i: (0, 0, 0))
    args = [a for parts in own for a in parts] + lasts
    specs = [first(a) for parts in own for a in parts] + [whole_spec(a) for a in lasts]
    shapes = [
        like(grid.unit, 512 * blocks, F32) if wide else like(grid.unit * blocks, 512, F32)
        for piece in pieces
        for blocks, wide in piece.forms
    ]
    return pl.pallas_call(
        functools.partial(shards_kernel, pieces, [len(p) for p in own] + [len(lasts)]),
        grid=(1,),
        in_specs=specs,
        out_specs=[whole_spec(s) for s in shapes],
        out_shape=shapes,
        name="shards",
    )(*args)


def from_rows(rows, blocks):
    unit = rows.shape[0] // blocks
    return rows.reshape(blocks, unit, 512).transpose(1, 0, 2).reshape(unit, blocks * 512)


HALF = 64
BIG = float(2**30)


def dot(a, b):
    return jnp.dot(a, b, preferred_element_type=jnp.float32)


def dot_t(a, b):
    return lax.dot_general(a, b, (((1,), (1,)), ((), ())), preferred_element_type=jnp.float32)


def t_dot(a, b):
    return lax.dot_general(a, b, (((0,), (0,)), ((), ())), preferred_element_type=jnp.float32)


def lanes(rows=1, width=128):
    return lax.broadcasted_iota(jnp.int32, (rows, width), 1)


def head_lanes(h):
    return jnp.where(lanes() // HALF == h, 1.0, 0.0).astype(jnp.bfloat16)


def one_lanes(h):
    at = lanes() - HALF * h
    return jnp.where((at >= 8) & (at < 11), 1.0, 0.0).astype(jnp.bfloat16)


def minus_parts(value):
    at = lanes() % HALF
    value = -value
    high = value.astype(jnp.bfloat16).astype(jnp.float32)
    rest = value - high
    mid = rest.astype(jnp.bfloat16).astype(jnp.float32)
    low = rest - mid
    out = jnp.where(at == 8, high, jnp.where(at == 9, mid, jnp.where(at == 10, low, 0.0)))
    return out.astype(jnp.bfloat16)


def pair(value, p):
    return value[:, 128 * p : 128 * (p + 1)]


def norm(summed):
    centred = summed - jnp.mean(summed, axis=-1, keepdims=True)
    inverse = lax.rsqrt(jnp.mean(centred * centred, axis=-1, keepdims=True) + norm_eps)
    return centred * inverse, inverse


def heads_forward(q, k, v, hot, bar):
    outs, logs = [], []
    for p in range(q.shape[1] // 128):
        qa = jnp.concatenate([pair(q, p) * jnp.bfloat16(scale_dot), hot], axis=1)
        total, tops = None, []
        for h in (0, 1):
            mask = head_lanes(h)
            ka = jnp.concatenate([pair(k, p) * mask, bar], axis=1)
            scores = dot_t(qa, ka)
            top = jnp.max(scores, axis=-1, keepdims=True)
            power = jnp.exp(scores - top).astype(jnp.bfloat16)
            va = jnp.concatenate(
                [pair(v, p) * mask, jnp.broadcast_to(mask, (v.shape[0], 128))], axis=1
            )
            part = dot(power, va)
            total = part if total is None else total + part
            tops.append(top)
        sums = total[:, 128:]
        outs.append(total[:, :128] / sums)
        logs.append(jnp.where(lanes() < HALF, tops[0], tops[1]) + jnp.log(sums))
    return jnp.concatenate(outs, axis=1), jnp.concatenate(logs, axis=1)


def heads_backward(go, q, k, v, o, lse, hot, bar):
    gqs, gks, gvs = [], [], []
    at = lax.broadcasted_iota(jnp.int32, (128, 128), 0) // HALF
    to = lax.broadcasted_iota(jnp.int32, (128, 128), 1) // HALF
    same = jnp.where(at == to, 1.0, 0.0).astype(jnp.bfloat16)
    same = jnp.concatenate([same, same], axis=0)
    for p in range(q.shape[1] // 128):
        qs = pair(q, p) * jnp.bfloat16(scale_dot)
        gp = pair(go, p)
        prod = gp.astype(jnp.float32) * pair(o, p)
        high = prod.astype(jnp.bfloat16)
        low = (prod - high.astype(jnp.float32)).astype(jnp.bfloat16)
        delta = dot(jnp.concatenate([high, low], axis=1), same)
        qa = jnp.concatenate([qs, hot + minus_parts(pair(lse, p))], axis=1)
        ga = jnp.concatenate([gp, minus_parts(delta)], axis=1)
        gq = gk = gv = None
        for h in (0, 1):
            mask, one = head_lanes(h), one_lanes(h)
            km = pair(k, p) * mask
            ka = jnp.concatenate([km, bar + one], axis=1)
            va = jnp.concatenate(
                [pair(v, p) * mask, jnp.broadcast_to(one, (v.shape[0], 128))], axis=1
            )
            probs = jnp.exp(dot_t(ka, qa))
            gs = (probs * dot_t(va, ga)).astype(jnp.bfloat16)
            gv_h = dot(probs.astype(jnp.bfloat16), gp * mask)
            gk_h = dot(gs, qs * mask)
            gq_h = t_dot(gs, km)
            gv = gv_h if gv is None else gv + gv_h
            gk = gk_h if gk is None else gk + gk_h
            gq = gq_h if gq is None else gq + gq_h
        gqs.append((gq * scale_dot).astype(jnp.bfloat16))
        gks.append(gk.astype(jnp.bfloat16))
        gvs.append(gv.astype(jnp.bfloat16))
    return tuple(jnp.concatenate(x, axis=1) for x in (gqs, gks, gvs))


def norm_back(grad, normed, inverse, gain):
    scaled = grad * gain
    back = inverse * (
        scaled
        - jnp.mean(scaled, axis=-1, keepdims=True)
        - normed * jnp.mean(scaled * normed, axis=-1, keepdims=True)
    )
    return back, jnp.sum(grad * normed, axis=0), jnp.sum(grad, axis=0)


def square(ref, k):
    return ref[k].reshape(512, 512)


def vec(vectors, k):
    return vectors[k : k + 1, :]


ANY = pl.BlockSpec(memory_space=pl.ANY)
SMEM = pl.BlockSpec(memory_space=pltpu.SMEM)


def whole_spec(array):
    return pl.BlockSpec(array.shape, lambda i: (0,) * array.ndim)


def row_spec(array):
    return pl.BlockSpec((ROW,) + array.shape[1:], lambda i: (i,) + (0,) * (array.ndim - 1))


def like(rows, width, kind):
    return jax.ShapeDtypeStruct((rows, width), kind)


def params():
    return pltpu.CompilerParams(vmem_limit_bytes=VMEM_LIMIT)


def cost(tokens, macs):
    return pl.CostEstimate(
        flops=2 * tokens * macs, bytes_accessed=16 * tokens * 512, transcendentals=0
    )


def attend_forward_kernel(mode, base, piece, small, *refs):
    refs = list(refs)
    me_ref = refs.pop(0)
    count = piece.refs
    take = lambda k: [refs.pop(0) for _ in range(k)]
    proj_refs = [take(count) for _ in range(3 if mode == "cross" else 2)]
    small_refs = take(count) if small is not None else None
    vectors_ref = None if small is not None else refs.pop(0)
    if mode == "cross":
        normed_ref, memory_ref = take(2)
    else:
        x_ref = refs.pop(0)
        if mode == "dec":
            lang_ref = refs.pop(0)
    hot_ref, bar_ref = take(2)
    q_out, k_out, v_out, o_out, lse_out, n_out, inv_out = take(7)
    if mode != "enc":
        low_out = refs.pop(0)
    if small is not None:
        vectors_out, small_out = take(2)
    weights = take(3 if mode == "cross" else 2)
    small_scr = refs.pop(0) if small is not None else None
    sems = refs.pop(0)
    out_w = weights[-1]

    @pl.when(pl.program_id(0) == 0)
    def _():
        me = me_ref[0]
        for k, (source, dst) in enumerate(zip(proj_refs, weights)):
            piece.fetch(k, me, source, dst, sems.at[k])
        if small is not None:
            piece.fetch(small, me, small_refs, small_scr, sems.at[3])
            finish(small_scr, sems.at[3])
            block = small_scr[0].reshape(512, 512)[:, :128]
            small_out[...] = block
            vectors_out[...] = block.astype(F32).T
        for k, dst in enumerate(weights):
            finish(dst, sems.at[k])

    vectors = (vectors_out if small is not None else vectors_ref)[...]
    if mode == "enc":
        low = x_ref[...]
        residual = low.astype(F32)
        memory = low
    elif mode == "dec":
        residual = x_ref[...].astype(F32) + dot(lang_ref[...], vectors.astype(BF))
        low = memory = residual.astype(BF)
    else:
        residual = normed_ref[...] * vec(vectors, DEC + 3) + vec(vectors, DEC + 4)
        low = residual.astype(BF)
        memory = memory_ref[...]
    if mode != "enc":
        low_out[...] = low
    if mode == "cross":
        wq, wk, wv = square(weights[0], 0), square(weights[1], 0), square(weights[1], 1)
    else:
        wq, wk, wv = (square(weights[0], j) for j in range(3))
    q = (dot(low, wq) + vec(vectors, base)).astype(BF)
    k = dot(memory, wk).astype(BF)
    v = (dot(memory, wv) + vec(vectors, base + 1)).astype(BF)
    q_out[...], k_out[...], v_out[...] = q, k, v
    o, lse = heads_forward(q, k, v, hot_ref[...], bar_ref[...])
    o_out[...], lse_out[...] = o, lse
    branch = dot(o.astype(BF), square(out_w, 0)) + vec(vectors, base + 2)
    n_out[...], inv_out[...] = norm(residual + branch)


def attend_forward(mode, base, me, piece, small, inputs, hot, bar, vectors):
    grid = piece.grid
    tokens = hot.shape[0]
    names = range(3 if mode == "cross" else 2)
    weights = [a for k in names for a in piece.arrays[k]]
    args = [me] + weights
    specs = [SMEM] + [ANY] * len(weights)
    if small is not None:
        args += list(piece.arrays[small])
        specs += [ANY] * len(piece.arrays[small])
    else:
        args.append(vectors)
        specs.append(whole_spec(vectors))
    rows = list(inputs) + [hot, bar]
    args += rows
    specs += [row_spec(a) for a in rows]
    outs = [like(tokens, 512, BF)] * 3 + [like(tokens, 512, F32)] * 3 + [like(tokens, 1, F32)]
    if mode != "enc":
        outs.append(like(tokens, 512, BF))
    out_specs = [row_spec(o) for o in outs]
    scratch = [pltpu.VMEM(piece.cut(k), BF) for k in names]
    if small is not None:
        extra = [like(128, 512, F32), like(512, 128, BF)]
        outs += extra
        out_specs += [whole_spec(e) for e in extra]
        scratch.append(pltpu.VMEM(piece.cut(small), BF))
    scratch.append(pltpu.SemaphoreType.DMA((4,)))
    return pl.pallas_call(
        functools.partial(attend_forward_kernel, mode, base, piece, small),
        grid=(tokens // ROW,),
        in_specs=specs,
        out_specs=out_specs,
        out_shape=outs,
        scratch_shapes=scratch,
        compiler_params=params(),
        cost_estimate=cost(tokens, 4 * 512 * 512 + 2 * 8 * 512 * 256),
        name="attend_forward_" + mode,
    )(*args)


def feed_forward_kernel(base, first, piece, own, *refs):
    refs = list(refs)
    me_ref = refs.pop(0)
    count = piece.refs
    take = lambda k: [refs.pop(0) for _ in range(k)]
    up_refs, down_refs = take(count), take(count)
    vectors_ref, bias_ref, n_ref = take(3)
    act_out, slope_out, n_out, inv_out, low_out = take(5)
    up, down, sems = take(3)

    @pl.when(pl.program_id(0) == 0)
    def _():
        me = me_ref[0]
        piece.fetch(own, me, up_refs, up, sems.at[0])
        piece.fetch(own + 1, me, down_refs, down, sems.at[1])
        finish(up, sems.at[0])
        finish(down, sems.at[1])

    vectors = vectors_ref[...]
    x = n_ref[...] * vec(vectors, first) + vec(vectors, first + 1)
    low = x.astype(BF)
    branch = None
    for j in range(4):
        h = dot(low, square(up, j)) + bias_ref[j : j + 1, :]
        act, slope = gate(h)
        act = act.astype(BF)
        act_out[j], slope_out[j] = act, slope.astype(BF)
        part = dot(act, tall(down, j))
        branch = part if branch is None else branch + part
    n, inv = norm(x + branch + vec(vectors, base))
    n_out[...], inv_out[...] = n, inv
    low_out[...] = (n * vec(vectors, base + 1) + vec(vectors, base + 2)).astype(BF)


def gate(h):
    c = 0.7978845608028654
    square_h = h * h
    t = jnp.tanh(h * (c + (c * 0.044715) * square_h))
    half = 0.5 + 0.5 * t
    slope = half + (0.5 * h) * (1.0 - t * t) * (c + (3.0 * c * 0.044715) * square_h)
    return h * half, slope


def tall(ref, j):
    size = ref.shape[0] // 4
    return ref[size * j : size * (j + 1)].reshape(512, 512)


def feed_forward(base, first, me, piece, own, vectors, bias, n):
    tokens = n.shape[0]
    weights = list(piece.arrays[own]) + list(piece.arrays[own + 1])
    chunk = jax.ShapeDtypeStruct((4, tokens, 512), BF)
    chunk_spec = pl.BlockSpec((4, ROW, 512), lambda i: (0, i, 0))
    outs = [chunk, chunk, like(tokens, 512, F32), like(tokens, 1, F32), like(tokens, 512, BF)]
    return pl.pallas_call(
        functools.partial(feed_forward_kernel, base, first, piece, own),
        grid=(tokens // ROW,),
        in_specs=[SMEM]
        + [ANY] * len(weights)
        + [whole_spec(vectors), whole_spec(bias), row_spec(n)],
        out_specs=[chunk_spec, chunk_spec] + [row_spec(o) for o in outs[2:]],
        out_shape=outs,
        scratch_shapes=[
            pltpu.VMEM(piece.cut(own), BF),
            pltpu.VMEM(piece.cut(own + 1), BF),
            pltpu.SemaphoreType.DMA((2,)),
        ],
        compiler_params=params(),
        cost_estimate=cost(tokens, 8 * 512 * 512),
        name="feed_forward",
    )(me, *weights, vectors, bias, n)


def feed_backward_kernel(base, first, piece, own, grads, at, *refs):
    refs = list(refs)
    me_ref = refs.pop(0)
    count = piece.refs
    take = lambda k: [refs.pop(0) for _ in range(k)]
    up_refs, down_refs = take(count), take(count)
    vectors_ref, grad_ref, n2_ref, inv2_ref, n1_ref, act_ref, slope_ref = take(7)
    grad_outs = take(len(grads.out_shapes()))
    dx_out, sums_out, bias_out = take(3)
    up, down, d_up, d_down, low_t, branch, sems = take(7)
    j = pl.program_id(0)
    vectors = vectors_ref[...]

    @pl.when(j == 0)
    def _():
        me = me_ref[0]
        piece.fetch(own, me, up_refs, up, sems.at[0])
        piece.fetch(own + 1, me, down_refs, down, sems.at[1])
        sums_out[...] = jnp.zeros_like(sums_out)
        for t in range(grad_ref.shape[0] // ROW):
            part = pl.ds(ROW * t, ROW)
            back, gain, shift = norm_back(
                grad_ref[part].astype(F32), n2_ref[part], inv2_ref[part], vec(vectors, base + 1)
            )
            dx_out[part] = back
            low = back.astype(BF)
            branch[part] = low
            sums_out[0:1] += jnp.sum(low.astype(F32), axis=0, keepdims=True)
            sums_out[1:2] += gain[None]
            sums_out[2:3] += shift[None]
            x = n1_ref[part] * vec(vectors, first) + vec(vectors, first + 1)
            low_t[:, part] = x.astype(BF).T
        finish(up, sems.at[0])
        finish(down, sems.at[1])

    size = down.shape[0] // 4
    down_j = down[pl.ds(size * j, size)].reshape(512, 512)
    up_j = up[j].reshape(512, 512)
    low = branch[...]
    hidden = (dot_t(low, down_j) * slope_ref[0].astype(F32)).astype(BF)
    bias_out[0] = jnp.broadcast_to(
        jnp.sum(hidden.astype(F32), axis=0, keepdims=True), bias_out.shape[1:]
    )
    dx_out[...] += dot_t(hidden, up_j)
    d_up[j] = dot(low_t[...], hidden).astype(BF).reshape(d_up.shape[1:])
    d_down[pl.ds(size * j, size)] = (
        t_dot(act_ref[0], low).astype(BF).reshape((size,) + d_down.shape[1:])
    )

    @pl.when(j == pl.num_programs(0) - 1)
    def _():
        me = me_ref[0]
        grads.store(at, me, d_up, grad_outs, sems.at[0])
        grads.store(at + 1, me, d_down, grad_outs, sems.at[1])
        finish(d_up, sems.at[0])
        finish(d_down, sems.at[1])


def feed_backward(base, first, me, piece, own, grads, at, vectors, grad, n2, inv2, n1, act, slope):
    tokens = n1.shape[0]
    weights = list(piece.arrays[own]) + list(piece.arrays[own + 1])
    held = [vectors, grad, n2, inv2, n1]
    chunk_spec = pl.BlockSpec((1, tokens, 512), lambda i: (i, 0, 0))
    outs = [like(tokens, 512, F32), like(8, 512, F32), jax.ShapeDtypeStruct((4, 8, 512), F32)]
    got = pl.pallas_call(
        functools.partial(feed_backward_kernel, base, first, piece, own, grads, at),
        grid=(4,),
        in_specs=[SMEM]
        + [ANY] * len(weights)
        + [whole_spec(a) for a in held]
        + [chunk_spec, chunk_spec],
        out_specs=[ANY] * len(grads.out_shapes())
        + [whole_spec(outs[0]), whole_spec(outs[1]), pl.BlockSpec((1, 8, 512), lambda i: (i, 0, 0))],
        out_shape=grads.out_shapes() + outs,
        scratch_shapes=[
            pltpu.VMEM(piece.cut(own), BF),
            pltpu.VMEM(piece.cut(own + 1), BF),
            pltpu.VMEM(grads.cut(at), BF),
            pltpu.VMEM(grads.cut(at + 1), BF),
            pltpu.VMEM((512, tokens), BF),
            pltpu.VMEM((tokens, 512), BF),
            pltpu.SemaphoreType.DMA((2,)),
        ],
        compiler_params=params(),
        cost_estimate=cost(tokens, 16 * 512 * 512),
        name="feed_backward",
    )(me, *weights, *held, act, slope)
    m = len(grads.out_shapes())
    return got[:m], got[m], got[m + 1], got[m + 2][:, 0, :]


def attend_backward_kernel(mode, base, piece, grads, first, shared, *refs):
    refs = list(refs)
    me_ref = refs.pop(0)
    count = piece.refs
    take = lambda k: [refs.pop(0) for _ in range(k)]
    kinds = 3 if mode == "cross" else 2
    weight_refs = [take(count) for _ in range(kinds)]
    vectors_ref, grad_ref, n_ref, inv_ref, q_ref, k_ref, v_ref, o_ref, lse_ref = take(9)
    hot_ref, bar_ref, low_ref = take(3)
    memory_ref = refs.pop(0) if mode == "cross" else None
    lang_ref = refs.pop(0) if mode == "dec" else None
    sum_refs = take(5) if mode == "enc" else None
    cols_ref = refs.pop(0) if mode == "enc" else None
    if shared:
        refs.pop(0)
    grad_outs = take(len(grads.out_shapes()))
    dx_out, sums_out = take(2)
    dm_out = refs.pop(0) if mode == "cross" else None
    lang_out = refs.pop(0) if mode == "dec" else None
    staged_kinds = 2 if mode == "dec" else 3
    weights, staged = take(kinds), take(staged_kinds)
    low_t, o_t, gqs, gks, gvs, gbs, sems = take(7)
    memory_t = refs.pop(0) if mode == "cross" else None
    all_sums = refs.pop(0) if mode == "enc" else None
    step = pl.program_id(0)
    vectors = vectors_ref[...]

    @pl.when(step == 0)
    def _():
        me = me_ref[0]
        for k, (source, dst) in enumerate(zip(weight_refs, weights)):
            piece.fetch(k, me, source, dst, sems.at[k])
        sums_out[...] = jnp.zeros_like(sums_out)
        if mode == "dec":
            lang_out[...] = jnp.zeros_like(lang_out)
        for k, dst in enumerate(weights):
            finish(dst, sems.at[k])

    back, gain, shift = norm_back(
        grad_ref[...], n_ref[...], inv_ref[...], vec(vectors, base + 3)
    )
    gb = back.astype(BF)
    go = dot_t(gb, square(weights[-1], 0)).astype(BF)
    q, k, v, o = q_ref[...], k_ref[...], v_ref[...], o_ref[...]
    gq, gk, gv = heads_backward(go, q, k, v, o, lse_ref[...], hot_ref[...], bar_ref[...])
    if mode == "cross":
        wq, wk, wv = square(weights[0], 0), square(weights[1], 0), square(weights[1], 1)
    else:
        wq, wk, wv = (square(weights[0], j) for j in range(3))
    dx = back + dot_t(gq, wq)
    dm = dot_t(gk, wk) + dot_t(gv, wv)
    if mode == "cross":
        dx_out[...] = dx
        dm_out[...] = dm
    else:
        dx = dx + dm
        dx_out[...] = dx.astype(BF)
    if mode == "dec":
        high = dx.astype(BF)
        rest = (dx - high.astype(F32)).astype(BF)
        hot_lang = lang_ref[...].T
        lang_out[...] += dot(hot_lang, high) + dot(hot_lang, rest)
    sums_out[0:1] += jnp.sum(gq.astype(F32), axis=0, keepdims=True)
    sums_out[1:2] += jnp.sum(gv.astype(F32), axis=0, keepdims=True)
    sums_out[2:3] += jnp.sum(gb.astype(F32), axis=0, keepdims=True)
    sums_out[3:4] += gain[None]
    sums_out[4:5] += shift[None]
    part = pl.ds(pl.multiple_of(step * ROW, ROW), ROW)
    gqs[part], gks[part], gvs[part], gbs[part] = gq, gk, gv, gb
    low_t[:, part] = low_ref[...].T
    o_t[:, part] = o.astype(BF).T
    if mode == "cross":
        memory_t[:, part] = memory_ref[...].T

    @pl.when(step == pl.num_programs(0) - 1)
    def _():
        me = me_ref[0]
        shape = staged[0].shape[1:]
        out_grad = dot(o_t[...], gbs[...]).astype(BF).reshape(shape)
        gq_grad = dot(low_t[...], gqs[...]).astype(BF).reshape(shape)
        kv_t = (memory_t if mode == "cross" else low_t)[...]
        gk_grad = dot(kv_t, gks[...]).astype(BF).reshape(shape)
        gv_grad = dot(kv_t, gvs[...]).astype(BF).reshape(shape)
        if mode == "cross":
            staged[0][0] = gq_grad
            staged[1][0], staged[1][1] = gk_grad, gv_grad
        else:
            staged[0][0], staged[0][1], staged[0][2] = gq_grad, gk_grad, gv_grad
        staged[kinds - 1][0] = out_grad
        if mode == "enc":
            all_sums[...] = jnp.zeros_like(all_sums)
            row = 0
            counts = (8, 5, 3, 5, 5, 3)
            for ref, count in zip([sum_refs[0], sums_out] + sum_refs[1:], counts):
                all_sums[row : row + count] = ref[:count]
                row += count
            block = (all_sums[...].T + cols_ref[...]).astype(BF)
            block = jnp.concatenate([block, jnp.zeros((512, 384), BF)], axis=1)
            staged[2][0] = block.reshape(shape)
        for k, src in enumerate(staged):
            grads.store(first + k, me, src, grad_outs, sems.at[k])
        for k, src in enumerate(staged):
            finish(src, sems.at[k])


def attend_backward(
    mode, base, me, piece, grads, first, vectors, grad, saved, hot, bar, low, extra, fixed=(), into=None
):
    q, k, v, o, lse, n, inv = saved
    tokens = hot.shape[0]
    kinds = range(3 if mode == "cross" else 2)
    weights = [a for i in kinds for a in piece.arrays[i]]
    rows = [grad, n, inv, q, k, v, o, lse, hot, bar, low] + list(extra)
    outs = [like(tokens, 512, F32 if mode == "cross" else BF), like(8, 512, F32)]
    out_specs = [row_spec(outs[0]), whole_spec(outs[1])]
    if mode == "cross":
        outs.append(like(tokens, 512, F32))
        out_specs.append(row_spec(outs[-1]))
    if mode == "dec":
        outs.append(like(128, 512, F32))
        out_specs.append(whole_spec(outs[-1]))
    grad_shapes = grads.out_shapes()
    scratch = [pltpu.VMEM(piece.cut(i), BF) for i in kinds]
    scratch += [pltpu.VMEM(grads.cut(first + i), BF) for i in range(2 if mode == "dec" else 3)]
    scratch += [pltpu.VMEM((512, tokens), BF)] * 2 + [pltpu.VMEM((tokens, 512), BF)] * 4
    scratch.append(pltpu.SemaphoreType.DMA((3,)))
    if mode == "cross":
        scratch.append(pltpu.VMEM((512, tokens), BF))
    if mode == "enc":
        scratch.append(pltpu.VMEM((128, 512), F32))
    args = [me, *weights, vectors, *rows, *fixed]
    shared = [] if into is None else [into]
    got = pl.pallas_call(
        functools.partial(attend_backward_kernel, mode, base, piece, grads, first, bool(shared)),
        grid=(tokens // ROW,),
        in_specs=[SMEM]
        + [ANY] * len(weights)
        + [whole_spec(vectors)]
        + [row_spec(a) for a in rows]
        + [whole_spec(a) for a in fixed]
        + [ANY] * len(shared),
        input_output_aliases={len(args): 0} if shared else {},
        out_specs=[ANY] * len(grad_shapes) + out_specs,
        out_shape=grad_shapes + outs,
        scratch_shapes=scratch,
        compiler_params=params(),
        cost_estimate=cost(tokens, 8 * 512 * 512 + 5 * 8 * 512 * 256),
        name="attend_backward_" + mode,
    )(*args, *shared)
    m = len(grad_shapes)
    return got[:m], got[m:]


def segment_marks(segments):
    flat = segments.reshape(-1)
    hot = flat[:, None] == jnp.arange(128, dtype=jnp.int32)[None, :]
    bar = jnp.where(~hot & (jnp.arange(128) < 8)[None, :], -BIG, 0.0)
    return hot.astype(BF), bar.astype(BF)


def language_marks(segments, language):
    picked = jnp.zeros_like(segments)
    for s in range(language.shape[1]):
        picked = jnp.where(segments == s, language[:, s : s + 1], picked)
    flat = picked.reshape(-1)
    return (flat[:, None] == jnp.arange(128, dtype=jnp.int32)[None, :]).astype(BF)


def layers(
    grid,
    source,
    target,
    source_segments,
    target_segments,
    target_language,
    cotangent,
    enc_qkv,
    enc_out,
    enc_up,
    enc_down,
    enc_vecs,
    enc_bias_up,
    dec_qkv,
    dec_out,
    cross_q,
    cross_kv,
    cross_out,
    dec_up,
    dec_down,
    dec_vecs,
    dec_bias_up,
    lang_table,
):
    unit = enc_qkv.shape[0]
    bias_unit = enc_bias_up.shape[0] // unit
    small = jnp.concatenate(
        [
            lang_table,
            enc_vecs,
            dec_vecs,
            enc_bias_up.reshape(unit, bias_unit),
            dec_bias_up.reshape(unit, bias_unit),
        ],
        axis=1,
    )
    small = jnp.pad(small, ((0, 0), (0, 512 - small.shape[1])))
    feed_forms = [(4, True), (4, False)]
    self_forms = [(3, True), (1, True)]
    cross_forms = [(1, True), (2, True), (1, True)]
    enc_self = Piece(grid, self_forms + [(1, True)])
    dec_self = Piece(grid, self_forms)
    enc_feed = Piece(grid, feed_forms)
    late = Piece(grid, cross_forms + feed_forms, plain=True)
    held = jnp.stack(z_gather(grid, pack(grid, [enc_qkv, enc_out, small, dec_qkv, dec_out])))
    held0, held1 = held[:, : 5 * unit], held[:, 5 * unit :]
    rows2 = pack(grid, after([enc_up, enc_down], held1))
    held2 = z_gather_halves(grid, rows2)
    rows3 = pack(grid, after([cross_q, cross_kv, cross_out, dec_up, dec_down], held1))
    late.arrive(lax.all_gather(rows3, AXES, axis=0, tiled=False))
    held0 = jnp.concatenate(xy_gather(grid, held0), axis=0)
    held0, held2 = after((held0, held2), held1)
    enc_self.arrive(held0, grid.swap_dp(held0, 1))
    held1, held2 = after((held1, held2), held0[0])
    parts1 = xy_gather(grid, held1)
    parts2 = xy_gather_early(grid, held2)

    me = grid.me().astype(jnp.int32).reshape(1)
    source_hot, source_bar = segment_marks(source_segments)
    target_hot, target_bar = segment_marks(target_segments)
    lang = language_marks(target_segments, target_language)

    *enc_saved, vectors, columns = attend_forward(
        "enc", ENC, me, enc_self, 2, (source,), source_hot, source_bar, None
    )
    token = enc_saved[6]
    held1 = jnp.concatenate(after(parts1, token), axis=0)
    dec_self.arrive(held1, grid.swap_dp(held1, 1))
    parts2 = parts2 + xy_gather_rest(grid, after(held2, token))
    enc_bias = columns[:, ENC_UP:DEC_UP].astype(F32).reshape(4, 512)
    dec_bias = columns[:, DEC_UP : DEC_UP + 4].astype(F32).reshape(4, 512)
    *dec_saved, target_low = attend_forward(
        "dec", DEC, me, dec_self, None, (target, lang), target_hot, target_bar, vectors
    )
    held2 = jnp.concatenate(after(parts2, dec_saved[6]), axis=0)
    enc_feed.arrive(held2, grid.swap_dp(held2, 1))
    enc_act, enc_slope, enc_n, enc_inv, encoded = feed_forward(
        ENC + 5, ENC + 3, me, enc_feed, 0, vectors, enc_bias, enc_saved[5]
    )
    *cross_saved, first_low = attend_forward(
        "cross", DEC + 5, me, late, None, (dec_saved[5], encoded), target_hot, source_bar, vectors
    )
    dec_act, dec_slope, dec_n, dec_inv, dec_output = feed_forward(
        DEC + 10, DEC + 8, me, late, 3, vectors, dec_bias, cross_saved[5]
    )

    late_back = Piece(grid, cross_forms + feed_forms, plain=True)
    enc_feed_back = Piece(grid, feed_forms)
    dec_back = Piece(grid, self_forms)
    enc_back = Piece(grid, self_forms + [(1, True)])
    outs, grad_second, dec_feed_sums, dec_bias_grad = feed_backward(
        DEC + 10, DEC + 8, me, late, 3, late_back, 3, vectors, cotangent, dec_n, dec_inv,
        cross_saved[5], dec_act, dec_slope,
    )
    shared = outs[0] if grid.tiled else None
    late_outs, (grad_first, cross_sums, grad_encoded) = attend_backward(
        "cross", DEC + 5, me, late, late_back, 0, vectors, grad_second, cross_saved,
        target_hot, source_bar, first_low, (encoded,), into=shared,
    )
    if not grid.tiled:
        late_outs = list(late_outs[:3]) + list(outs[3:])
    late_total = scatter_plain(grid, *late_back.ready(late_outs))

    outs, grad_enc_first, enc_feed_sums, enc_bias_grad = feed_backward(
        ENC + 5, ENC + 3, me, enc_feed, 0, enc_feed_back, 0, vectors, grad_encoded, enc_n, enc_inv,
        enc_saved[5], enc_act, enc_slope,
    )
    keep2, send2 = enc_feed_back.ready(outs)
    got2 = grid.swap_dp(send2, 1)
    grad_first = after(grad_first, enc_feed_sums)
    outs, (target_grad, dec_sums, lang_grad) = attend_backward(
        "dec", DEC, me, dec_self, dec_back, 0, vectors, grad_first, dec_saved,
        target_hot, target_bar, target_low, (lang,),
    )
    keep3, send3 = dec_back.ready(outs)
    got3 = grid.swap_dp(send3, 1)
    got2 = after(got2, dec_sums)
    held2, sends = core_sum(grid, keep2, got2)
    parts2 = xy_scatter(grid, sends)
    cols = jnp.concatenate([enc_bias_grad.reshape(512, 4), dec_bias_grad.reshape(512, 4)], axis=1)
    cols = jnp.pad(cols, ((0, 0), (ENC_UP, 128 - ENC_UP - 8)))
    grad_enc_first = after(grad_enc_first, got2)
    outs, (source_grad, enc_sums) = attend_backward(
        "enc", ENC, me, enc_self, enc_back, 0, vectors, grad_enc_first, enc_saved,
        source_hot, source_bar, source, (), fixed=(lang_grad, enc_feed_sums, dec_sums, cross_sums, dec_feed_sums, cols),
    )
    keep4, send4 = enc_back.ready(outs)
    got4 = grid.swap_dp(send4, 1)
    got3, parts2 = after((got3, parts2), enc_sums)
    held3, sends = core_sum(grid, keep3, got3)
    parts3 = xy_scatter(grid, sends)
    held4, sends = core_sum(grid, keep4, got4)
    parts4 = xy_scatter(grid, sends)

    def last_swaps(*pieces):
        kind = pieces[0][0].dtype
        sends = [
            jnp.concatenate([xy_sum(grid, p, z).astype(kind) for p in pieces])
            for z in range(1, grid.nf)
        ]
        return [grid.swap_fsdp(s, z) for z, s in zip(range(1, grid.nf), sends)]

    all2, all3, all4 = held2 + parts2, held3 + parts3, held4 + parts4
    enc_up_grad, enc_down_grad, dec_qkv_grad, dec_out_grad = shards(
        grid, [enc_feed_back, dec_back], [all2, all3], last_swaps(all2, all3)
    )
    cross_q_grad, cross_kv_grad, cross_out_grad, dec_up_grad, dec_down_grad = shards(
        grid, [late_back], [[late_total[None]]], []
    )
    enc_qkv_grad, enc_out_grad, rest = shards(grid, [enc_back], [all4], last_swaps(all4))

    return (
        dec_output,
        source_grad,
        target_grad,
        enc_qkv_grad,
        enc_out_grad,
        enc_up_grad,
        enc_down_grad,
        rest[:, ENC:DEC],
        rest[:, ENC_UP:DEC_UP].reshape(-1),
        dec_qkv_grad,
        dec_out_grad,
        cross_q_grad,
        cross_kv_grad,
        cross_out_grad,
        dec_up_grad,
        dec_down_grad,
        rest[:, DEC:ENC_UP],
        rest[:, DEC_UP : DEC_UP + 4].reshape(-1),
        rest[:, :ENC],
    )


def solution(mesh):
    split = P(("dp", "fsdp"))
    return jax.shard_map(
        functools.partial(layers, Grid(mesh)),
        mesh=mesh,
        in_specs=(split,) * 22,
        out_specs=(split,) * 19,
        check_vma=False,
    )
```

```python
import functools

import jax
import jax.numpy as jnp
from jax import lax
from jax.experimental import pallas as pl
from jax.experimental.pallas import tpu as pltpu
from jax.sharding import PartitionSpec as P

AXES = ("dp", "fsdp")
LANGS = 8
ROW = 512
CHUNK = 512
scale_dot = 0.125
norm_eps = 1e-05

ENC = 8
DEC = 16
ENC_UP = 29
DEC_UP = 33
SMALL = ((0, 8), (8, 8), (16, 13), (29, 4), (33, 4))
BF = jnp.bfloat16
F32 = jnp.float32


class Grid:
    def __init__(self, mesh):
        self.nd = mesh.shape["dp"]
        self.nf = mesh.shape["fsdp"]
        self.n = self.nd * self.nf
        self.nh = self.nd // 2
        self.hz = self.nh * self.nf
        self.unit = ROW // self.n
        self.tiled = self.unit % 16 == 0
        self.cut = (self.n, self.unit) if self.tiled else (32, 16)

    def me(self):
        return lax.axis_index("dp") * self.nf + lax.axis_index("fsdp")

    def swap_dp(self, value, flip):
        return lax.ppermute(value, "dp", [(i, i ^ flip) for i in range(self.nd)])

    def swap_fsdp(self, value, flip):
        return lax.ppermute(value, "fsdp", [(i, i ^ flip) for i in range(self.nf)])

    def relative(self, part, at):
        return (at // self.nf * 2 + part) * self.nf + at % self.nf

    def spot(self, me, part, at, across):
        if not across:
            return jnp.bitwise_xor(me, self.relative(part, at))
        flip = (at // self.nf * 2 + part) * self.nf
        return jnp.bitwise_xor(me - lax.rem(me, self.nf), flip) + at % self.nf


def after(value, token):
    if token is None:
        return value
    return lax.optimization_barrier((value, token))[0]


def z_copies(grid, shard):
    return lax.all_to_all(
        jnp.broadcast_to(shard[None], (grid.nf,) + shard.shape), "fsdp", 0, 0, tiled=False
    )


def z_gather(grid, shard):
    return [shard] + [grid.swap_fsdp(shard, m) for m in range(1, grid.nf)]


def z_gather_halves(grid, shard):
    order = [0]
    flips = [1 << b for b in range(grid.nf.bit_length() - 1)]
    held = shard[None]
    for flip in reversed(flips):
        held = jnp.concatenate([held, grid.swap_fsdp(held, flip)])
        order = order + [o | flip for o in order]
    return jnp.stack([held[order.index(z)] for z in range(grid.nf)])


def xy_gather(grid, held):
    return [held] + [grid.swap_dp(held, h << 1) for h in range(1, grid.nh)]


def xy_gather_early(grid, held):
    return [held] + [grid.swap_dp(held, h << 1) for h in range(1, grid.nh - 1)]


def xy_gather_rest(grid, held):
    return [grid.swap_dp(held, grid.nh - 1 << 1)]


def core_sum(grid, keep, got):
    shape = (grid.nh, grid.nf) + keep.shape[1:]
    keep, got = keep.reshape(shape), got.reshape(shape)
    kind = keep.dtype
    sends = [(keep[h].astype(F32) + got[h].astype(F32)).astype(kind) for h in range(1, grid.nh)]
    return [keep[0], got[0]], sends


def xy_scatter(grid, sends):
    return [grid.swap_dp(s, h << 1) for h, s in zip(range(1, grid.nh), sends)]


def xy_sum(grid, parts, z):
    out = parts[0][z].astype(F32)
    for part in parts[1:]:
        out = out + part[z].astype(F32)
    return out


class Piece:
    def __init__(self, grid, forms, plain=False, across=False):
        self.grid, self.forms, self.plain, self.across = grid, forms, plain, across
        self.starts = [sum(b for b, _ in forms[:k]) for k in range(len(forms))]
        self.blocks = sum(b for b, _ in forms)
        self.refs = 1 if plain or not grid.tiled else 2

    def cut(self, k):
        blocks, wide = self.forms[k]
        a, b = self.grid.cut
        return (a, blocks, b, 512) if wide is False else (blocks, a, b, 512)

    def arrive(self, *held):
        grid = self.grid
        if grid.tiled:
            shape = (-1, self.blocks, grid.unit, 512)
            self.arrays = [tuple(near_not(h.reshape(shape)) for h in held)] * len(self.forms)
            return
        whole = jnp.concatenate(held)
        if not self.plain:
            spots = [
                grid.spot(grid.me(), part, at, self.across)
                for part in range(2)
                for at in range(grid.hz)
            ]
            index = jnp.zeros((grid.n,), jnp.int32).at[jnp.stack(spots)].set(
                jnp.arange(grid.n, dtype=jnp.int32)
            )
            whole = jnp.take(whole, index, axis=0)
        self.arrays = []
        for k, (blocks, wide) in enumerate(self.forms):
            row = self.starts[k] * grid.unit
            part = whole[:, row : row + blocks * grid.unit]
            if wide is not False:
                part = part.reshape(grid.n, blocks, grid.unit, 512).transpose(1, 0, 2, 3)
            self.arrays.append((part.reshape(self.cut(k)),))

    def pairs(self, k, me, refs, held):
        grid = self.grid
        blocks, wide = self.forms[k]
        start = self.starts[k]
        if not grid.tiled:
            yield refs[0 if len(refs) == 1 else k], held
        elif self.plain and wide is not False:
            for j in range(blocks):
                yield refs[0].at[:, start + j], held.at[j]
        elif self.plain:
            yield refs[0].at[:, pl.ds(start, blocks)], held
        else:
            for part, ref in enumerate(refs):
                for at in range(grid.hz):
                    i = grid.spot(me, part, at, self.across)
                    yield ref.at[at, pl.ds(start, blocks)], held.at[i] if wide is False else held.at[:, i]

    def fetch(self, k, me, refs, dst, sem):
        for there, here in self.pairs(k, me, refs, dst):
            pltpu.make_async_copy(there, here, sem).start()

    def store(self, k, me, src, refs, sem):
        for there, here in self.pairs(k, me, refs, src):
            pltpu.make_async_copy(here, there, sem).start()

    def out_shapes(self):
        grid = self.grid
        if not grid.tiled:
            return [jax.ShapeDtypeStruct(self.cut(k), BF) for k in range(len(self.forms))]
        if self.plain:
            return [jax.ShapeDtypeStruct((grid.n, self.blocks, grid.unit, 512), BF)]
        return [jax.ShapeDtypeStruct((grid.hz, self.blocks, grid.unit, 512), BF)] * 2

    def ready(self, outs):
        grid = self.grid
        rows = self.blocks * grid.unit
        if grid.tiled:
            return [out.reshape(-1, rows, 512) for out in outs]
        parts = []
        for k, (blocks, wide) in enumerate(self.forms):
            part = outs[k]
            if wide is not False:
                part = part.reshape(blocks, grid.n, grid.unit, 512).transpose(1, 0, 2, 3)
            parts.append(part.reshape(grid.n, blocks * grid.unit, 512))
        whole = jnp.concatenate(parts, axis=1)
        return [whole] if self.plain else spread_blocks(grid, whole)


def scatter_plain(grid, whole):
    rows = whole.shape[1]
    part = lax.psum_scatter(
        whole.reshape(grid.nd, grid.nf * rows, 512), "dp", scatter_dimension=0, tiled=False
    )
    return lax.psum_scatter(
        part.reshape(grid.nf, rows, 512), "fsdp", scatter_dimension=0, tiled=False
    )


def spread_blocks(grid, whole):
    sides = []
    for part in range(2):
        table = [grid.relative(part, at) for at in range(grid.hz)]
        sides.append(jnp.take(whole, jnp.array(table, jnp.int32) ^ grid.me(), axis=0))
    return sides


def finish(ref, sem):
    pltpu.make_async_copy(ref, ref, sem).wait()


def to_rows(shard):
    unit = shard.shape[0]
    blocks = shard.shape[1] // 512
    return shard.reshape(unit, blocks, 512).transpose(1, 0, 2).reshape(blocks * unit, 512)


def fours(rows, start, width):
    k = lax.broadcasted_iota(jnp.int32, (4 * rows, width), 0)
    return lax.broadcasted_iota(jnp.int32, (4 * rows, width), 1) == start + lax.rem(k, 4)


def own_row(rows):
    k = lax.broadcasted_iota(jnp.int32, (rows, 4 * rows), 1)
    return lax.broadcasted_iota(jnp.int32, (rows, 4 * rows), 0) == k // 4


def flatten_fours(value, start):
    rows = value.shape[0]
    wide = lax.dot_general(
        value,
        fours(rows, start, 128).astype(F32),
        (((1,), (1,)), ((), ())),
        precision=lax.Precision.HIGHEST,
        preferred_element_type=F32,
    )
    return jnp.sum(jnp.where(own_row(rows), wide, 0.0), axis=0, keepdims=True)


def place_small(parts, rows):
    total = None
    for (start, width), part in zip(SMALL, parts):
        value = part[...]
        if width == 4:
            value = jnp.where(own_row(rows), value.astype(F32), 0.0).astype(BF)
            spots = fours(rows, start, 512)
        else:
            r = lax.broadcasted_iota(jnp.int32, (width, 512), 0)
            spots = lax.broadcasted_iota(jnp.int32, (width, 512), 1) == start + r
        value = jnp.dot(value, jnp.where(spots, 1.0, 0.0).astype(BF), preferred_element_type=F32)
        total = value if total is None else total + value
    return total.astype(BF)


def pack_kernel(counts, unit, *refs):
    refs = list(refs)
    small = [refs.pop(0) for _ in SMALL]
    groups = [[refs.pop(0) for _ in range(count)] for count in counts]
    refs[0][4 * unit : 5 * unit] = place_small(small, unit)
    for group, out in zip(groups, refs):
        at = 0
        for ref in group:
            rows = ref.shape[0]
            for j in range(ref.shape[1] // 512):
                if out is refs[0] and at == 4 * unit:
                    at += unit
                out[at : at + rows] = ref[:, 512 * j : 512 * (j + 1)]
                at += rows


def pack(grid, small, *groups):
    if not grid.tiled:
        flat = [p.reshape(grid.unit, 4) if w == 4 else p for (_, w), p in zip(SMALL, small)]
        flat = jnp.concatenate(flat, axis=1)
        flat = jnp.pad(flat, ((0, 0), (0, 512 - flat.shape[1])))
        first, *rest = groups
        groups = [list(first[:2]) + [flat] + list(first[2:])] + rest
        return [
            jnp.concatenate([to_rows(a) if a.shape[0] == grid.unit else a for a in arrays])
            for arrays in groups
        ]
    rows = [sum(a.size for a in arrays) // 512 for arrays in groups]
    rows[0] += grid.unit
    flat = [p.reshape(1, -1) if w == 4 else p for (_, w), p in zip(SMALL, small)]
    return pl.pallas_call(
        functools.partial(pack_kernel, [len(arrays) for arrays in groups], grid.unit),
        out_shape=[like(r, 512, BF) for r in rows],
        compiler_params=params(56),
        name="pack",
    )(*flat, *[a for arrays in groups for a in arrays])


def shards_kernel(pieces, counts, *refs):
    refs = list(refs)
    own = [[refs.pop(0) for _ in range(count)] for count in counts[:-1]]
    lasts = [refs.pop(0) for _ in range(counts[-1])]
    at = 0
    for piece, parts in zip(pieces, own):
        rows = piece.blocks * piece.grid.unit
        total = None
        for part in parts:
            total = part[0].astype(F32) if total is None else total + part[0].astype(F32)
        for last in lasts:
            total = total + last[at : at + rows].astype(F32)
        at += rows
        row, unit = 0, piece.grid.unit
        for blocks, wide in piece.forms:
            if wide is None:
                value = total[row : row + unit]
                for start, width in SMALL:
                    out = refs.pop(0)
                    if width == 4:
                        out[...] = flatten_fours(value[:, :128], start)
                    else:
                        out[...] = value[:, start : start + width]
                row += unit
                continue
            out = refs.pop(0)
            for j in range(blocks):
                value = total[row : row + unit]
                if wide:
                    out[:, 512 * j : 512 * (j + 1)] = value
                else:
                    out[unit * j : unit * (j + 1)] = value
                row += unit


def shards(grid, pieces, own, lasts):
    if not grid.tiled:
        total = jnp.concatenate(
            [functools.reduce(lambda a, b: a + b, [p[0].astype(F32) for p in parts]) for parts in own]
        )
        for last in lasts:
            total = total + last.astype(F32)
        outs, row = [], 0
        for piece in pieces:
            for blocks, wide in piece.forms:
                part = total[row : row + blocks * grid.unit]
                if wide is None:
                    outs += [part[:, start : start + width] for start, width in SMALL]
                else:
                    outs.append(from_rows(part, blocks) if wide else part)
                row += blocks * grid.unit
        return outs
    first = lambda a: pl.BlockSpec((1,) + a.shape[1:], lambda i: (0, 0, 0))
    args = [a for parts in own for a in parts] + lasts
    specs = [first(a) for parts in own for a in parts] + [whole_spec(a) for a in lasts]
    shapes = []
    for piece in pieces:
        for blocks, wide in piece.forms:
            if wide is None:
                shapes += [
                    like(1, grid.unit * 4, F32) if width == 4 else like(grid.unit, width, F32)
                    for _, width in SMALL
                ]
            elif wide:
                shapes.append(like(grid.unit, 512 * blocks, F32))
            else:
                shapes.append(like(grid.unit * blocks, 512, F32))
    return pl.pallas_call(
        functools.partial(shards_kernel, pieces, [len(p) for p in own] + [len(lasts)]),
        grid=(1,),
        in_specs=specs,
        out_specs=[whole_spec(s) for s in shapes],
        out_shape=shapes,
        compiler_params=params(56),
        name="shards",
    )(*args)


def from_rows(rows, blocks):
    unit = rows.shape[0] // blocks
    return rows.reshape(blocks, unit, 512).transpose(1, 0, 2).reshape(unit, blocks * 512)


HALF = 64
BIG = float(2**30)


def dot(a, b):
    return jnp.dot(a, b, preferred_element_type=jnp.float32)


def dot_t(a, b):
    return lax.dot_general(a, b, (((1,), (1,)), ((), ())), preferred_element_type=jnp.float32)


def t_dot(a, b):
    return lax.dot_general(a, b, (((0,), (0,)), ((), ())), preferred_element_type=jnp.float32)


def lanes(rows=1, width=128):
    return lax.broadcasted_iota(jnp.int32, (rows, width), 1)


def head_lanes(h):
    return jnp.where(lanes() // HALF == h, 1.0, 0.0).astype(jnp.bfloat16)


def one_lanes(h):
    at = lanes() - HALF * h
    return jnp.where((at >= 8) & (at < 11), 1.0, 0.0).astype(jnp.bfloat16)


def minus_parts(value):
    at = lanes() % HALF
    value = -value
    high = value.astype(jnp.bfloat16).astype(jnp.float32)
    rest = value - high
    mid = rest.astype(jnp.bfloat16).astype(jnp.float32)
    low = rest - mid
    out = jnp.where(at == 8, high, jnp.where(at == 9, mid, jnp.where(at == 10, low, 0.0)))
    return out.astype(jnp.bfloat16)


def pair(value, p):
    return value[:, 128 * p : 128 * (p + 1)]


def norm(summed):
    centred = summed - jnp.mean(summed, axis=-1, keepdims=True)
    inverse = lax.rsqrt(jnp.mean(centred * centred, axis=-1, keepdims=True) + norm_eps)
    return centred * inverse, inverse


def heads_forward(q, k, v, hot, bar):
    outs, logs = [], []
    for p in range(q.shape[1] // 128):
        qa = jnp.concatenate([pair(q, p) * jnp.bfloat16(scale_dot), hot], axis=1)
        total, tops = None, []
        for h in (0, 1):
            mask = head_lanes(h)
            ka = jnp.concatenate([pair(k, p) * mask, bar], axis=1)
            scores = dot_t(qa, ka)
            top = jnp.max(scores, axis=-1, keepdims=True)
            power = jnp.exp(scores - top).astype(jnp.bfloat16)
            va = jnp.concatenate(
                [pair(v, p) * mask, jnp.broadcast_to(mask, (v.shape[0], 128))], axis=1
            )
            part = dot(power, va)
            total = part if total is None else total + part
            tops.append(top)
        sums = total[:, 128:]
        outs.append(total[:, :128] / sums)
        logs.append(jnp.where(lanes() < HALF, tops[0], tops[1]) + jnp.log(sums))
    return jnp.concatenate(outs, axis=1), jnp.concatenate(logs, axis=1)


def heads_backward(go, q, k, v, o, lse, hot, bar):
    gqs, gks, gvs = [], [], []
    at = lax.broadcasted_iota(jnp.int32, (128, 128), 0) // HALF
    to = lax.broadcasted_iota(jnp.int32, (128, 128), 1) // HALF
    same = jnp.where(at == to, 1.0, 0.0).astype(jnp.bfloat16)
    same = jnp.concatenate([same, same], axis=0)
    for p in range(q.shape[1] // 128):
        qs = pair(q, p) * jnp.bfloat16(scale_dot)
        gp = pair(go, p)
        prod = gp.astype(jnp.float32) * pair(o, p)
        high = prod.astype(jnp.bfloat16)
        low = (prod - high.astype(jnp.float32)).astype(jnp.bfloat16)
        delta = dot(jnp.concatenate([high, low], axis=1), same)
        qa = jnp.concatenate([qs, hot + minus_parts(pair(lse, p))], axis=1)
        ga = jnp.concatenate([gp, minus_parts(delta)], axis=1)
        gq = gk = gv = None
        for h in (0, 1):
            mask, one = head_lanes(h), one_lanes(h)
            km = pair(k, p) * mask
            ka = jnp.concatenate([km, bar + one], axis=1)
            va = jnp.concatenate(
                [pair(v, p) * mask, jnp.broadcast_to(one, (v.shape[0], 128))], axis=1
            )
            probs = jnp.exp(dot_t(ka, qa))
            gs = (probs * dot_t(va, ga)).astype(jnp.bfloat16)
            gv_h = dot(probs.astype(jnp.bfloat16), gp * mask)
            gk_h = dot(gs, qs * mask)
            gq_h = t_dot(gs, km)
            gv = gv_h if gv is None else gv + gv_h
            gk = gk_h if gk is None else gk + gk_h
            gq = gq_h if gq is None else gq + gq_h
        gqs.append((gq * scale_dot).astype(jnp.bfloat16))
        gks.append(gk.astype(jnp.bfloat16))
        gvs.append(gv.astype(jnp.bfloat16))
    return tuple(jnp.concatenate(x, axis=1) for x in (gqs, gks, gvs))


def norm_back(grad, normed, inverse, gain):
    scaled = grad * gain
    back = inverse * (
        scaled
        - jnp.mean(scaled, axis=-1, keepdims=True)
        - normed * jnp.mean(scaled * normed, axis=-1, keepdims=True)
    )
    return back, jnp.sum(grad * normed, axis=0), jnp.sum(grad, axis=0)


def square(ref, k):
    return ref[k].reshape(512, 512)


def vec(vectors, k):
    return vectors[k : k + 1, :]


ANY = pl.BlockSpec(memory_space=pl.ANY)
SMEM = pl.BlockSpec(memory_space=pltpu.SMEM)


def whole_spec(array):
    return pl.BlockSpec(array.shape, lambda i: (0,) * array.ndim)


def row_spec(array):
    return pl.BlockSpec((ROW,) + array.shape[1:], lambda i: (i,) + (0,) * (array.ndim - 1))


def near_not(array):
    return pltpu.with_memory_space_constraint(array, pltpu.HBM)


def far(shape):
    return pltpu.HBM(shape.shape, shape.dtype)


def like(rows, width, kind):
    return jax.ShapeDtypeStruct((rows, width), kind)


def params(mebibytes):
    return pltpu.CompilerParams(vmem_limit_bytes=mebibytes * 1024 * 1024)


def cost(tokens, macs):
    return pl.CostEstimate(
        flops=2 * tokens * macs, bytes_accessed=16 * tokens * 512, transcendentals=0
    )


def attend_forward_kernel(mode, base, piece, small, *refs):
    refs = list(refs)
    me_ref = refs.pop(0)
    count = piece.refs
    take = lambda k: [refs.pop(0) for _ in range(k)]
    proj_refs = [take(count) for _ in range(3 if mode == "cross" else 2)]
    small_refs = take(count) if small is not None else None
    vectors_ref = None if small is not None else refs.pop(0)
    if mode == "cross":
        normed_ref, memory_ref = take(2)
    else:
        x_ref = refs.pop(0)
        if mode == "dec":
            lang_ref = refs.pop(0)
    hot_ref, bar_ref = take(2)
    q_out, k_out, v_out, o_out, lse_out, n_out, inv_out = take(7)
    if mode != "enc":
        low_out = refs.pop(0)
    if small is not None:
        vectors_out, small_out = take(2)
    weights = take(3 if mode == "cross" else 2)
    small_scr = refs.pop(0) if small is not None else None
    sems = refs.pop(0)
    out_w = weights[-1]

    @pl.when(pl.program_id(0) == 0)
    def _():
        me = me_ref[0]
        for k, (source, dst) in enumerate(zip(proj_refs, weights)):
            piece.fetch(k, me, source, dst, sems.at[k])
        if small is not None:
            piece.fetch(small, me, small_refs, small_scr, sems.at[3])
            finish(small_scr, sems.at[3])
            block = small_scr[0].reshape(512, 512)[:, :128]
            small_out[...] = block
            vectors_out[...] = block.astype(F32).T
        for k, dst in enumerate(weights):
            finish(dst, sems.at[k])

    vectors = (vectors_out if small is not None else vectors_ref)[...]
    if mode == "enc":
        low = x_ref[...]
        residual = low.astype(F32)
        memory = low
    elif mode == "dec":
        residual = x_ref[...].astype(F32) + dot(lang_ref[...], vectors.astype(BF))
        low = memory = residual.astype(BF)
    else:
        residual = normed_ref[...] * vec(vectors, DEC + 3) + vec(vectors, DEC + 4)
        low = residual.astype(BF)
        memory = memory_ref[...]
    if mode != "enc":
        low_out[...] = low
    if mode == "cross":
        wq, wk, wv = square(weights[0], 0), square(weights[1], 0), square(weights[1], 1)
    else:
        wq, wk, wv = (square(weights[0], j) for j in range(3))
    q = (dot(low, wq) + vec(vectors, base)).astype(BF)
    k = dot(memory, wk).astype(BF)
    v = (dot(memory, wv) + vec(vectors, base + 1)).astype(BF)
    q_out[...], k_out[...], v_out[...] = q, k, v
    o, lse = heads_forward(q, k, v, hot_ref[...], bar_ref[...])
    o_out[...], lse_out[...] = o, lse
    branch = dot(o.astype(BF), square(out_w, 0)) + vec(vectors, base + 2)
    n_out[...], inv_out[...] = norm(residual + branch)


def attend_forward(mode, base, me, piece, small, inputs, hot, bar, vectors):
    grid = piece.grid
    tokens = hot.shape[0]
    names = range(3 if mode == "cross" else 2)
    weights = [a for k in names for a in piece.arrays[k]]
    args = [me] + weights
    specs = [SMEM] + [ANY] * len(weights)
    if small is not None:
        args += list(piece.arrays[small])
        specs += [ANY] * len(piece.arrays[small])
    else:
        args.append(vectors)
        specs.append(whole_spec(vectors))
    rows = [near_not(inputs[0])] + list(inputs[1:]) + [hot, bar]
    args += rows
    specs += [row_spec(a) for a in rows]
    outs = [like(tokens, 512, BF)] * 3 + [like(tokens, 512, F32)] * 3 + [like(tokens, 1, F32)]
    if mode != "enc":
        outs.append(like(tokens, 512, BF))
    out_specs = [row_spec(o) for o in outs]
    outs = [o if i == 5 and mode == "cross" else far(o) for i, o in enumerate(outs)]
    scratch = [pltpu.VMEM(piece.cut(k), BF) for k in names]
    if small is not None:
        extra = [like(128, 512, F32), like(512, 128, BF)]
        outs += extra
        out_specs += [whole_spec(e) for e in extra]
        scratch.append(pltpu.VMEM(piece.cut(small), BF))
    scratch.append(pltpu.SemaphoreType.DMA((4,)))
    return pl.pallas_call(
        functools.partial(attend_forward_kernel, mode, base, piece, small),
        grid=(tokens // ROW,),
        in_specs=specs,
        out_specs=out_specs,
        out_shape=outs,
        scratch_shapes=scratch,
        compiler_params=params(24),
        cost_estimate=cost(tokens, 4 * 512 * 512 + 2 * 8 * 512 * 256),
        name="attend_forward_" + mode,
    )(*args)


def feed_forward_kernel(base, first, piece, own, *refs):
    refs = list(refs)
    me_ref = refs.pop(0)
    count = piece.refs
    take = lambda k: [refs.pop(0) for _ in range(k)]
    up_refs, down_refs = take(count), take(count)
    vectors_ref, bias_ref, n_ref = take(3)
    act_out, slope_out, n_out, inv_out, low_out = take(5)
    up, down, sems = take(3)

    @pl.when(pl.program_id(0) == 0)
    def _():
        me = me_ref[0]
        piece.fetch(own, me, up_refs, up, sems.at[0])
        piece.fetch(own + 1, me, down_refs, down, sems.at[1])
        finish(up, sems.at[0])
        finish(down, sems.at[1])

    vectors = vectors_ref[...]
    x = n_ref[...] * vec(vectors, first) + vec(vectors, first + 1)
    low = x.astype(BF)
    branch = None
    for j in range(4):
        h = dot(low, square(up, j)) + bias_ref[j : j + 1, :]
        act, slope = gate(h)
        act = act.astype(BF)
        act_out[j], slope_out[j] = act, slope.astype(BF)
        part = dot(act, tall(down, j))
        branch = part if branch is None else branch + part
    n, inv = norm(x + branch + vec(vectors, base))
    n_out[...], inv_out[...] = n, inv
    low_out[...] = (n * vec(vectors, base + 1) + vec(vectors, base + 2)).astype(BF)


def gate(h):
    c = 0.7978845608028654
    square_h = h * h
    t = jnp.tanh(h * (c + (c * 0.044715) * square_h))
    half = 0.5 + 0.5 * t
    slope = half + (0.5 * h) * (1.0 - t * t) * (c + (3.0 * c * 0.044715) * square_h)
    return h * half, slope


def tall(ref, j):
    size = ref.shape[0] // 4
    return ref[size * j : size * (j + 1)].reshape(512, 512)


def feed_forward(base, first, me, piece, own, vectors, bias, n):
    tokens = n.shape[0]
    weights = list(piece.arrays[own]) + list(piece.arrays[own + 1])
    chunk = jax.ShapeDtypeStruct((4, tokens, 512), BF)
    chunk_spec = pl.BlockSpec((4, ROW, 512), lambda i: (0, i, 0))
    outs = [chunk, chunk, like(tokens, 512, F32), like(tokens, 1, F32), like(tokens, 512, BF)]
    out_specs = [chunk_spec, chunk_spec] + [row_spec(o) for o in outs[2:]]
    outs = [far(o) for o in outs[:4]] + outs[4:]
    return pl.pallas_call(
        functools.partial(feed_forward_kernel, base, first, piece, own),
        grid=(tokens // ROW,),
        in_specs=[SMEM]
        + [ANY] * len(weights)
        + [whole_spec(vectors), whole_spec(bias), row_spec(n)],
        out_specs=out_specs,
        out_shape=outs,
        scratch_shapes=[
            pltpu.VMEM(piece.cut(own), BF),
            pltpu.VMEM(piece.cut(own + 1), BF),
            pltpu.SemaphoreType.DMA((2,)),
        ],
        compiler_params=params(26),
        cost_estimate=cost(tokens, 8 * 512 * 512),
        name="feed_forward",
    )(me, *weights, vectors, bias, near_not(n))


def feed_backward_kernel(base, first, piece, own, grads, at, *refs):
    refs = list(refs)
    me_ref = refs.pop(0)
    count = piece.refs
    take = lambda k: [refs.pop(0) for _ in range(k)]
    up_refs, down_refs = take(count), take(count)
    vectors_ref, grad_ref, n2_ref, inv2_ref, n1_ref, act_ref, slope_ref = take(7)
    grad_outs = take(len(grads.out_shapes()))
    dx_out, sums_out, bias_out = take(3)
    up, down, d_up, d_down, low_t, branch, sems = take(7)
    j = pl.program_id(0)
    vectors = vectors_ref[...]

    @pl.when(j == 0)
    def _():
        me = me_ref[0]
        piece.fetch(own, me, up_refs, up, sems.at[0])
        piece.fetch(own + 1, me, down_refs, down, sems.at[1])
        sums_out[...] = jnp.zeros_like(sums_out)
        for t in range(grad_ref.shape[0] // ROW):
            part = pl.ds(ROW * t, ROW)
            back, gain, shift = norm_back(
                grad_ref[part].astype(F32), n2_ref[part], inv2_ref[part], vec(vectors, base + 1)
            )
            dx_out[part] = back
            low = back.astype(BF)
            branch[part] = low
            sums_out[0:1] += jnp.sum(low.astype(F32), axis=0, keepdims=True)
            sums_out[1:2] += gain[None]
            sums_out[2:3] += shift[None]
            x = n1_ref[part] * vec(vectors, first) + vec(vectors, first + 1)
            low_t[:, part] = x.astype(BF).T
        finish(up, sems.at[0])
        finish(down, sems.at[1])

    size = down.shape[0] // 4
    down_j = down[pl.ds(size * j, size)].reshape(512, 512)
    up_j = up[j].reshape(512, 512)
    low = branch[...]
    hidden = (dot_t(low, down_j) * slope_ref[0].astype(F32)).astype(BF)
    bias_out[0] = jnp.broadcast_to(
        jnp.sum(hidden.astype(F32), axis=0, keepdims=True), bias_out.shape[1:]
    )
    dx_out[...] += dot_t(hidden, up_j)
    d_up[j] = dot(low_t[...], hidden).astype(BF).reshape(d_up.shape[1:])
    d_down[pl.ds(size * j, size)] = (
        t_dot(act_ref[0], low).astype(BF).reshape((size,) + d_down.shape[1:])
    )

    @pl.when(j == pl.num_programs(0) - 1)
    def _():
        me = me_ref[0]
        grads.store(at, me, d_up, grad_outs, sems.at[0])
        grads.store(at + 1, me, d_down, grad_outs, sems.at[1])
        finish(d_up, sems.at[0])
        finish(d_down, sems.at[1])


def feed_backward(base, first, me, piece, own, grads, at, vectors, grad, n2, inv2, n1, act, slope):
    tokens = n1.shape[0]
    weights = list(piece.arrays[own]) + list(piece.arrays[own + 1])
    act, slope, n2, inv2, n1 = (near_not(a) for a in (act, slope, n2, inv2, n1))
    held = [vectors, grad, n2, inv2, n1]
    chunk_spec = pl.BlockSpec((1, tokens, 512), lambda i: (i, 0, 0))
    outs = [like(tokens, 512, F32), like(8, 512, F32), jax.ShapeDtypeStruct((4, 8, 512), F32)]
    got = pl.pallas_call(
        functools.partial(feed_backward_kernel, base, first, piece, own, grads, at),
        grid=(4,),
        in_specs=[SMEM]
        + [ANY] * len(weights)
        + [whole_spec(a) for a in held]
        + [chunk_spec, chunk_spec],
        out_specs=[ANY] * len(grads.out_shapes())
        + [whole_spec(outs[0]), whole_spec(outs[1]), pl.BlockSpec((1, 8, 512), lambda i: (i, 0, 0))],
        out_shape=[far(s) for s in grads.out_shapes()] + [far(outs[0])] + outs[1:],
        scratch_shapes=[
            pltpu.VMEM(piece.cut(own), BF),
            pltpu.VMEM(piece.cut(own + 1), BF),
            pltpu.VMEM(grads.cut(at), BF),
            pltpu.VMEM(grads.cut(at + 1), BF),
            pltpu.VMEM((512, tokens), BF),
            pltpu.VMEM((tokens, 512), BF),
            pltpu.SemaphoreType.DMA((2,)),
        ],
        compiler_params=params(32),
        cost_estimate=cost(tokens, 16 * 512 * 512),
        name="feed_backward",
    )(me, *weights, *held, act, slope)
    m = len(grads.out_shapes())
    return got[:m], got[m], got[m + 1], got[m + 2][:, 0, :]


def feed_both_kernel(base, first, piece, own, grads, at, tiles, *refs):
    refs = list(refs)
    me_ref = refs.pop(0)
    take = lambda k: [refs.pop(0) for _ in range(k)]
    up_refs, down_refs = take(piece.refs), take(piece.refs)
    vectors_ref, bias_ref, n1_ref, grad_ref = take(4)
    grad_outs = take(len(grads.out_shapes()))
    low_out, dx_out, sums_out, bias_out = take(4)
    up, down, d_up, d_down, acts, slopes, low_t, branches, sems = take(9)
    step = pl.program_id(0)
    vectors = vectors_ref[...]

    @pl.when(step == 0)
    def _():
        me = me_ref[0]
        piece.fetch(own, me, up_refs, up, sems.at[0])
        piece.fetch(own + 1, me, down_refs, down, sems.at[1])
        sums_out[...] = jnp.zeros_like(sums_out)
        finish(up, sems.at[0])
        finish(down, sems.at[1])

    @pl.when(step < tiles)
    def _():
        x = n1_ref[...] * vec(vectors, first) + vec(vectors, first + 1)
        low = x.astype(BF)
        rows = pl.ds(pl.multiple_of(step * ROW, ROW), ROW)
        branch = None
        for j in range(4):
            h = dot(low, square(up, j)) + bias_ref[j : j + 1, :]
            act, slope = gate(h)
            act = act.astype(BF)
            acts[j, rows], slopes[j, rows] = act, slope.astype(BF)
            part = dot(act, tall(down, j))
            branch = part if branch is None else branch + part
        n, inv = norm(x + branch + vec(vectors, base))
        gain = vec(vectors, base + 1)
        low_out[...] = (n * gain + vec(vectors, base + 2)).astype(BF)
        back, d_gain, d_shift = norm_back(grad_ref[...].astype(F32), n, inv, gain)
        dx_out[rows] = back
        back = back.astype(BF)
        branches[rows] = back
        sums_out[0:1] += jnp.sum(back.astype(F32), axis=0, keepdims=True)
        sums_out[1:2] += d_gain[None]
        sums_out[2:3] += d_shift[None]
        low_t[:, rows] = low.T

    @pl.when(step >= tiles)
    def _():
        j = step - tiles
        size = down.shape[0] // 4
        low = branches[...]
        hidden = dot_t(low, down[pl.ds(size * j, size)].reshape(512, 512))
        hidden = (hidden * slopes[j].astype(F32)).astype(BF)
        bias_out[0] = jnp.broadcast_to(
            jnp.sum(hidden.astype(F32), axis=0, keepdims=True), bias_out.shape[1:]
        )
        dx_out[...] += dot_t(hidden, up[j].reshape(512, 512))
        d_up[j] = dot(low_t[...], hidden).astype(BF).reshape(d_up.shape[1:])
        d_down[pl.ds(size * j, size)] = (
            t_dot(acts[j], low).astype(BF).reshape((size,) + d_down.shape[1:])
        )

    @pl.when(step == pl.num_programs(0) - 1)
    def _():
        me = me_ref[0]
        grads.store(at, me, d_up, grad_outs, sems.at[0])
        grads.store(at + 1, me, d_down, grad_outs, sems.at[1])
        finish(d_up, sems.at[0])
        finish(d_down, sems.at[1])


def feed_both(base, first, me, piece, own, grads, at, vectors, bias, n1, grad):
    tokens = n1.shape[0]
    tiles = tokens // ROW
    weights = list(piece.arrays[own]) + list(piece.arrays[own + 1])
    tile_spec = pl.BlockSpec((ROW, 512), lambda i: (jnp.minimum(i, tiles - 1), 0))
    outs = [
        like(tokens, 512, BF),
        like(tokens, 512, F32),
        like(8, 512, F32),
        jax.ShapeDtypeStruct((4, 8, 512), F32),
    ]
    got = pl.pallas_call(
        functools.partial(feed_both_kernel, base, first, piece, own, grads, at, tiles),
        grid=(tiles + 4,),
        in_specs=[SMEM]
        + [ANY] * len(weights)
        + [whole_spec(vectors), whole_spec(bias), tile_spec, tile_spec],
        out_specs=[ANY] * len(grads.out_shapes())
        + [
            tile_spec,
            whole_spec(outs[1]),
            whole_spec(outs[2]),
            pl.BlockSpec((1, 8, 512), lambda i: (jnp.maximum(i - tiles, 0), 0, 0)),
        ],
        out_shape=[far(s) for s in grads.out_shapes()] + outs,
        scratch_shapes=[
            pltpu.VMEM(piece.cut(own), BF),
            pltpu.VMEM(piece.cut(own + 1), BF),
            pltpu.VMEM(grads.cut(at), BF),
            pltpu.VMEM(grads.cut(at + 1), BF),
            pltpu.VMEM((4, tokens, 512), BF),
            pltpu.VMEM((4, tokens, 512), BF),
            pltpu.VMEM((512, tokens), BF),
            pltpu.VMEM((tokens, 512), BF),
            pltpu.SemaphoreType.DMA((2,)),
        ],
        compiler_params=params(44),
        cost_estimate=cost(tokens, 24 * 512 * 512),
        name="feed_both",
    )(me, *weights, vectors, bias, n1, grad)
    m = len(grads.out_shapes())
    return got[:m], got[m], got[m + 1], got[m + 2], got[m + 3][:, 0, :]


def attend_backward_kernel(mode, base, piece, grads, first, shared, *refs):
    refs = list(refs)
    me_ref = refs.pop(0)
    count = piece.refs
    take = lambda k: [refs.pop(0) for _ in range(k)]
    kinds = 3 if mode == "cross" else 2
    weight_refs = [take(count) for _ in range(kinds)]
    vectors_ref, grad_ref, n_ref, inv_ref, q_ref, k_ref, v_ref, o_ref, lse_ref = take(9)
    hot_ref, bar_ref, low_ref = take(3)
    memory_ref = refs.pop(0) if mode == "cross" else None
    lang_ref = refs.pop(0) if mode == "dec" else None
    sum_refs = take(5) if mode == "enc" else None
    cols_ref = refs.pop(0) if mode == "enc" else None
    if shared:
        refs.pop(0)
    grad_outs = take(len(grads.out_shapes()))
    dx_out, sums_out = take(2)
    dm_out = refs.pop(0) if mode == "cross" else None
    lang_out = refs.pop(0) if mode == "dec" else None
    staged_kinds = 2 if mode == "dec" else 3
    weights, staged = take(kinds), take(staged_kinds)
    low_t, o_t, gqs, gks, gvs, gbs, sems = take(7)
    memory_t = refs.pop(0) if mode == "cross" else None
    all_sums = refs.pop(0) if mode == "enc" else None
    step = pl.program_id(0)
    vectors = vectors_ref[...]

    @pl.when(step == 0)
    def _():
        me = me_ref[0]
        for k, (source, dst) in enumerate(zip(weight_refs, weights)):
            piece.fetch(k, me, source, dst, sems.at[k])
        sums_out[...] = jnp.zeros_like(sums_out)
        if mode == "dec":
            lang_out[...] = jnp.zeros_like(lang_out)
        for k, dst in enumerate(weights):
            finish(dst, sems.at[k])

    back, gain, shift = norm_back(
        grad_ref[...], n_ref[...], inv_ref[...], vec(vectors, base + 3)
    )
    gb = back.astype(BF)
    go = dot_t(gb, square(weights[-1], 0)).astype(BF)
    q, k, v, o = q_ref[...], k_ref[...], v_ref[...], o_ref[...]
    gq, gk, gv = heads_backward(go, q, k, v, o, lse_ref[...], hot_ref[...], bar_ref[...])
    if mode == "cross":
        wq, wk, wv = square(weights[0], 0), square(weights[1], 0), square(weights[1], 1)
    else:
        wq, wk, wv = (square(weights[0], j) for j in range(3))
    dx = back + dot_t(gq, wq)
    dm = dot_t(gk, wk) + dot_t(gv, wv)
    if mode == "cross":
        dx_out[...] = dx
        dm_out[...] = dm
    else:
        dx = dx + dm
        dx_out[...] = dx.astype(BF)
    if mode == "dec":
        high = dx.astype(BF)
        rest = (dx - high.astype(F32)).astype(BF)
        hot_lang = lang_ref[...].T
        lang_out[...] += dot(hot_lang, high) + dot(hot_lang, rest)
    sums_out[0:1] += jnp.sum(gq.astype(F32), axis=0, keepdims=True)
    sums_out[1:2] += jnp.sum(gv.astype(F32), axis=0, keepdims=True)
    sums_out[2:3] += jnp.sum(gb.astype(F32), axis=0, keepdims=True)
    sums_out[3:4] += gain[None]
    sums_out[4:5] += shift[None]
    part = pl.ds(pl.multiple_of(step * ROW, ROW), ROW)
    gqs[part], gks[part], gvs[part], gbs[part] = gq, gk, gv, gb
    low_t[:, part] = low_ref[...].T
    o_t[:, part] = o.astype(BF).T
    if mode == "cross":
        memory_t[:, part] = memory_ref[...].T

    @pl.when(step == pl.num_programs(0) - 1)
    def _():
        me = me_ref[0]
        shape = staged[0].shape[1:]
        out_grad = dot(o_t[...], gbs[...]).astype(BF).reshape(shape)
        gq_grad = dot(low_t[...], gqs[...]).astype(BF).reshape(shape)
        kv_t = (memory_t if mode == "cross" else low_t)[...]
        gk_grad = dot(kv_t, gks[...]).astype(BF).reshape(shape)
        gv_grad = dot(kv_t, gvs[...]).astype(BF).reshape(shape)
        if mode == "cross":
            staged[0][0] = gq_grad
            staged[1][0], staged[1][1] = gk_grad, gv_grad
        else:
            staged[0][0], staged[0][1], staged[0][2] = gq_grad, gk_grad, gv_grad
        staged[kinds - 1][0] = out_grad
        if mode == "enc":
            all_sums[...] = jnp.zeros_like(all_sums)
            row = 0
            counts = (8, 5, 3, 5, 5, 3)
            for ref, count in zip([sum_refs[0], sums_out] + sum_refs[1:], counts):
                all_sums[row : row + count] = ref[:count]
                row += count
            block = (all_sums[...].T + cols_ref[...]).astype(BF)
            block = jnp.concatenate([block, jnp.zeros((512, 384), BF)], axis=1)
            staged[2][0] = block.reshape(shape)
        for k, src in enumerate(staged):
            grads.store(first + k, me, src, grad_outs, sems.at[k])
        for k, src in enumerate(staged):
            finish(src, sems.at[k])


def attend_backward(
    mode, base, me, piece, grads, first, vectors, grad, saved, hot, bar, low, extra, fixed=(), into=None
):
    q, k, v, o, lse, n, inv = (near_not(a) for a in saved)
    low = near_not(low)
    extra = [near_not(a) for a in extra]
    grad = grad if mode == "cross" else near_not(grad)
    tokens = hot.shape[0]
    kinds = range(3 if mode == "cross" else 2)
    weights = [a for i in kinds for a in piece.arrays[i]]
    rows = [grad, n, inv, q, k, v, o, lse, hot, bar, low] + list(extra)
    outs = [like(tokens, 512, F32 if mode == "cross" else BF), like(8, 512, F32)]
    out_specs = [row_spec(outs[0]), whole_spec(outs[1])]
    if mode == "cross":
        outs.append(like(tokens, 512, F32))
        out_specs.append(row_spec(outs[-1]))
    if mode == "dec":
        outs.append(like(128, 512, F32))
        out_specs.append(whole_spec(outs[-1]))
    grad_shapes = grads.out_shapes()
    scratch = [pltpu.VMEM(piece.cut(i), BF) for i in kinds]
    scratch += [pltpu.VMEM(grads.cut(first + i), BF) for i in range(2 if mode == "dec" else 3)]
    scratch += [pltpu.VMEM((512, tokens), BF)] * 2 + [pltpu.VMEM((tokens, 512), BF)] * 4
    scratch.append(pltpu.SemaphoreType.DMA((3,)))
    if mode == "cross":
        scratch.append(pltpu.VMEM((512, tokens), BF))
    if mode == "enc":
        scratch.append(pltpu.VMEM((128, 512), F32))
    args = [me, *weights, vectors, *rows, *fixed]
    shared = [] if into is None else [into]
    got = pl.pallas_call(
        functools.partial(attend_backward_kernel, mode, base, piece, grads, first, bool(shared)),
        grid=(tokens // ROW,),
        in_specs=[SMEM]
        + [ANY] * len(weights)
        + [whole_spec(vectors)]
        + [row_spec(a) for a in rows]
        + [whole_spec(a) for a in fixed]
        + [ANY] * len(shared),
        input_output_aliases={len(args): 0} if shared else {},
        out_specs=[ANY] * len(grad_shapes) + out_specs,
        out_shape=[far(s) for s in grad_shapes] + [far(outs[0])] + outs[1:],
        scratch_shapes=scratch,
        compiler_params=params(42),
        cost_estimate=cost(tokens, 8 * 512 * 512 + 5 * 8 * 512 * 256),
        name="attend_backward_" + mode,
    )(*args, *shared)
    m = len(grad_shapes)
    return got[:m], got[m:]


def segment_marks(segments):
    flat = segments.reshape(-1)
    hot = flat[:, None] == jnp.arange(128, dtype=jnp.int32)[None, :]
    bar = jnp.where(~hot & (jnp.arange(128) < 8)[None, :], -BIG, 0.0)
    return hot.astype(BF), bar.astype(BF)


def language_marks(segments, language):
    picked = jnp.zeros_like(segments)
    for s in range(language.shape[1]):
        picked = jnp.where(segments == s, language[:, s : s + 1], picked)
    flat = picked.reshape(-1)
    return (flat[:, None] == jnp.arange(128, dtype=jnp.int32)[None, :]).astype(BF)


def layers(
    grid,
    source,
    target,
    source_segments,
    target_segments,
    target_language,
    cotangent,
    enc_qkv,
    enc_out,
    enc_up,
    enc_down,
    enc_vecs,
    enc_bias_up,
    dec_qkv,
    dec_out,
    cross_q,
    cross_kv,
    cross_out,
    dec_up,
    dec_down,
    dec_vecs,
    dec_bias_up,
    lang_table,
):
    unit = enc_qkv.shape[0]
    feed_forms = [(4, True), (4, False)]
    self_forms = [(3, True), (1, True)]
    cross_forms = [(1, True), (2, True), (1, True)]
    enc_self = Piece(grid, self_forms + [(1, True)])
    dec_self = Piece(grid, self_forms)
    enc_feed = Piece(grid, feed_forms)
    late = Piece(grid, cross_forms + feed_forms, plain=True)
    rows01, rows2, rows3 = pack(
        grid,
        [lang_table, enc_vecs, dec_vecs, enc_bias_up, dec_bias_up],
        [enc_qkv, enc_out, dec_qkv, dec_out],
        [enc_up, enc_down],
        [cross_q, cross_kv, cross_out, dec_up, dec_down],
    )
    held = jnp.stack(z_gather(grid, rows01))
    held0, held1 = held[:, : 5 * unit], held[:, 5 * unit :]
    held2 = z_gather_halves(grid, after(rows2, held1))
    late.arrive(lax.all_gather(rows3, AXES, axis=0, tiled=False))
    held0 = jnp.concatenate(xy_gather(grid, held0), axis=0)
    held0, held2 = after((held0, held2), held1)
    enc_self.arrive(held0, grid.swap_dp(held0, 1))
    held1, held2 = after((held1, held2), held0[0])
    parts1 = xy_gather(grid, held1)
    parts2 = xy_gather_early(grid, held2)

    me = grid.me().astype(jnp.int32).reshape(1)
    source_hot, source_bar = segment_marks(source_segments)
    target_hot, target_bar = segment_marks(target_segments)
    lang = language_marks(target_segments, target_language)

    *enc_saved, vectors, columns = attend_forward(
        "enc", ENC, me, enc_self, 2, (source,), source_hot, source_bar, None
    )
    token = enc_saved[6]
    held1 = jnp.concatenate(after(parts1, token), axis=0)
    dec_self.arrive(held1, grid.swap_dp(held1, 1))
    parts2 = parts2 + xy_gather_rest(grid, after(held2, token))
    enc_bias = columns[:, ENC_UP:DEC_UP].astype(F32).reshape(4, 512)
    dec_bias = columns[:, DEC_UP : DEC_UP + 4].astype(F32).reshape(4, 512)
    *dec_saved, target_low = attend_forward(
        "dec", DEC, me, dec_self, None, (target, lang), target_hot, target_bar, vectors
    )
    held2 = jnp.concatenate(after(parts2, dec_saved[6]), axis=0)
    enc_feed.arrive(held2, grid.swap_dp(held2, 1))
    enc_act, enc_slope, enc_n, enc_inv, encoded = feed_forward(
        ENC + 5, ENC + 3, me, enc_feed, 0, vectors, enc_bias, enc_saved[5]
    )
    *cross_saved, first_low = attend_forward(
        "cross", DEC + 5, me, late, None, (dec_saved[5], encoded), target_hot, source_bar, vectors
    )
    late_back = Piece(grid, cross_forms + feed_forms, plain=True)
    enc_feed_back = Piece(grid, feed_forms)
    dec_back = Piece(grid, self_forms)
    enc_back = Piece(grid, self_forms + [(1, None)])
    outs, dec_output, grad_second, dec_feed_sums, dec_bias_grad = feed_both(
        DEC + 10, DEC + 8, me, late, 3, late_back, 3, vectors, dec_bias, cross_saved[5], cotangent
    )
    shared = outs[0] if grid.tiled else None
    late_outs, (grad_first, cross_sums, grad_encoded) = attend_backward(
        "cross", DEC + 5, me, late, late_back, 0, vectors, grad_second, cross_saved,
        target_hot, source_bar, first_low, (encoded,), into=shared,
    )
    if not grid.tiled:
        late_outs = list(late_outs[:3]) + list(outs[3:])
    late_total = scatter_plain(grid, *late_back.ready(late_outs))

    outs, grad_enc_first, enc_feed_sums, enc_bias_grad = feed_backward(
        ENC + 5, ENC + 3, me, enc_feed, 0, enc_feed_back, 0, vectors, grad_encoded, enc_n, enc_inv,
        enc_saved[5], enc_act, enc_slope,
    )
    keep2, send2 = enc_feed_back.ready(outs)
    got2 = grid.swap_dp(send2, 1)
    grad_first = after(grad_first, enc_feed_sums)
    outs, (target_grad, dec_sums, lang_grad) = attend_backward(
        "dec", DEC, me, dec_self, dec_back, 0, vectors, grad_first, dec_saved,
        target_hot, target_bar, target_low, (lang,),
    )
    keep3, send3 = dec_back.ready(outs)
    got3 = grid.swap_dp(send3, 1)
    got2 = after(got2, dec_sums)
    held2, sends = core_sum(grid, keep2, got2)
    parts2 = xy_scatter(grid, sends)
    cols = jnp.concatenate([enc_bias_grad.reshape(512, 4), dec_bias_grad.reshape(512, 4)], axis=1)
    cols = jnp.pad(cols, ((0, 0), (ENC_UP, 128 - ENC_UP - 8)))
    grad_enc_first = after(grad_enc_first, got2)
    outs, (source_grad, enc_sums) = attend_backward(
        "enc", ENC, me, enc_self, enc_back, 0, vectors, grad_enc_first, enc_saved,
        source_hot, source_bar, source, (), fixed=(lang_grad, enc_feed_sums, dec_sums, cross_sums, dec_feed_sums, cols),
    )
    keep4, send4 = enc_back.ready(outs)
    got4 = grid.swap_dp(send4, 1)
    got3, parts2 = after((got3, parts2), enc_sums)
    held3, sends = core_sum(grid, keep3, got3)
    parts3 = xy_scatter(grid, sends)
    held4, sends = core_sum(grid, keep4, got4)
    parts4 = xy_scatter(grid, sends)

    def last_swaps(*pieces):
        kind = pieces[0][0].dtype
        sends = [
            jnp.concatenate([xy_sum(grid, p, z).astype(kind) for p in pieces])
            for z in range(1, grid.nf)
        ]
        return [grid.swap_fsdp(s, z) for z, s in zip(range(1, grid.nf), sends)]

    all2, all3, all4 = held2 + parts2, held3 + parts3, held4 + parts4
    enc_up_grad, enc_down_grad, dec_qkv_grad, dec_out_grad = shards(
        grid, [enc_feed_back, dec_back], [all2, all3], last_swaps(all2, all3)
    )
    cross_q_grad, cross_kv_grad, cross_out_grad, dec_up_grad, dec_down_grad = shards(
        grid, [late_back], [[late_total[None]]], []
    )
    all4 = after(all4, cross_q_grad)
    enc_qkv_grad, enc_out_grad, *rest = shards(grid, [enc_back], [all4], last_swaps(all4))

    return (
        dec_output,
        source_grad,
        target_grad,
        enc_qkv_grad,
        enc_out_grad,
        enc_up_grad,
        enc_down_grad,
        rest[1],
        rest[3].reshape(-1),
        dec_qkv_grad,
        dec_out_grad,
        cross_q_grad,
        cross_kv_grad,
        cross_out_grad,
        dec_up_grad,
        dec_down_grad,
        rest[2],
        rest[4].reshape(-1),
        rest[0],
    )


def solution(mesh):
    split = P(("dp", "fsdp"))
    return jax.shard_map(
        functools.partial(layers, Grid(mesh)),
        mesh=mesh,
        in_specs=(split,) * 22,
        out_specs=(split,) * 19,
        check_vma=False,
    )
```

```python
import functools

import jax
import jax.numpy as jnp
from jax import lax
from jax.experimental import pallas as pl
from jax.experimental.pallas import tpu as pltpu
from jax.sharding import PartitionSpec as P

AXES = ("dp", "fsdp")
LANGS = 8
ROW = 512
CHUNK = 512
scale_dot = 0.125
norm_eps = 1e-05

ENC = 8
DEC = 16
ENC_UP = 29
DEC_UP = 33
SMALL = ((0, 8), (8, 8), (16, 13), (29, 4), (33, 4))
BF = jnp.bfloat16
F32 = jnp.float32


class Grid:
    def __init__(self, mesh):
        self.nd = mesh.shape["dp"]
        self.nf = mesh.shape["fsdp"]
        self.n = self.nd * self.nf
        self.nh = self.nd // 2
        self.hz = self.nh * self.nf
        self.unit = ROW // self.n
        self.tiled = self.unit % 16 == 0
        self.cut = (self.n, self.unit) if self.tiled else (32, 16)

    def me(self):
        return lax.axis_index("dp") * self.nf + lax.axis_index("fsdp")

    def swap_dp(self, value, flip):
        return lax.ppermute(value, "dp", [(i, i ^ flip) for i in range(self.nd)])

    def swap_fsdp(self, value, flip):
        return lax.ppermute(value, "fsdp", [(i, i ^ flip) for i in range(self.nf)])

    def relative(self, part, at):
        return (at // self.nf * 2 + part) * self.nf + at % self.nf

    def spot(self, me, part, at, across):
        if not across:
            return jnp.bitwise_xor(me, self.relative(part, at))
        flip = (at // self.nf * 2 + part) * self.nf
        return jnp.bitwise_xor(me - lax.rem(me, self.nf), flip) + at % self.nf


def after(value, token):
    if token is None:
        return value
    return lax.optimization_barrier((value, token))[0]


def z_copies(grid, shard):
    return lax.all_to_all(
        jnp.broadcast_to(shard[None], (grid.nf,) + shard.shape), "fsdp", 0, 0, tiled=False
    )


def z_gather(grid, shard):
    return [shard] + [grid.swap_fsdp(shard, m) for m in range(1, grid.nf)]


def z_gather_halves(grid, shard):
    order = [0]
    flips = [1 << b for b in range(grid.nf.bit_length() - 1)]
    held = shard[None]
    for flip in reversed(flips):
        held = jnp.concatenate([held, grid.swap_fsdp(held, flip)])
        order = order + [o | flip for o in order]
    return jnp.stack([held[order.index(z)] for z in range(grid.nf)])


def xy_gather(grid, held):
    return [held] + [grid.swap_dp(held, h << 1) for h in range(1, grid.nh)]


def xy_gather_early(grid, held):
    return [held] + [grid.swap_dp(held, h << 1) for h in range(1, grid.nh - 1)]


def xy_gather_rest(grid, held):
    return [grid.swap_dp(held, grid.nh - 1 << 1)]


def core_sum(grid, keep, got):
    shape = (grid.nh, grid.nf) + keep.shape[1:]
    keep, got = keep.reshape(shape), got.reshape(shape)
    kind = keep.dtype
    sends = [(keep[h].astype(F32) + got[h].astype(F32)).astype(kind) for h in range(1, grid.nh)]
    return [keep[0], got[0]], sends


def xy_scatter(grid, sends):
    return [grid.swap_dp(s, h << 1) for h, s in zip(range(1, grid.nh), sends)]


def xy_sum(grid, parts, z):
    out = parts[0][z].astype(F32)
    for part in parts[1:]:
        out = out + part[z].astype(F32)
    return out


class Piece:
    def __init__(self, grid, forms, plain=False, across=False):
        self.grid, self.forms, self.plain, self.across = grid, forms, plain, across
        self.starts = [sum(b for b, _ in forms[:k]) for k in range(len(forms))]
        self.blocks = sum(b for b, _ in forms)
        self.refs = 1 if plain or not grid.tiled else 2

    def cut(self, k):
        blocks, wide = self.forms[k]
        a, b = self.grid.cut
        return (a, blocks, b, 512) if wide is False else (blocks, a, b, 512)

    def arrive(self, *held):
        grid = self.grid
        if grid.tiled:
            shape = (-1, self.blocks, grid.unit, 512)
            self.arrays = [tuple(near_not(h.reshape(shape)) for h in held)] * len(self.forms)
            return
        whole = jnp.concatenate(held)
        if not self.plain:
            spots = [
                grid.spot(grid.me(), part, at, self.across)
                for part in range(2)
                for at in range(grid.hz)
            ]
            index = jnp.zeros((grid.n,), jnp.int32).at[jnp.stack(spots)].set(
                jnp.arange(grid.n, dtype=jnp.int32)
            )
            whole = jnp.take(whole, index, axis=0)
        self.arrays = []
        for k, (blocks, wide) in enumerate(self.forms):
            row = self.starts[k] * grid.unit
            part = whole[:, row : row + blocks * grid.unit]
            if wide is not False:
                part = part.reshape(grid.n, blocks, grid.unit, 512).transpose(1, 0, 2, 3)
            self.arrays.append((part.reshape(self.cut(k)),))

    def pairs(self, k, me, refs, held):
        grid = self.grid
        blocks, wide = self.forms[k]
        start = self.starts[k]
        if not grid.tiled:
            yield refs[0 if len(refs) == 1 else k], held
        elif self.plain and wide is not False:
            for j in range(blocks):
                yield refs[0].at[:, start + j], held.at[j]
        elif self.plain:
            yield refs[0].at[:, pl.ds(start, blocks)], held
        else:
            for part, ref in enumerate(refs):
                for at in range(grid.hz):
                    i = grid.spot(me, part, at, self.across)
                    yield ref.at[at, pl.ds(start, blocks)], held.at[i] if wide is False else held.at[:, i]

    def fetch(self, k, me, refs, dst, sem):
        for there, here in self.pairs(k, me, refs, dst):
            pltpu.make_async_copy(there, here, sem).start()

    def store(self, k, me, src, refs, sem):
        for there, here in self.pairs(k, me, refs, src):
            pltpu.make_async_copy(here, there, sem).start()

    def out_shapes(self):
        grid = self.grid
        if not grid.tiled:
            return [jax.ShapeDtypeStruct(self.cut(k), BF) for k in range(len(self.forms))]
        if self.plain:
            return [jax.ShapeDtypeStruct((grid.n, self.blocks, grid.unit, 512), BF)]
        return [jax.ShapeDtypeStruct((grid.hz, self.blocks, grid.unit, 512), BF)] * 2

    def ready(self, outs):
        grid = self.grid
        rows = self.blocks * grid.unit
        if grid.tiled:
            return [out.reshape(-1, rows, 512) for out in outs]
        parts = []
        for k, (blocks, wide) in enumerate(self.forms):
            part = outs[k]
            if wide is not False:
                part = part.reshape(blocks, grid.n, grid.unit, 512).transpose(1, 0, 2, 3)
            parts.append(part.reshape(grid.n, blocks * grid.unit, 512))
        whole = jnp.concatenate(parts, axis=1)
        return [whole] if self.plain else spread_blocks(grid, whole)


def scatter_plain(grid, whole):
    rows = whole.shape[1]
    part = lax.psum_scatter(
        whole.reshape(grid.nd, grid.nf * rows, 512), "dp", scatter_dimension=0, tiled=False
    )
    return lax.psum_scatter(
        part.reshape(grid.nf, rows, 512), "fsdp", scatter_dimension=0, tiled=False
    )


def spread_blocks(grid, whole):
    sides = []
    for part in range(2):
        table = [grid.relative(part, at) for at in range(grid.hz)]
        sides.append(jnp.take(whole, jnp.array(table, jnp.int32) ^ grid.me(), axis=0))
    return sides


def finish(ref, sem):
    pltpu.make_async_copy(ref, ref, sem).wait()


def to_rows(shard):
    unit = shard.shape[0]
    blocks = shard.shape[1] // 512
    return shard.reshape(unit, blocks, 512).transpose(1, 0, 2).reshape(blocks * unit, 512)


def fours(rows, start, width):
    k = lax.broadcasted_iota(jnp.int32, (4 * rows, width), 0)
    return lax.broadcasted_iota(jnp.int32, (4 * rows, width), 1) == start + lax.rem(k, 4)


def own_row(rows):
    k = lax.broadcasted_iota(jnp.int32, (rows, 4 * rows), 1)
    return lax.broadcasted_iota(jnp.int32, (rows, 4 * rows), 0) == k // 4


def flatten_fours(value, start):
    rows = value.shape[0]
    wide = lax.dot_general(
        value,
        fours(rows, start, 128).astype(F32),
        (((1,), (1,)), ((), ())),
        precision=lax.Precision.HIGHEST,
        preferred_element_type=F32,
    )
    return jnp.sum(jnp.where(own_row(rows), wide, 0.0), axis=0, keepdims=True)


def place_small(parts, rows):
    total = None
    for (start, width), part in zip(SMALL, parts):
        value = part[...]
        if width == 4:
            value = jnp.where(own_row(rows), value.astype(F32), 0.0).astype(BF)
            spots = fours(rows, start, 512)
        else:
            r = lax.broadcasted_iota(jnp.int32, (width, 512), 0)
            spots = lax.broadcasted_iota(jnp.int32, (width, 512), 1) == start + r
        value = jnp.dot(value, jnp.where(spots, 1.0, 0.0).astype(BF), preferred_element_type=F32)
        total = value if total is None else total + value
    return total.astype(BF)


def pack_kernel(counts, unit, *refs):
    refs = list(refs)
    small = [refs.pop(0) for _ in SMALL]
    groups = [[refs.pop(0) for _ in range(count)] for count in counts]
    refs[0][4 * unit : 5 * unit] = place_small(small, unit)
    for group, out in zip(groups, refs):
        at = 0
        for ref in group:
            rows = ref.shape[0]
            for j in range(ref.shape[1] // 512):
                if out is refs[0] and at == 4 * unit:
                    at += unit
                out[at : at + rows] = ref[:, 512 * j : 512 * (j + 1)]
                at += rows


def pack(grid, small, *groups):
    if not grid.tiled:
        flat = [p.reshape(grid.unit, 4) if w == 4 else p for (_, w), p in zip(SMALL, small)]
        flat = jnp.concatenate(flat, axis=1)
        flat = jnp.pad(flat, ((0, 0), (0, 512 - flat.shape[1])))
        first, *rest = groups
        groups = [list(first[:2]) + [flat] + list(first[2:])] + rest
        return [
            jnp.concatenate([to_rows(a) if a.shape[0] == grid.unit else a for a in arrays])
            for arrays in groups
        ]
    rows = [sum(a.size for a in arrays) // 512 for arrays in groups]
    rows[0] += grid.unit
    flat = [p.reshape(1, -1) if w == 4 else p for (_, w), p in zip(SMALL, small)]
    return pl.pallas_call(
        functools.partial(pack_kernel, [len(arrays) for arrays in groups], grid.unit),
        out_shape=[like(r, 512, BF) for r in rows],
        compiler_params=params(56),
        name="pack",
    )(*flat, *[a for arrays in groups for a in arrays])


def shards_kernel(pieces, counts, *refs):
    refs = list(refs)
    own = [[refs.pop(0) for _ in range(count)] for count in counts[:-1]]
    lasts = [refs.pop(0) for _ in range(counts[-1])]
    at = 0
    for piece, parts in zip(pieces, own):
        rows = piece.blocks * piece.grid.unit
        total = None
        for part in parts:
            total = part[0].astype(F32) if total is None else total + part[0].astype(F32)
        for last in lasts:
            total = total + last[at : at + rows].astype(F32)
        at += rows
        row, unit = 0, piece.grid.unit
        for blocks, wide in piece.forms:
            if wide is None:
                value = total[row : row + unit]
                for start, width in SMALL:
                    out = refs.pop(0)
                    if width == 4:
                        out[...] = flatten_fours(value[:, :128], start)
                    else:
                        out[...] = value[:, start : start + width]
                row += unit
                continue
            out = refs.pop(0)
            for j in range(blocks):
                value = total[row : row + unit]
                if wide:
                    out[:, 512 * j : 512 * (j + 1)] = value
                else:
                    out[unit * j : unit * (j + 1)] = value
                row += unit


def shards(grid, pieces, own, lasts):
    if not grid.tiled:
        total = jnp.concatenate(
            [functools.reduce(lambda a, b: a + b, [p[0].astype(F32) for p in parts]) for parts in own]
        )
        for last in lasts:
            total = total + last.astype(F32)
        outs, row = [], 0
        for piece in pieces:
            for blocks, wide in piece.forms:
                part = total[row : row + blocks * grid.unit]
                if wide is None:
                    outs += [part[:, start : start + width] for start, width in SMALL]
                else:
                    outs.append(from_rows(part, blocks) if wide else part)
                row += blocks * grid.unit
        return outs
    first = lambda a: pl.BlockSpec((1,) + a.shape[1:], lambda i: (0, 0, 0))
    args = [a for parts in own for a in parts] + lasts
    specs = [first(a) for parts in own for a in parts] + [whole_spec(a) for a in lasts]
    shapes = []
    for piece in pieces:
        for blocks, wide in piece.forms:
            if wide is None:
                shapes += [
                    like(1, grid.unit * 4, F32) if width == 4 else like(grid.unit, width, F32)
                    for _, width in SMALL
                ]
            elif wide:
                shapes.append(like(grid.unit, 512 * blocks, F32))
            else:
                shapes.append(like(grid.unit * blocks, 512, F32))
    return pl.pallas_call(
        functools.partial(shards_kernel, pieces, [len(p) for p in own] + [len(lasts)]),
        grid=(1,),
        in_specs=specs,
        out_specs=[whole_spec(s) for s in shapes],
        out_shape=shapes,
        compiler_params=params(56),
        name="shards",
    )(*args)


def from_rows(rows, blocks):
    unit = rows.shape[0] // blocks
    return rows.reshape(blocks, unit, 512).transpose(1, 0, 2).reshape(unit, blocks * 512)


HALF = 64
BIG = float(2**30)


def dot(a, b):
    return jnp.dot(a, b, preferred_element_type=jnp.float32)


def dot_t(a, b):
    return lax.dot_general(a, b, (((1,), (1,)), ((), ())), preferred_element_type=jnp.float32)


def t_dot(a, b):
    return lax.dot_general(a, b, (((0,), (0,)), ((), ())), preferred_element_type=jnp.float32)


def lanes(rows=1, width=128):
    return lax.broadcasted_iota(jnp.int32, (rows, width), 1)


def head_lanes(h):
    return jnp.where(lanes() // HALF == h, 1.0, 0.0).astype(jnp.bfloat16)


def one_lanes(h):
    at = lanes() - HALF * h
    return jnp.where((at >= 8) & (at < 11), 1.0, 0.0).astype(jnp.bfloat16)


def minus_parts(value):
    at = lanes() % HALF
    value = -value
    high = value.astype(jnp.bfloat16).astype(jnp.float32)
    rest = value - high
    mid = rest.astype(jnp.bfloat16).astype(jnp.float32)
    low = rest - mid
    out = jnp.where(at == 8, high, jnp.where(at == 9, mid, jnp.where(at == 10, low, 0.0)))
    return out.astype(jnp.bfloat16)


def pair(value, p):
    return value[:, 128 * p : 128 * (p + 1)]


def norm(summed):
    centred = summed - jnp.mean(summed, axis=-1, keepdims=True)
    inverse = lax.rsqrt(jnp.mean(centred * centred, axis=-1, keepdims=True) + norm_eps)
    return centred * inverse, inverse


def heads_forward(q, k, v, hot, bar):
    outs, logs = [], []
    for p in range(q.shape[1] // 128):
        qa = jnp.concatenate([pair(q, p) * jnp.bfloat16(scale_dot), hot], axis=1)
        total, tops = None, []
        for h in (0, 1):
            mask = head_lanes(h)
            ka = jnp.concatenate([pair(k, p) * mask, bar], axis=1)
            scores = dot_t(qa, ka)
            top = jnp.max(scores, axis=-1, keepdims=True)
            power = jnp.exp(scores - top).astype(jnp.bfloat16)
            va = jnp.concatenate(
                [pair(v, p) * mask, jnp.broadcast_to(mask, (v.shape[0], 128))], axis=1
            )
            part = dot(power, va)
            total = part if total is None else total + part
            tops.append(top)
        sums = total[:, 128:]
        outs.append(total[:, :128] / sums)
        logs.append(minus_parts(jnp.where(lanes() < HALF, tops[0], tops[1]) + jnp.log(sums)))
    return jnp.concatenate(outs, axis=1), jnp.concatenate(logs, axis=1)


def heads_backward(go, q, k, v, o, lse, hot, bar):
    gqs, gks, gvs = [], [], []
    at = lax.broadcasted_iota(jnp.int32, (128, 128), 0) // HALF
    to = lax.broadcasted_iota(jnp.int32, (128, 128), 1) // HALF
    same = jnp.where(at == to, 1.0, 0.0).astype(jnp.bfloat16)
    same = jnp.concatenate([same, same], axis=0)
    for p in range(q.shape[1] // 128):
        qs = pair(q, p) * jnp.bfloat16(scale_dot)
        gp = pair(go, p)
        prod = gp.astype(jnp.float32) * pair(o, p)
        high = prod.astype(jnp.bfloat16)
        low = (prod - high.astype(jnp.float32)).astype(jnp.bfloat16)
        delta = dot(jnp.concatenate([high, low], axis=1), same)
        qa = jnp.concatenate([qs, hot + pair(lse, p)], axis=1)
        ga = jnp.concatenate([gp, minus_parts(delta)], axis=1)
        gq = gk = gv = None
        for h in (0, 1):
            mask, one = head_lanes(h), one_lanes(h)
            km = pair(k, p) * mask
            ka = jnp.concatenate([km, bar + one], axis=1)
            va = jnp.concatenate(
                [pair(v, p) * mask, jnp.broadcast_to(one, (v.shape[0], 128))], axis=1
            )
            probs = jnp.exp(dot_t(ka, qa))
            gs = (probs * dot_t(va, ga)).astype(jnp.bfloat16)
            gv_h = dot(probs.astype(jnp.bfloat16), gp * mask)
            gk_h = dot(gs, qs * mask)
            gq_h = t_dot(gs, km)
            gv = gv_h if gv is None else gv + gv_h
            gk = gk_h if gk is None else gk + gk_h
            gq = gq_h if gq is None else gq + gq_h
        gqs.append((gq * scale_dot).astype(jnp.bfloat16))
        gks.append(gk.astype(jnp.bfloat16))
        gvs.append(gv.astype(jnp.bfloat16))
    return tuple(jnp.concatenate(x, axis=1) for x in (gqs, gks, gvs))


def norm_back(grad, normed, inverse, gain):
    scaled = grad * gain
    back = inverse * (
        scaled
        - jnp.mean(scaled, axis=-1, keepdims=True)
        - normed * jnp.mean(scaled * normed, axis=-1, keepdims=True)
    )
    return back, jnp.sum(grad * normed, axis=0), jnp.sum(grad, axis=0)


def square(ref, k):
    return ref[k].reshape(512, 512)


def vec(vectors, k):
    return vectors[k : k + 1, :]


ANY = pl.BlockSpec(memory_space=pl.ANY)
SMEM = pl.BlockSpec(memory_space=pltpu.SMEM)


def whole_spec(array):
    return pl.BlockSpec(array.shape, lambda i: (0,) * array.ndim)


def row_spec(array):
    return pl.BlockSpec((ROW,) + array.shape[1:], lambda i: (i,) + (0,) * (array.ndim - 1))


def near_not(array):
    return pltpu.with_memory_space_constraint(array, pltpu.HBM)


def far(shape):
    return pltpu.HBM(shape.shape, shape.dtype)


def like(rows, width, kind):
    return jax.ShapeDtypeStruct((rows, width), kind)


def params(mebibytes):
    return pltpu.CompilerParams(vmem_limit_bytes=mebibytes * 1024 * 1024)


def cost(tokens, macs):
    return pl.CostEstimate(
        flops=2 * tokens * macs, bytes_accessed=16 * tokens * 512, transcendentals=0
    )


def attend_forward_kernel(mode, base, piece, small, *refs):
    refs = list(refs)
    me_ref = refs.pop(0)
    count = piece.refs
    take = lambda k: [refs.pop(0) for _ in range(k)]
    proj_refs = [take(count) for _ in range(3 if mode == "cross" else 2)]
    small_refs = take(count) if small is not None else None
    vectors_ref = None if small is not None else refs.pop(0)
    if mode == "cross":
        normed_ref, memory_ref = take(2)
    else:
        x_ref = refs.pop(0)
        if mode == "dec":
            lang_ref = refs.pop(0)
    hot_ref, bar_ref = take(2)
    q_out, k_out, v_out, o_out, lse_out, n_out, inv_out = take(7)
    if mode != "enc":
        low_out = refs.pop(0)
    if small is not None:
        vectors_out, small_out = take(2)
    weights = take(3 if mode == "cross" else 2)
    small_scr = refs.pop(0) if small is not None else None
    sems = refs.pop(0)
    out_w = weights[-1]

    @pl.when(pl.program_id(0) == 0)
    def _():
        me = me_ref[0]
        if small is not None:
            piece.fetch(small, me, small_refs, small_scr, sems.at[3])
        for k, (source, dst) in enumerate(zip(proj_refs, weights)):
            piece.fetch(k, me, source, dst, sems.at[k])
        if small is not None:
            finish(small_scr, sems.at[3])
            block = small_scr[0].reshape(512, 512)[:, :128]
            small_out[...] = block
            vectors_out[...] = block.astype(F32).T
        for k, dst in enumerate(weights[:-1]):
            finish(dst, sems.at[k])

    vectors = (vectors_out if small is not None else vectors_ref)[...]
    if mode == "enc":
        low = x_ref[...]
        residual = low.astype(F32)
        memory = low
    elif mode == "dec":
        residual = x_ref[...].astype(F32) + dot(lang_ref[...], vectors.astype(BF))
        low = memory = residual.astype(BF)
    else:
        residual = normed_ref[...] * vec(vectors, DEC + 3) + vec(vectors, DEC + 4)
        low = residual.astype(BF)
        memory = memory_ref[...]
    if mode != "enc":
        low_out[...] = low
    if mode == "cross":
        wq, wk, wv = square(weights[0], 0), square(weights[1], 0), square(weights[1], 1)
    else:
        wq, wk, wv = (square(weights[0], j) for j in range(3))
    q = (dot(low, wq) + vec(vectors, base)).astype(BF)
    k = dot(memory, wk).astype(BF)
    v = (dot(memory, wv) + vec(vectors, base + 1)).astype(BF)
    q_out[...], k_out[...], v_out[...] = q, k, v
    o, lse = heads_forward(q, k, v, hot_ref[...], bar_ref[...])
    o_out[...], lse_out[...] = o, lse

    @pl.when(pl.program_id(0) == 0)
    def _():
        finish(out_w, sems.at[len(weights) - 1])

    branch = dot(o.astype(BF), square(out_w, 0)) + vec(vectors, base + 2)
    n_out[...], inv_out[...] = norm(residual + branch)


def attend_forward(mode, base, me, piece, small, inputs, hot, bar, vectors):
    grid = piece.grid
    tokens = hot.shape[0]
    names = range(3 if mode == "cross" else 2)
    weights = [a for k in names for a in piece.arrays[k]]
    args = [me] + weights
    specs = [SMEM] + [ANY] * len(weights)
    if small is not None:
        args += list(piece.arrays[small])
        specs += [ANY] * len(piece.arrays[small])
    else:
        args.append(vectors)
        specs.append(whole_spec(vectors))
    rows = [near_not(inputs[0])] + list(inputs[1:]) + [hot, bar]
    args += rows
    specs += [row_spec(a) for a in rows]
    outs = [like(tokens, 512, BF)] * 3 + [like(tokens, 512, F32), like(tokens, 512, BF)]
    outs += [like(tokens, 512, F32), like(tokens, 1, F32)]
    if mode != "enc":
        outs.append(like(tokens, 512, BF))
    out_specs = [row_spec(o) for o in outs]
    outs = [o if i == 5 and mode == "cross" else far(o) for i, o in enumerate(outs)]
    scratch = [pltpu.VMEM(piece.cut(k), BF) for k in names]
    if small is not None:
        extra = [like(128, 512, F32), like(512, 128, BF)]
        outs += extra
        out_specs += [whole_spec(e) for e in extra]
        scratch.append(pltpu.VMEM(piece.cut(small), BF))
    scratch.append(pltpu.SemaphoreType.DMA((4,)))
    return pl.pallas_call(
        functools.partial(attend_forward_kernel, mode, base, piece, small),
        grid=(tokens // ROW,),
        in_specs=specs,
        out_specs=out_specs,
        out_shape=outs,
        scratch_shapes=scratch,
        compiler_params=params(24),
        cost_estimate=cost(tokens, 4 * 512 * 512 + 2 * 8 * 512 * 256),
        name="attend_forward_" + mode,
    )(*args)


def feed_forward_kernel(base, first, piece, own, *refs):
    refs = list(refs)
    me_ref = refs.pop(0)
    count = piece.refs
    take = lambda k: [refs.pop(0) for _ in range(k)]
    up_refs, down_refs = take(count), take(count)
    vectors_ref, bias_ref, n_ref = take(3)
    act_out, slope_out, n_out, inv_out, low_out = take(5)
    up, down, sems = take(3)

    @pl.when(pl.program_id(0) == 0)
    def _():
        me = me_ref[0]
        piece.fetch(own, me, up_refs, up, sems.at[0])
        piece.fetch(own + 1, me, down_refs, down, sems.at[1])
        finish(up, sems.at[0])
        finish(down, sems.at[1])

    vectors = vectors_ref[...]
    x = n_ref[...] * vec(vectors, first) + vec(vectors, first + 1)
    low = x.astype(BF)
    branch = None
    for j in range(4):
        h = dot(low, square(up, j)) + bias_ref[j : j + 1, :]
        act, slope = gate(h)
        act = act.astype(BF)
        act_out[j], slope_out[j] = act, slope.astype(BF)
        part = dot(act, tall(down, j))
        branch = part if branch is None else branch + part
    n, inv = norm(x + branch + vec(vectors, base))
    n_out[...], inv_out[...] = n, inv
    low_out[...] = (n * vec(vectors, base + 1) + vec(vectors, base + 2)).astype(BF)


def gate(h):
    c = 0.7978845608028654
    square_h = h * h
    t = jnp.tanh(h * (c + (c * 0.044715) * square_h))
    half = 0.5 + 0.5 * t
    slope = half + (0.5 * h) * (1.0 - t * t) * (c + (3.0 * c * 0.044715) * square_h)
    return h * half, slope


def tall(ref, j):
    size = ref.shape[0] // 4
    return ref[size * j : size * (j + 1)].reshape(512, 512)


def feed_forward(base, first, me, piece, own, vectors, bias, n):
    tokens = n.shape[0]
    weights = list(piece.arrays[own]) + list(piece.arrays[own + 1])
    chunk = jax.ShapeDtypeStruct((4, tokens, 512), BF)
    chunk_spec = pl.BlockSpec((4, ROW, 512), lambda i: (0, i, 0))
    outs = [chunk, chunk, like(tokens, 512, F32), like(tokens, 1, F32), like(tokens, 512, BF)]
    out_specs = [chunk_spec, chunk_spec] + [row_spec(o) for o in outs[2:]]
    outs = [far(o) for o in outs[:4]] + outs[4:]
    return pl.pallas_call(
        functools.partial(feed_forward_kernel, base, first, piece, own),
        grid=(tokens // ROW,),
        in_specs=[SMEM]
        + [ANY] * len(weights)
        + [whole_spec(vectors), whole_spec(bias), row_spec(n)],
        out_specs=out_specs,
        out_shape=outs,
        scratch_shapes=[
            pltpu.VMEM(piece.cut(own), BF),
            pltpu.VMEM(piece.cut(own + 1), BF),
            pltpu.SemaphoreType.DMA((2,)),
        ],
        compiler_params=params(26),
        cost_estimate=cost(tokens, 8 * 512 * 512),
        name="feed_forward",
    )(me, *weights, vectors, bias, near_not(n))


def feed_backward_kernel(base, first, piece, own, grads, at, *refs):
    refs = list(refs)
    me_ref = refs.pop(0)
    count = piece.refs
    take = lambda k: [refs.pop(0) for _ in range(k)]
    up_refs, down_refs = take(count), take(count)
    vectors_ref, grad_ref, n2_ref, inv2_ref, n1_ref, act_ref, slope_ref = take(7)
    grad_outs = take(len(grads.out_shapes()))
    dx_out, sums_out, bias_out = take(3)
    up, down, d_up, d_down, low_t, branch, sems = take(7)
    j = pl.program_id(0)
    vectors = vectors_ref[...]

    @pl.when(j == 0)
    def _():
        me = me_ref[0]
        piece.fetch(own, me, up_refs, up, sems.at[0])
        piece.fetch(own + 1, me, down_refs, down, sems.at[1])
        sums_out[...] = jnp.zeros_like(sums_out)
        for t in range(grad_ref.shape[0] // ROW):
            part = pl.ds(ROW * t, ROW)
            back, gain, shift = norm_back(
                grad_ref[part].astype(F32), n2_ref[part], inv2_ref[part], vec(vectors, base + 1)
            )
            dx_out[part] = back
            low = back.astype(BF)
            branch[part] = low
            sums_out[0:1] += jnp.sum(low.astype(F32), axis=0, keepdims=True)
            sums_out[1:2] += gain[None]
            sums_out[2:3] += shift[None]
            x = n1_ref[part] * vec(vectors, first) + vec(vectors, first + 1)
            low_t[:, part] = x.astype(BF).T
        finish(up, sems.at[0])
        finish(down, sems.at[1])

    size = down.shape[0] // 4
    down_j = down[pl.ds(size * j, size)].reshape(512, 512)
    up_j = up[j].reshape(512, 512)
    low = branch[...]
    hidden = (dot_t(low, down_j) * slope_ref[0].astype(F32)).astype(BF)
    bias_out[0] = jnp.broadcast_to(
        jnp.sum(hidden.astype(F32), axis=0, keepdims=True), bias_out.shape[1:]
    )
    dx_out[...] += dot_t(hidden, up_j)
    d_up[j] = dot(low_t[...], hidden).astype(BF).reshape(d_up.shape[1:])
    d_down[pl.ds(size * j, size)] = (
        t_dot(act_ref[0], low).astype(BF).reshape((size,) + d_down.shape[1:])
    )

    @pl.when(j == pl.num_programs(0) - 1)
    def _():
        me = me_ref[0]
        grads.store(at, me, d_up, grad_outs, sems.at[0])
        grads.store(at + 1, me, d_down, grad_outs, sems.at[1])
        finish(d_up, sems.at[0])
        finish(d_down, sems.at[1])


def feed_backward(base, first, me, piece, own, grads, at, vectors, grad, n2, inv2, n1, act, slope):
    tokens = n1.shape[0]
    weights = list(piece.arrays[own]) + list(piece.arrays[own + 1])
    act, slope, n2, inv2, n1 = (near_not(a) for a in (act, slope, n2, inv2, n1))
    held = [vectors, grad, n2, inv2, n1]
    chunk_spec = pl.BlockSpec((1, tokens, 512), lambda i: (i, 0, 0))
    outs = [like(tokens, 512, F32), like(8, 512, F32), jax.ShapeDtypeStruct((4, 8, 512), F32)]
    got = pl.pallas_call(
        functools.partial(feed_backward_kernel, base, first, piece, own, grads, at),
        grid=(4,),
        in_specs=[SMEM]
        + [ANY] * len(weights)
        + [whole_spec(a) for a in held]
        + [chunk_spec, chunk_spec],
        out_specs=[ANY] * len(grads.out_shapes())
        + [whole_spec(outs[0]), whole_spec(outs[1]), pl.BlockSpec((1, 8, 512), lambda i: (i, 0, 0))],
        out_shape=[far(s) for s in grads.out_shapes()] + [far(outs[0])] + outs[1:],
        scratch_shapes=[
            pltpu.VMEM(piece.cut(own), BF),
            pltpu.VMEM(piece.cut(own + 1), BF),
            pltpu.VMEM(grads.cut(at), BF),
            pltpu.VMEM(grads.cut(at + 1), BF),
            pltpu.VMEM((512, tokens), BF),
            pltpu.VMEM((tokens, 512), BF),
            pltpu.SemaphoreType.DMA((2,)),
        ],
        compiler_params=params(32),
        cost_estimate=cost(tokens, 16 * 512 * 512),
        name="feed_backward",
    )(me, *weights, *held, act, slope)
    m = len(grads.out_shapes())
    return got[:m], got[m], got[m + 1], got[m + 2][:, 0, :]


def feed_both_kernel(base, first, piece, own, grads, at, tiles, *refs):
    refs = list(refs)
    me_ref = refs.pop(0)
    take = lambda k: [refs.pop(0) for _ in range(k)]
    up_refs, down_refs = take(piece.refs), take(piece.refs)
    vectors_ref, bias_ref, n1_ref, grad_ref = take(4)
    grad_outs = take(len(grads.out_shapes()))
    low_out, dx_out, sums_out, bias_out = take(4)
    up, down, d_up, d_down, acts, slopes, low_t, branches, sems = take(9)
    step = pl.program_id(0)
    vectors = vectors_ref[...]

    @pl.when(step == 0)
    def _():
        me = me_ref[0]
        piece.fetch(own, me, up_refs, up, sems.at[0])
        piece.fetch(own + 1, me, down_refs, down, sems.at[1])
        sums_out[...] = jnp.zeros_like(sums_out)
        finish(up, sems.at[0])
        finish(down, sems.at[1])

    @pl.when(step < tiles)
    def _():
        x = n1_ref[...] * vec(vectors, first) + vec(vectors, first + 1)
        low = x.astype(BF)
        rows = pl.ds(pl.multiple_of(step * ROW, ROW), ROW)
        branch = None
        for j in range(4):
            h = dot(low, square(up, j)) + bias_ref[j : j + 1, :]
            act, slope = gate(h)
            act = act.astype(BF)
            acts[j, rows], slopes[j, rows] = act, slope.astype(BF)
            part = dot(act, tall(down, j))
            branch = part if branch is None else branch + part
        n, inv = norm(x + branch + vec(vectors, base))
        gain = vec(vectors, base + 1)
        low_out[...] = (n * gain + vec(vectors, base + 2)).astype(BF)
        back, d_gain, d_shift = norm_back(grad_ref[...].astype(F32), n, inv, gain)
        dx_out[rows] = back
        back = back.astype(BF)
        branches[rows] = back
        sums_out[0:1] += jnp.sum(back.astype(F32), axis=0, keepdims=True)
        sums_out[1:2] += d_gain[None]
        sums_out[2:3] += d_shift[None]
        low_t[:, rows] = low.T

    @pl.when(step >= tiles)
    def _():
        j = step - tiles
        size = down.shape[0] // 4
        low = branches[...]
        hidden = dot_t(low, down[pl.ds(size * j, size)].reshape(512, 512))
        hidden = (hidden * slopes[j].astype(F32)).astype(BF)
        bias_out[0] = jnp.broadcast_to(
            jnp.sum(hidden.astype(F32), axis=0, keepdims=True), bias_out.shape[1:]
        )
        dx_out[...] += dot_t(hidden, up[j].reshape(512, 512))
        d_up[j] = dot(low_t[...], hidden).astype(BF).reshape(d_up.shape[1:])
        d_down[pl.ds(size * j, size)] = (
            t_dot(acts[j], low).astype(BF).reshape((size,) + d_down.shape[1:])
        )

    @pl.when(step == pl.num_programs(0) - 1)
    def _():
        me = me_ref[0]
        grads.store(at, me, d_up, grad_outs, sems.at[0])
        grads.store(at + 1, me, d_down, grad_outs, sems.at[1])
        finish(d_up, sems.at[0])
        finish(d_down, sems.at[1])


def feed_both(base, first, me, piece, own, grads, at, vectors, bias, n1, grad):
    tokens = n1.shape[0]
    tiles = tokens // ROW
    weights = list(piece.arrays[own]) + list(piece.arrays[own + 1])
    tile_spec = pl.BlockSpec((ROW, 512), lambda i: (jnp.minimum(i, tiles - 1), 0))
    outs = [
        like(tokens, 512, BF),
        like(tokens, 512, F32),
        like(8, 512, F32),
        jax.ShapeDtypeStruct((4, 8, 512), F32),
    ]
    got = pl.pallas_call(
        functools.partial(feed_both_kernel, base, first, piece, own, grads, at, tiles),
        grid=(tiles + 4,),
        in_specs=[SMEM]
        + [ANY] * len(weights)
        + [whole_spec(vectors), whole_spec(bias), tile_spec, tile_spec],
        out_specs=[ANY] * len(grads.out_shapes())
        + [
            tile_spec,
            whole_spec(outs[1]),
            whole_spec(outs[2]),
            pl.BlockSpec((1, 8, 512), lambda i: (jnp.maximum(i - tiles, 0), 0, 0)),
        ],
        out_shape=[far(s) for s in grads.out_shapes()] + outs,
        scratch_shapes=[
            pltpu.VMEM(piece.cut(own), BF),
            pltpu.VMEM(piece.cut(own + 1), BF),
            pltpu.VMEM(grads.cut(at), BF),
            pltpu.VMEM(grads.cut(at + 1), BF),
            pltpu.VMEM((4, tokens, 512), BF),
            pltpu.VMEM((4, tokens, 512), BF),
            pltpu.VMEM((512, tokens), BF),
            pltpu.VMEM((tokens, 512), BF),
            pltpu.SemaphoreType.DMA((2,)),
        ],
        compiler_params=params(44),
        cost_estimate=cost(tokens, 24 * 512 * 512),
        name="feed_both",
    )(me, *weights, vectors, bias, n1, grad)
    m = len(grads.out_shapes())
    return got[:m], got[m], got[m + 1], got[m + 2], got[m + 3][:, 0, :]


def attend_backward_kernel(mode, base, piece, grads, first, shared, *refs):
    refs = list(refs)
    me_ref = refs.pop(0)
    count = piece.refs
    take = lambda k: [refs.pop(0) for _ in range(k)]
    kinds = 3 if mode == "cross" else 2
    weight_refs = [take(count) for _ in range(kinds)]
    vectors_ref, grad_ref, n_ref, inv_ref, q_ref, k_ref, v_ref, o_ref, lse_ref = take(9)
    hot_ref, bar_ref, low_ref = take(3)
    memory_ref = refs.pop(0) if mode == "cross" else None
    lang_ref = refs.pop(0) if mode == "dec" else None
    sum_refs = take(5) if mode == "enc" else None
    cols_ref = refs.pop(0) if mode == "enc" else None
    if shared:
        refs.pop(0)
    grad_outs = take(len(grads.out_shapes()))
    dx_out, sums_out = take(2)
    dm_out = refs.pop(0) if mode == "cross" else None
    lang_out = refs.pop(0) if mode == "dec" else None
    staged_kinds = 2 if mode == "dec" else 3
    weights, staged = take(kinds), take(staged_kinds)
    low_t, o_t, gqs, gks, gvs, gbs, sems = take(7)
    memory_t = refs.pop(0) if mode == "cross" else None
    all_sums = refs.pop(0) if mode == "enc" else None
    step = pl.program_id(0)
    vectors = vectors_ref[...]

    @pl.when(step == 0)
    def _():
        me = me_ref[0]
        for k, (source, dst) in enumerate(zip(weight_refs, weights)):
            piece.fetch(k, me, source, dst, sems.at[k])
        sums_out[...] = jnp.zeros_like(sums_out)
        if mode == "dec":
            lang_out[...] = jnp.zeros_like(lang_out)

    back, gain, shift = norm_back(
        grad_ref[...], n_ref[...], inv_ref[...], vec(vectors, base + 3)
    )
    gb = back.astype(BF)

    @pl.when(step == 0)
    def _():
        for k, dst in enumerate(weights):
            finish(dst, sems.at[k])

    go = dot_t(gb, square(weights[-1], 0)).astype(BF)
    q, k, v, o = q_ref[...], k_ref[...], v_ref[...], o_ref[...]
    gq, gk, gv = heads_backward(go, q, k, v, o, lse_ref[...], hot_ref[...], bar_ref[...])
    if mode == "cross":
        wq, wk, wv = square(weights[0], 0), square(weights[1], 0), square(weights[1], 1)
    else:
        wq, wk, wv = (square(weights[0], j) for j in range(3))
    dx = back + dot_t(gq, wq)
    dm = dot_t(gk, wk) + dot_t(gv, wv)
    if mode == "cross":
        dx_out[...] = dx
        dm_out[...] = dm
    else:
        dx = dx + dm
        dx_out[...] = dx.astype(BF)
    if mode == "dec":
        high = dx.astype(BF)
        rest = (dx - high.astype(F32)).astype(BF)
        hot_lang = lang_ref[...].T
        lang_out[...] += dot(hot_lang, high) + dot(hot_lang, rest)
    sums_out[0:1] += jnp.sum(gq.astype(F32), axis=0, keepdims=True)
    sums_out[1:2] += jnp.sum(gv.astype(F32), axis=0, keepdims=True)
    sums_out[2:3] += jnp.sum(gb.astype(F32), axis=0, keepdims=True)
    sums_out[3:4] += gain[None]
    sums_out[4:5] += shift[None]
    part = pl.ds(pl.multiple_of(step * ROW, ROW), ROW)
    gqs[part], gks[part], gvs[part], gbs[part] = gq, gk, gv, gb
    low_t[:, part] = low_ref[...].T
    o_t[:, part] = o.astype(BF).T
    if mode == "cross":
        memory_t[:, part] = memory_ref[...].T

    @pl.when(step == pl.num_programs(0) - 1)
    def _():
        me = me_ref[0]
        shape = staged[0].shape[1:]
        out_grad = dot(o_t[...], gbs[...]).astype(BF).reshape(shape)
        gq_grad = dot(low_t[...], gqs[...]).astype(BF).reshape(shape)
        kv_t = (memory_t if mode == "cross" else low_t)[...]
        gk_grad = dot(kv_t, gks[...]).astype(BF).reshape(shape)
        gv_grad = dot(kv_t, gvs[...]).astype(BF).reshape(shape)
        if mode == "cross":
            staged[0][0] = gq_grad
            staged[1][0], staged[1][1] = gk_grad, gv_grad
        else:
            staged[0][0], staged[0][1], staged[0][2] = gq_grad, gk_grad, gv_grad
        staged[kinds - 1][0] = out_grad
        if mode == "enc":
            all_sums[...] = jnp.zeros_like(all_sums)
            row = 0
            counts = (8, 5, 3, 5, 5, 3)
            for ref, count in zip([sum_refs[0], sums_out] + sum_refs[1:], counts):
                all_sums[row : row + count] = ref[:count]
                row += count
            block = (all_sums[...].T + cols_ref[...]).astype(BF)
            block = jnp.concatenate([block, jnp.zeros((512, 384), BF)], axis=1)
            staged[2][0] = block.reshape(shape)
        for k, src in enumerate(staged):
            grads.store(first + k, me, src, grad_outs, sems.at[k])
        for k, src in enumerate(staged):
            finish(src, sems.at[k])


def attend_backward(
    mode, base, me, piece, grads, first, vectors, grad, saved, hot, bar, low, extra, fixed=(), into=None
):
    q, k, v, o, lse, n, inv = (near_not(a) for a in saved)
    low = near_not(low)
    extra = [near_not(a) for a in extra]
    grad = grad if mode == "cross" else near_not(grad)
    tokens = hot.shape[0]
    kinds = range(3 if mode == "cross" else 2)
    weights = [a for i in kinds for a in piece.arrays[i]]
    rows = [grad, n, inv, q, k, v, o, lse, hot, bar, low] + list(extra)
    outs = [like(tokens, 512, F32 if mode == "cross" else BF), like(8, 512, F32)]
    out_specs = [row_spec(outs[0]), whole_spec(outs[1])]
    if mode == "cross":
        outs.append(like(tokens, 512, F32))
        out_specs.append(row_spec(outs[-1]))
    if mode == "dec":
        outs.append(like(128, 512, F32))
        out_specs.append(whole_spec(outs[-1]))
    grad_shapes = grads.out_shapes()
    scratch = [pltpu.VMEM(piece.cut(i), BF) for i in kinds]
    scratch += [pltpu.VMEM(grads.cut(first + i), BF) for i in range(2 if mode == "dec" else 3)]
    scratch += [pltpu.VMEM((512, tokens), BF)] * 2 + [pltpu.VMEM((tokens, 512), BF)] * 4
    scratch.append(pltpu.SemaphoreType.DMA((3,)))
    if mode == "cross":
        scratch.append(pltpu.VMEM((512, tokens), BF))
    if mode == "enc":
        scratch.append(pltpu.VMEM((128, 512), F32))
    args = [me, *weights, vectors, *rows, *fixed]
    shared = [] if into is None else [into]
    got = pl.pallas_call(
        functools.partial(attend_backward_kernel, mode, base, piece, grads, first, bool(shared)),
        grid=(tokens // ROW,),
        in_specs=[SMEM]
        + [ANY] * len(weights)
        + [whole_spec(vectors)]
        + [row_spec(a) for a in rows]
        + [whole_spec(a) for a in fixed]
        + [ANY] * len(shared),
        input_output_aliases={len(args): 0} if shared else {},
        out_specs=[ANY] * len(grad_shapes) + out_specs,
        out_shape=[far(s) for s in grad_shapes] + [far(outs[0])] + outs[1:],
        scratch_shapes=scratch,
        compiler_params=params(42),
        cost_estimate=cost(tokens, 8 * 512 * 512 + 5 * 8 * 512 * 256),
        name="attend_backward_" + mode,
    )(*args, *shared)
    m = len(grad_shapes)
    return got[:m], got[m:]


def segment_marks(segments):
    flat = segments.reshape(-1)
    hot = flat[:, None] == jnp.arange(128, dtype=jnp.int32)[None, :]
    bar = jnp.where(~hot & (jnp.arange(128) < 8)[None, :], -BIG, 0.0)
    return hot.astype(BF), bar.astype(BF)


def language_marks(segments, language):
    picked = jnp.zeros_like(segments)
    for s in range(language.shape[1]):
        picked = jnp.where(segments == s, language[:, s : s + 1], picked)
    flat = picked.reshape(-1)
    return (flat[:, None] == jnp.arange(128, dtype=jnp.int32)[None, :]).astype(BF)


def layers(
    grid,
    source,
    target,
    source_segments,
    target_segments,
    target_language,
    cotangent,
    enc_qkv,
    enc_out,
    enc_up,
    enc_down,
    enc_vecs,
    enc_bias_up,
    dec_qkv,
    dec_out,
    cross_q,
    cross_kv,
    cross_out,
    dec_up,
    dec_down,
    dec_vecs,
    dec_bias_up,
    lang_table,
):
    unit = enc_qkv.shape[0]
    feed_forms = [(4, True), (4, False)]
    self_forms = [(3, True), (1, True)]
    cross_forms = [(1, True), (2, True), (1, True)]
    enc_self = Piece(grid, self_forms + [(1, True)])
    dec_self = Piece(grid, self_forms)
    enc_feed = Piece(grid, feed_forms)
    late = Piece(grid, cross_forms + feed_forms, plain=True)
    rows01, rows2, rows3 = pack(
        grid,
        [lang_table, enc_vecs, dec_vecs, enc_bias_up, dec_bias_up],
        [enc_qkv, enc_out, dec_qkv, dec_out],
        [enc_up, enc_down],
        [cross_q, cross_kv, cross_out, dec_up, dec_down],
    )
    held = jnp.stack(z_gather(grid, rows01))
    held0, held1 = held[:, : 5 * unit], held[:, 5 * unit :]
    held2 = z_gather_halves(grid, after(rows2, held1))
    late.arrive(lax.all_gather(rows3, AXES, axis=0, tiled=False))
    held0 = jnp.concatenate(xy_gather(grid, held0), axis=0)
    held0, held2 = after((held0, held2), held1)
    enc_self.arrive(held0, grid.swap_dp(held0, 1))
    held1, held2 = after((held1, held2), held0[0])
    parts1 = xy_gather(grid, held1)
    parts2 = xy_gather_early(grid, held2)

    me = grid.me().astype(jnp.int32).reshape(1)
    source_hot, source_bar = segment_marks(source_segments)
    target_hot, target_bar = segment_marks(target_segments)
    lang = language_marks(target_segments, target_language)

    *enc_saved, vectors, columns = attend_forward(
        "enc", ENC, me, enc_self, 2, (source,), source_hot, source_bar, None
    )
    token = enc_saved[6]
    held1 = jnp.concatenate(after(parts1, token), axis=0)
    dec_self.arrive(held1, grid.swap_dp(held1, 1))
    parts2 = parts2 + xy_gather_rest(grid, after(held2, token))
    enc_bias = columns[:, ENC_UP:DEC_UP].astype(F32).reshape(4, 512)
    dec_bias = columns[:, DEC_UP : DEC_UP + 4].astype(F32).reshape(4, 512)
    *dec_saved, target_low = attend_forward(
        "dec", DEC, me, dec_self, None, (target, lang), target_hot, target_bar, vectors
    )
    held2 = jnp.concatenate(after(parts2, dec_saved[6]), axis=0)
    enc_feed.arrive(held2, grid.swap_dp(held2, 1))
    enc_act, enc_slope, enc_n, enc_inv, encoded = feed_forward(
        ENC + 5, ENC + 3, me, enc_feed, 0, vectors, enc_bias, enc_saved[5]
    )
    *cross_saved, first_low = attend_forward(
        "cross", DEC + 5, me, late, None, (dec_saved[5], encoded), target_hot, source_bar, vectors
    )
    late_back = Piece(grid, cross_forms + feed_forms, plain=True)
    enc_feed_back = Piece(grid, feed_forms)
    dec_back = Piece(grid, self_forms)
    enc_back = Piece(grid, self_forms + [(1, None)])
    outs, dec_output, grad_second, dec_feed_sums, dec_bias_grad = feed_both(
        DEC + 10, DEC + 8, me, late, 3, late_back, 3, vectors, dec_bias, cross_saved[5], cotangent
    )
    shared = outs[0] if grid.tiled else None
    late_outs, (grad_first, cross_sums, grad_encoded) = attend_backward(
        "cross", DEC + 5, me, late, late_back, 0, vectors, grad_second, cross_saved,
        target_hot, source_bar, first_low, (encoded,), into=shared,
    )
    if not grid.tiled:
        late_outs = list(late_outs[:3]) + list(outs[3:])
    late_total = scatter_plain(grid, *late_back.ready(late_outs))

    outs, grad_enc_first, enc_feed_sums, enc_bias_grad = feed_backward(
        ENC + 5, ENC + 3, me, enc_feed, 0, enc_feed_back, 0, vectors, grad_encoded, enc_n, enc_inv,
        enc_saved[5], enc_act, enc_slope,
    )
    keep2, send2 = enc_feed_back.ready(outs)
    got2 = grid.swap_dp(send2, 1)
    grad_first = after(grad_first, enc_feed_sums)
    outs, (target_grad, dec_sums, lang_grad) = attend_backward(
        "dec", DEC, me, dec_self, dec_back, 0, vectors, grad_first, dec_saved,
        target_hot, target_bar, target_low, (lang,),
    )
    keep3, send3 = dec_back.ready(outs)
    got3 = grid.swap_dp(send3, 1)
    got2 = after(got2, dec_sums)
    held2, sends = core_sum(grid, keep2, got2)
    parts2 = xy_scatter(grid, sends)
    cols = jnp.concatenate([enc_bias_grad.reshape(512, 4), dec_bias_grad.reshape(512, 4)], axis=1)
    cols = jnp.pad(cols, ((0, 0), (ENC_UP, 128 - ENC_UP - 8)))
    grad_enc_first = after(grad_enc_first, got2)
    outs, (source_grad, enc_sums) = attend_backward(
        "enc", ENC, me, enc_self, enc_back, 0, vectors, grad_enc_first, enc_saved,
        source_hot, source_bar, source, (), fixed=(lang_grad, enc_feed_sums, dec_sums, cross_sums, dec_feed_sums, cols),
    )
    keep4, send4 = enc_back.ready(outs)
    got3, parts2 = after((got3, parts2), enc_sums)
    got4 = grid.swap_dp(after(send4, (parts2, got3)), 1)
    held3, sends = core_sum(grid, keep3, got3)
    parts3 = xy_scatter(grid, sends)
    held4, sends = core_sum(grid, keep4, got4)
    parts3 = after(parts3, sends)
    parts4 = xy_scatter(grid, sends)

    def last_swaps(*pieces):
        kind = pieces[0][0].dtype
        sends = [
            jnp.concatenate([xy_sum(grid, p, z).astype(kind) for p in pieces])
            for z in range(1, grid.nf)
        ]
        return [grid.swap_fsdp(s, z) for z, s in zip(range(1, grid.nf), sends)]

    all2, all3, all4 = held2 + parts2, held3 + parts3, held4 + parts4
    enc_up_grad, enc_down_grad, dec_qkv_grad, dec_out_grad = shards(
        grid, [enc_feed_back, dec_back], [all2, all3], last_swaps(all2, all3)
    )
    cross_q_grad, cross_kv_grad, cross_out_grad, dec_up_grad, dec_down_grad = shards(
        grid, [late_back], [[late_total[None]]], []
    )
    all4 = after(all4, cross_q_grad)
    enc_qkv_grad, enc_out_grad, *rest = shards(grid, [enc_back], [all4], last_swaps(all4))

    return (
        dec_output,
        source_grad,
        target_grad,
        enc_qkv_grad,
        enc_out_grad,
        enc_up_grad,
        enc_down_grad,
        rest[1],
        rest[3].reshape(-1),
        dec_qkv_grad,
        dec_out_grad,
        cross_q_grad,
        cross_kv_grad,
        cross_out_grad,
        dec_up_grad,
        dec_down_grad,
        rest[2],
        rest[4].reshape(-1),
        rest[0],
    )


def solution(mesh):
    split = P(("dp", "fsdp"))
    return jax.shard_map(
        functools.partial(layers, Grid(mesh)),
        mesh=mesh,
        in_specs=(split,) * 22,
        out_specs=(split,) * 19,
        check_vma=False,
    )
```

```python
import functools

import jax
import jax.numpy as jnp
from jax import lax
from jax.experimental import pallas as pl
from jax.experimental.pallas import tpu as pltpu
from jax.sharding import PartitionSpec as P

AXES = ("dp", "fsdp")
LANGS = 8
ROW = 512
CHUNK = 512
scale_dot = 0.125
norm_eps = 1e-05

ENC = 8
DEC = 16
ENC_UP = 29
DEC_UP = 33
SMALL = ((0, 8), (8, 8), (16, 13), (29, 4), (33, 4))
BF = jnp.bfloat16
F32 = jnp.float32


class Grid:
    def __init__(self, mesh):
        self.nd = mesh.shape["dp"]
        self.nf = mesh.shape["fsdp"]
        self.n = self.nd * self.nf
        self.nh = self.nd // 2
        self.hz = self.nh * self.nf
        self.unit = ROW // self.n
        self.tiled = self.unit % 16 == 0
        self.cut = (self.n, self.unit) if self.tiled else (32, 16)

    def me(self):
        return lax.axis_index("dp") * self.nf + lax.axis_index("fsdp")

    def swap_dp(self, value, flip):
        return lax.ppermute(value, "dp", [(i, i ^ flip) for i in range(self.nd)])

    def swap_fsdp(self, value, flip):
        return lax.ppermute(value, "fsdp", [(i, i ^ flip) for i in range(self.nf)])

    def relative(self, part, at):
        return (at // self.nf * 2 + part) * self.nf + at % self.nf

    def spot(self, me, part, at, across):
        if not across:
            return jnp.bitwise_xor(me, self.relative(part, at))
        flip = (at // self.nf * 2 + part) * self.nf
        return jnp.bitwise_xor(me - lax.rem(me, self.nf), flip) + at % self.nf


def after(value, token):
    if token is None:
        return value
    return lax.optimization_barrier((value, token))[0]


def z_copies(grid, shard):
    return lax.all_to_all(
        jnp.broadcast_to(shard[None], (grid.nf,) + shard.shape), "fsdp", 0, 0, tiled=False
    )


def z_gather(grid, shard):
    return [shard] + [grid.swap_fsdp(shard, m) for m in range(1, grid.nf)]


def z_gather_halves(grid, shard):
    order = [0]
    flips = [1 << b for b in range(grid.nf.bit_length() - 1)]
    held = shard[None]
    for flip in reversed(flips):
        held = jnp.concatenate([held, grid.swap_fsdp(held, flip)])
        order = order + [o | flip for o in order]
    return jnp.stack([held[order.index(z)] for z in range(grid.nf)])


def xy_gather(grid, held):
    return [held] + [grid.swap_dp(held, h << 1) for h in range(1, grid.nh)]


def xy_gather_early(grid, held):
    return [held] + [grid.swap_dp(held, h << 1) for h in range(1, grid.nh - 1)]


def xy_gather_rest(grid, held):
    return [grid.swap_dp(held, grid.nh - 1 << 1)]


def core_sum(grid, keep, got):
    shape = (grid.nh, grid.nf) + keep.shape[1:]
    keep, got = keep.reshape(shape), got.reshape(shape)
    kind = keep.dtype
    sends = [(keep[h].astype(F32) + got[h].astype(F32)).astype(kind) for h in range(1, grid.nh)]
    return [keep[0], got[0]], sends


def xy_scatter(grid, sends):
    return [grid.swap_dp(s, h << 1) for h, s in zip(range(1, grid.nh), sends)]


def xy_sum(grid, parts, z):
    out = parts[0][z].astype(F32)
    for part in parts[1:]:
        out = out + part[z].astype(F32)
    return out


class Piece:
    def __init__(self, grid, forms, plain=False, across=False):
        self.grid, self.forms, self.plain, self.across = grid, forms, plain, across
        self.starts = [sum(b for b, _ in forms[:k]) for k in range(len(forms))]
        self.blocks = sum(b for b, _ in forms)
        self.refs = 1 if plain or not grid.tiled else 2

    def cut(self, k):
        blocks, wide = self.forms[k]
        a, b = self.grid.cut
        return (a, blocks, b, 512) if wide is False else (blocks, a, b, 512)

    def arrive(self, *held):
        grid = self.grid
        if grid.tiled:
            shape = (-1, self.blocks, grid.unit, 512)
            self.arrays = [tuple(near_not(h.reshape(shape)) for h in held)] * len(self.forms)
            return
        whole = jnp.concatenate(held)
        if not self.plain:
            spots = [
                grid.spot(grid.me(), part, at, self.across)
                for part in range(2)
                for at in range(grid.hz)
            ]
            index = jnp.zeros((grid.n,), jnp.int32).at[jnp.stack(spots)].set(
                jnp.arange(grid.n, dtype=jnp.int32)
            )
            whole = jnp.take(whole, index, axis=0)
        self.arrays = []
        for k, (blocks, wide) in enumerate(self.forms):
            row = self.starts[k] * grid.unit
            part = whole[:, row : row + blocks * grid.unit]
            if wide is not False:
                part = part.reshape(grid.n, blocks, grid.unit, 512).transpose(1, 0, 2, 3)
            self.arrays.append((part.reshape(self.cut(k)),))

    def pairs(self, k, me, refs, held):
        grid = self.grid
        blocks, wide = self.forms[k]
        start = self.starts[k]
        if not grid.tiled:
            yield refs[0 if len(refs) == 1 else k], held
        elif self.plain and wide is not False:
            for j in range(blocks):
                yield refs[0].at[:, start + j], held.at[j]
        elif self.plain:
            yield refs[0].at[:, pl.ds(start, blocks)], held
        else:
            for part, ref in enumerate(refs):
                for at in range(grid.hz):
                    i = grid.spot(me, part, at, self.across)
                    yield ref.at[at, pl.ds(start, blocks)], held.at[i] if wide is False else held.at[:, i]

    def fetch(self, k, me, refs, dst, sem):
        for there, here in self.pairs(k, me, refs, dst):
            pltpu.make_async_copy(there, here, sem).start()

    def store(self, k, me, src, refs, sem):
        for there, here in self.pairs(k, me, refs, src):
            pltpu.make_async_copy(here, there, sem).start()

    def out_shapes(self):
        grid = self.grid
        if not grid.tiled:
            return [jax.ShapeDtypeStruct(self.cut(k), BF) for k in range(len(self.forms))]
        if self.plain:
            return [jax.ShapeDtypeStruct((grid.n, self.blocks, grid.unit, 512), BF)]
        return [jax.ShapeDtypeStruct((grid.hz, self.blocks, grid.unit, 512), BF)] * 2

    def ready(self, outs):
        grid = self.grid
        rows = self.blocks * grid.unit
        if grid.tiled:
            return [out.reshape(-1, rows, 512) for out in outs]
        parts = []
        for k, (blocks, wide) in enumerate(self.forms):
            part = outs[k]
            if wide is not False:
                part = part.reshape(blocks, grid.n, grid.unit, 512).transpose(1, 0, 2, 3)
            parts.append(part.reshape(grid.n, blocks * grid.unit, 512))
        whole = jnp.concatenate(parts, axis=1)
        return [whole] if self.plain else spread_blocks(grid, whole)


def scatter_plain(grid, whole):
    rows = whole.shape[1]
    part = lax.psum_scatter(
        whole.reshape(grid.nd, grid.nf * rows, 512), "dp", scatter_dimension=0, tiled=False
    )
    return lax.psum_scatter(
        part.reshape(grid.nf, rows, 512), "fsdp", scatter_dimension=0, tiled=False
    )


def spread_blocks(grid, whole):
    sides = []
    for part in range(2):
        table = [grid.relative(part, at) for at in range(grid.hz)]
        sides.append(jnp.take(whole, jnp.array(table, jnp.int32) ^ grid.me(), axis=0))
    return sides


def finish(ref, sem):
    pltpu.make_async_copy(ref, ref, sem).wait()


def to_rows(shard):
    unit = shard.shape[0]
    blocks = shard.shape[1] // 512
    return shard.reshape(unit, blocks, 512).transpose(1, 0, 2).reshape(blocks * unit, 512)


def fours(rows, start, width):
    k = lax.broadcasted_iota(jnp.int32, (4 * rows, width), 0)
    return lax.broadcasted_iota(jnp.int32, (4 * rows, width), 1) == start + lax.rem(k, 4)


def own_row(rows):
    k = lax.broadcasted_iota(jnp.int32, (rows, 4 * rows), 1)
    return lax.broadcasted_iota(jnp.int32, (rows, 4 * rows), 0) == k // 4


def flatten_fours(value, start):
    rows = value.shape[0]
    wide = lax.dot_general(
        value,
        fours(rows, start, 128).astype(F32),
        (((1,), (1,)), ((), ())),
        precision=lax.Precision.HIGHEST,
        preferred_element_type=F32,
    )
    return jnp.sum(jnp.where(own_row(rows), wide, 0.0), axis=0, keepdims=True)


def place_small(parts, rows):
    total = None
    for (start, width), part in zip(SMALL, parts):
        value = part[...]
        if width == 4:
            value = jnp.where(own_row(rows), value.astype(F32), 0.0).astype(BF)
            spots = fours(rows, start, 512)
        else:
            r = lax.broadcasted_iota(jnp.int32, (width, 512), 0)
            spots = lax.broadcasted_iota(jnp.int32, (width, 512), 1) == start + r
        value = jnp.dot(value, jnp.where(spots, 1.0, 0.0).astype(BF), preferred_element_type=F32)
        total = value if total is None else total + value
    return total.astype(BF)


def pack_kernel(counts, unit, *refs):
    refs = list(refs)
    small = [refs.pop(0) for _ in SMALL]
    groups = [[refs.pop(0) for _ in range(count)] for count in counts]
    refs[0][4 * unit : 5 * unit] = place_small(small, unit)
    for group, out in zip(groups, refs):
        at = 0
        for ref in group:
            rows = ref.shape[0]
            for j in range(ref.shape[1] // 512):
                if out is refs[0] and at == 4 * unit:
                    at += unit
                out[at : at + rows] = ref[:, 512 * j : 512 * (j + 1)]
                at += rows


def pack(grid, small, *groups):
    if not grid.tiled:
        flat = [p.reshape(grid.unit, 4) if w == 4 else p for (_, w), p in zip(SMALL, small)]
        flat = jnp.concatenate(flat, axis=1)
        flat = jnp.pad(flat, ((0, 0), (0, 512 - flat.shape[1])))
        first, *rest = groups
        groups = [list(first[:2]) + [flat] + list(first[2:])] + rest
        return [
            jnp.concatenate([to_rows(a) if a.shape[0] == grid.unit else a for a in arrays])
            for arrays in groups
        ]
    rows = [sum(a.size for a in arrays) // 512 for arrays in groups]
    rows[0] += grid.unit
    flat = [p.reshape(1, -1) if w == 4 else p for (_, w), p in zip(SMALL, small)]
    return pl.pallas_call(
        functools.partial(pack_kernel, [len(arrays) for arrays in groups], grid.unit),
        out_shape=[like(r, 512, BF) for r in rows],
        compiler_params=params(56),
        name="pack",
    )(*flat, *[a for arrays in groups for a in arrays])


def shards_kernel(pieces, counts, *refs):
    refs = list(refs)
    own = [[refs.pop(0) for _ in range(count)] for count in counts[:-1]]
    lasts = [refs.pop(0) for _ in range(counts[-1])]
    at = 0
    for piece, parts in zip(pieces, own):
        rows = piece.blocks * piece.grid.unit
        total = None
        for part in parts:
            total = part[0].astype(F32) if total is None else total + part[0].astype(F32)
        for last in lasts:
            total = total + last[at : at + rows].astype(F32)
        at += rows
        row, unit = 0, piece.grid.unit
        for blocks, wide in piece.forms:
            if wide is None:
                value = total[row : row + unit]
                for start, width in SMALL:
                    out = refs.pop(0)
                    if width == 4:
                        out[...] = flatten_fours(value[:, :128], start)
                    else:
                        out[...] = value[:, start : start + width]
                row += unit
                continue
            out = refs.pop(0)
            for j in range(blocks):
                value = total[row : row + unit]
                if wide:
                    out[:, 512 * j : 512 * (j + 1)] = value
                else:
                    out[unit * j : unit * (j + 1)] = value
                row += unit


def shards(grid, pieces, own, lasts):
    if not grid.tiled:
        total = jnp.concatenate(
            [functools.reduce(lambda a, b: a + b, [p[0].astype(F32) for p in parts]) for parts in own]
        )
        for last in lasts:
            total = total + last.astype(F32)
        outs, row = [], 0
        for piece in pieces:
            for blocks, wide in piece.forms:
                part = total[row : row + blocks * grid.unit]
                if wide is None:
                    outs += [part[:, start : start + width] for start, width in SMALL]
                else:
                    outs.append(from_rows(part, blocks) if wide else part)
                row += blocks * grid.unit
        return outs
    first = lambda a: pl.BlockSpec((1,) + a.shape[1:], lambda i: (0, 0, 0))
    args = [a for parts in own for a in parts] + lasts
    specs = [first(a) for parts in own for a in parts] + [whole_spec(a) for a in lasts]
    shapes = []
    for piece in pieces:
        for blocks, wide in piece.forms:
            if wide is None:
                shapes += [
                    like(1, grid.unit * 4, F32) if width == 4 else like(grid.unit, width, F32)
                    for _, width in SMALL
                ]
            elif wide:
                shapes.append(like(grid.unit, 512 * blocks, F32))
            else:
                shapes.append(like(grid.unit * blocks, 512, F32))
    return pl.pallas_call(
        functools.partial(shards_kernel, pieces, [len(p) for p in own] + [len(lasts)]),
        grid=(1,),
        in_specs=specs,
        out_specs=[whole_spec(s) for s in shapes],
        out_shape=shapes,
        compiler_params=params(56),
        name="shards",
    )(*args)


def from_rows(rows, blocks):
    unit = rows.shape[0] // blocks
    return rows.reshape(blocks, unit, 512).transpose(1, 0, 2).reshape(unit, blocks * 512)


HALF = 64
BIG = float(2**30)


def dot(a, b):
    return jnp.dot(a, b, preferred_element_type=jnp.float32)


def dot_t(a, b):
    return lax.dot_general(a, b, (((1,), (1,)), ((), ())), preferred_element_type=jnp.float32)


def t_dot(a, b):
    return lax.dot_general(a, b, (((0,), (0,)), ((), ())), preferred_element_type=jnp.float32)


def lanes(rows=1, width=128):
    return lax.broadcasted_iota(jnp.int32, (rows, width), 1)


def head_lanes(h):
    return jnp.where(lanes() // HALF == h, 1.0, 0.0).astype(jnp.bfloat16)


def one_lanes(h):
    at = lanes() - HALF * h
    return jnp.where((at >= 8) & (at < 11), 1.0, 0.0).astype(jnp.bfloat16)


def minus_parts(value):
    at = lanes() % HALF
    value = -value
    high = value.astype(jnp.bfloat16).astype(jnp.float32)
    rest = value - high
    mid = rest.astype(jnp.bfloat16).astype(jnp.float32)
    low = rest - mid
    out = jnp.where(at == 8, high, jnp.where(at == 9, mid, jnp.where(at == 10, low, 0.0)))
    return out.astype(jnp.bfloat16)


def pair(value, p):
    return value[:, 128 * p : 128 * (p + 1)]


def norm(summed):
    centred = summed - jnp.mean(summed, axis=-1, keepdims=True)
    inverse = lax.rsqrt(jnp.mean(centred * centred, axis=-1, keepdims=True) + norm_eps)
    return centred * inverse, inverse


def heads_forward(q, k, v, hot, bar):
    outs, logs = [], []
    for p in range(q.shape[1] // 128):
        qa = jnp.concatenate([pair(q, p) * jnp.bfloat16(scale_dot), hot], axis=1)
        total, tops = None, []
        for h in (0, 1):
            mask = head_lanes(h)
            ka = jnp.concatenate([pair(k, p) * mask, bar], axis=1)
            scores = dot_t(qa, ka)
            top = jnp.max(scores, axis=-1, keepdims=True)
            power = jnp.exp(scores - top).astype(jnp.bfloat16)
            va = jnp.concatenate(
                [pair(v, p) * mask, jnp.broadcast_to(mask, (v.shape[0], 128))], axis=1
            )
            part = dot(power, va)
            total = part if total is None else total + part
            tops.append(top)
        sums = total[:, 128:]
        outs.append(total[:, :128] / sums)
        logs.append(minus_parts(jnp.where(lanes() < HALF, tops[0], tops[1]) + jnp.log(sums)))
    return jnp.concatenate(outs, axis=1), jnp.concatenate(logs, axis=1)


def heads_backward(go, q, k, v, o, lse, hot, bar):
    gqs, gks, gvs = [], [], []
    at = lax.broadcasted_iota(jnp.int32, (128, 128), 0) // HALF
    to = lax.broadcasted_iota(jnp.int32, (128, 128), 1) // HALF
    same = jnp.where(at == to, 1.0, 0.0).astype(jnp.bfloat16)
    same = jnp.concatenate([same, same], axis=0)
    for p in range(q.shape[1] // 128):
        qs = pair(q, p) * jnp.bfloat16(scale_dot)
        gp = pair(go, p)
        prod = gp.astype(jnp.float32) * pair(o, p)
        high = prod.astype(jnp.bfloat16)
        low = (prod - high.astype(jnp.float32)).astype(jnp.bfloat16)
        delta = dot(jnp.concatenate([high, low], axis=1), same)
        qa = jnp.concatenate([qs, hot + pair(lse, p)], axis=1)
        ga = jnp.concatenate([gp, minus_parts(delta)], axis=1)
        gq = gk = gv = None
        for h in (0, 1):
            mask, one = head_lanes(h), one_lanes(h)
            km = pair(k, p) * mask
            ka = jnp.concatenate([km, bar + one], axis=1)
            va = jnp.concatenate(
                [pair(v, p) * mask, jnp.broadcast_to(one, (v.shape[0], 128))], axis=1
            )
            probs = jnp.exp(dot_t(ka, qa))
            gs = (probs * dot_t(va, ga)).astype(jnp.bfloat16)
            gv_h = dot(probs.astype(jnp.bfloat16), gp * mask)
            gk_h = dot(gs, qs * mask)
            gq_h = t_dot(gs, km)
            gv = gv_h if gv is None else gv + gv_h
            gk = gk_h if gk is None else gk + gk_h
            gq = gq_h if gq is None else gq + gq_h
        gqs.append((gq * scale_dot).astype(jnp.bfloat16))
        gks.append(gk.astype(jnp.bfloat16))
        gvs.append(gv.astype(jnp.bfloat16))
    return tuple(jnp.concatenate(x, axis=1) for x in (gqs, gks, gvs))


def norm_back(grad, normed, inverse, gain):
    scaled = grad * gain
    back = inverse * (
        scaled
        - jnp.mean(scaled, axis=-1, keepdims=True)
        - normed * jnp.mean(scaled * normed, axis=-1, keepdims=True)
    )
    return back, jnp.sum(grad * normed, axis=0), jnp.sum(grad, axis=0)


def square(ref, k):
    return ref[k].reshape(512, 512)


def vec(vectors, k):
    return vectors[k : k + 1, :]


ANY = pl.BlockSpec(memory_space=pl.ANY)
SMEM = pl.BlockSpec(memory_space=pltpu.SMEM)


def whole_spec(array):
    return pl.BlockSpec(array.shape, lambda i: (0,) * array.ndim)


def row_spec(array):
    return pl.BlockSpec((ROW,) + array.shape[1:], lambda i: (i,) + (0,) * (array.ndim - 1))


def near_not(array):
    return pltpu.with_memory_space_constraint(array, pltpu.HBM)


def far(shape):
    return pltpu.HBM(shape.shape, shape.dtype)


def like(rows, width, kind):
    return jax.ShapeDtypeStruct((rows, width), kind)


def params(mebibytes):
    return pltpu.CompilerParams(vmem_limit_bytes=mebibytes * 1024 * 1024)


def cost(tokens, macs):
    return pl.CostEstimate(
        flops=2 * tokens * macs, bytes_accessed=16 * tokens * 512, transcendentals=0
    )


def attend_forward_kernel(mode, base, piece, small, *refs):
    refs = list(refs)
    me_ref = refs.pop(0)
    count = piece.refs
    take = lambda k: [refs.pop(0) for _ in range(k)]
    proj_refs = [take(count) for _ in range(3 if mode == "cross" else 2)]
    small_refs = take(count) if small is not None else None
    vectors_ref = None if small is not None else refs.pop(0)
    if mode == "cross":
        normed_ref, memory_ref = take(2)
    else:
        x_ref = refs.pop(0)
        if mode == "dec":
            lang_ref = refs.pop(0)
    hot_ref, bar_ref = take(2)
    q_out, k_out, v_out, o_out, lse_out, n_out, inv_out = take(7)
    if mode != "enc":
        low_out = refs.pop(0)
    if small is not None:
        vectors_out, small_out = take(2)
    weights = take(3 if mode == "cross" else 2)
    small_scr = refs.pop(0) if small is not None else None
    sems = refs.pop(0)
    out_w = weights[-1]

    @pl.when(pl.program_id(0) == 0)
    def _():
        me = me_ref[0]
        if small is not None:
            piece.fetch(small, me, small_refs, small_scr, sems.at[3])
        for k, (source, dst) in enumerate(zip(proj_refs, weights)):
            piece.fetch(k, me, source, dst, sems.at[k])
        if small is not None:
            finish(small_scr, sems.at[3])
            block = small_scr[0].reshape(512, 512)[:, :128]
            small_out[...] = block
            vectors_out[...] = block.astype(F32).T
        for k, dst in enumerate(weights[:-1]):
            finish(dst, sems.at[k])

    vectors = (vectors_out if small is not None else vectors_ref)[...]
    if mode == "enc":
        low = x_ref[...]
        residual = low.astype(F32)
        memory = low
    elif mode == "dec":
        residual = x_ref[...].astype(F32) + dot(lang_ref[...], vectors.astype(BF))
        low = memory = residual.astype(BF)
    else:
        residual = normed_ref[...] * vec(vectors, DEC + 3) + vec(vectors, DEC + 4)
        low = residual.astype(BF)
        memory = memory_ref[...]
    if mode != "enc":
        low_out[...] = low
    if mode == "cross":
        wq, wk, wv = square(weights[0], 0), square(weights[1], 0), square(weights[1], 1)
    else:
        wq, wk, wv = (square(weights[0], j) for j in range(3))
    q = (dot(low, wq) + vec(vectors, base)).astype(BF)
    k = dot(memory, wk).astype(BF)
    v = (dot(memory, wv) + vec(vectors, base + 1)).astype(BF)
    q_out[...], k_out[...], v_out[...] = q, k, v
    o, lse = heads_forward(q, k, v, hot_ref[...], bar_ref[...])
    o_out[...], lse_out[...] = o, lse

    @pl.when(pl.program_id(0) == 0)
    def _():
        finish(out_w, sems.at[len(weights) - 1])

    branch = dot(o.astype(BF), square(out_w, 0)) + vec(vectors, base + 2)
    n_out[...], inv_out[...] = norm(residual + branch)


def attend_forward(mode, base, me, piece, small, inputs, hot, bar, vectors):
    grid = piece.grid
    tokens = hot.shape[0]
    names = range(3 if mode == "cross" else 2)
    weights = [a for k in names for a in piece.arrays[k]]
    args = [me] + weights
    specs = [SMEM] + [ANY] * len(weights)
    if small is not None:
        args += list(piece.arrays[small])
        specs += [ANY] * len(piece.arrays[small])
    else:
        args.append(vectors)
        specs.append(whole_spec(vectors))
    rows = [near_not(inputs[0])] + list(inputs[1:]) + [hot, bar]
    args += rows
    specs += [row_spec(a) for a in rows]
    outs = [like(tokens, 512, BF)] * 3 + [like(tokens, 512, F32), like(tokens, 512, BF)]
    outs += [like(tokens, 512, F32), like(tokens, 1, F32)]
    if mode != "enc":
        outs.append(like(tokens, 512, BF))
    out_specs = [row_spec(o) for o in outs]
    outs = [o if i == 5 and mode == "cross" else far(o) for i, o in enumerate(outs)]
    scratch = [pltpu.VMEM(piece.cut(k), BF) for k in names]
    if small is not None:
        extra = [like(128, 512, F32), like(512, 128, BF)]
        outs += extra
        out_specs += [whole_spec(e) for e in extra]
        scratch.append(pltpu.VMEM(piece.cut(small), BF))
    scratch.append(pltpu.SemaphoreType.DMA((4,)))
    return pl.pallas_call(
        functools.partial(attend_forward_kernel, mode, base, piece, small),
        grid=(tokens // ROW,),
        in_specs=specs,
        out_specs=out_specs,
        out_shape=outs,
        scratch_shapes=scratch,
        compiler_params=params(24),
        cost_estimate=cost(tokens, 4 * 512 * 512 + 2 * 8 * 512 * 256),
        name="attend_forward_" + mode,
    )(*args)


def feed_forward_kernel(base, first, piece, own, *refs):
    refs = list(refs)
    me_ref = refs.pop(0)
    count = piece.refs
    take = lambda k: [refs.pop(0) for _ in range(k)]
    up_refs, down_refs = take(count), take(count)
    vectors_ref, bias_ref, n_ref = take(3)
    act_out, slope_out, n_out, inv_out, low_out = take(5)
    up, down, sems = take(3)

    @pl.when(pl.program_id(0) == 0)
    def _():
        me = me_ref[0]
        piece.fetch(own, me, up_refs, up, sems.at[0])
        piece.fetch(own + 1, me, down_refs, down, sems.at[1])
        finish(up, sems.at[0])
        finish(down, sems.at[1])

    vectors = vectors_ref[...]
    x = n_ref[...] * vec(vectors, first) + vec(vectors, first + 1)
    low = x.astype(BF)
    branch = None
    for j in range(4):
        h = dot(low, square(up, j)) + bias_ref[j : j + 1, :]
        act, slope = gate(h)
        act = act.astype(BF)
        act_out[j], slope_out[j] = act, slope.astype(BF)
        part = dot(act, tall(down, j))
        branch = part if branch is None else branch + part
    n, inv = norm(x + branch + vec(vectors, base))
    n_out[...], inv_out[...] = n, inv
    low_out[...] = (n * vec(vectors, base + 1) + vec(vectors, base + 2)).astype(BF)


def gate(h):
    c = 0.7978845608028654
    square_h = h * h
    t = jnp.tanh(h * (c + (c * 0.044715) * square_h))
    half = 0.5 + 0.5 * t
    slope = half + (0.5 * h) * (1.0 - t * t) * (c + (3.0 * c * 0.044715) * square_h)
    return h * half, slope


def tall(ref, j):
    size = ref.shape[0] // 4
    return ref[size * j : size * (j + 1)].reshape(512, 512)


def feed_forward(base, first, me, piece, own, vectors, bias, n):
    tokens = n.shape[0]
    weights = list(piece.arrays[own]) + list(piece.arrays[own + 1])
    chunk = jax.ShapeDtypeStruct((4, tokens, 512), BF)
    chunk_spec = pl.BlockSpec((4, ROW, 512), lambda i: (0, i, 0))
    outs = [chunk, chunk, like(tokens, 512, F32), like(tokens, 1, F32), like(tokens, 512, BF)]
    out_specs = [chunk_spec, chunk_spec] + [row_spec(o) for o in outs[2:]]
    outs = [far(o) for o in outs[:4]] + outs[4:]
    return pl.pallas_call(
        functools.partial(feed_forward_kernel, base, first, piece, own),
        grid=(tokens // ROW,),
        in_specs=[SMEM]
        + [ANY] * len(weights)
        + [whole_spec(vectors), whole_spec(bias), row_spec(n)],
        out_specs=out_specs,
        out_shape=outs,
        scratch_shapes=[
            pltpu.VMEM(piece.cut(own), BF),
            pltpu.VMEM(piece.cut(own + 1), BF),
            pltpu.SemaphoreType.DMA((2,)),
        ],
        compiler_params=params(26),
        cost_estimate=cost(tokens, 8 * 512 * 512),
        name="feed_forward",
    )(me, *weights, vectors, bias, near_not(n))


def feed_backward_kernel(base, first, piece, own, grads, at, *refs):
    refs = list(refs)
    me_ref = refs.pop(0)
    count = piece.refs
    take = lambda k: [refs.pop(0) for _ in range(k)]
    up_refs, down_refs = take(count), take(count)
    vectors_ref, grad_ref, n2_ref, inv2_ref, n1_ref, act_ref, slope_ref = take(7)
    grad_outs = take(len(grads.out_shapes()))
    dx_out, sums_out, bias_out = take(3)
    up, down, d_up, d_down, low_t, branch, sems = take(7)
    j = pl.program_id(0)
    vectors = vectors_ref[...]

    @pl.when(j == 0)
    def _():
        me = me_ref[0]
        piece.fetch(own, me, up_refs, up, sems.at[0])
        piece.fetch(own + 1, me, down_refs, down, sems.at[1])
        sums_out[...] = jnp.zeros_like(sums_out)
        for t in range(grad_ref.shape[0] // ROW):
            part = pl.ds(ROW * t, ROW)
            back, gain, shift = norm_back(
                grad_ref[part].astype(F32), n2_ref[part], inv2_ref[part], vec(vectors, base + 1)
            )
            dx_out[part] = back
            low = back.astype(BF)
            branch[part] = low
            sums_out[0:1] += jnp.sum(low.astype(F32), axis=0, keepdims=True)
            sums_out[1:2] += gain[None]
            sums_out[2:3] += shift[None]
            x = n1_ref[part] * vec(vectors, first) + vec(vectors, first + 1)
            low_t[:, part] = x.astype(BF).T
        finish(up, sems.at[0])
        finish(down, sems.at[1])

    size = down.shape[0] // 4
    down_j = down[pl.ds(size * j, size)].reshape(512, 512)
    up_j = up[j].reshape(512, 512)
    low = branch[...]
    hidden = (dot_t(low, down_j) * slope_ref[0].astype(F32)).astype(BF)
    bias_out[0] = jnp.broadcast_to(
        jnp.sum(hidden.astype(F32), axis=0, keepdims=True), bias_out.shape[1:]
    )
    dx_out[...] += dot_t(hidden, up_j)
    d_up[j] = dot(low_t[...], hidden).astype(BF).reshape(d_up.shape[1:])
    d_down[pl.ds(size * j, size)] = (
        t_dot(act_ref[0], low).astype(BF).reshape((size,) + d_down.shape[1:])
    )

    @pl.when(j == pl.num_programs(0) - 1)
    def _():
        me = me_ref[0]
        grads.store(at, me, d_up, grad_outs, sems.at[0])
        grads.store(at + 1, me, d_down, grad_outs, sems.at[1])
        finish(d_up, sems.at[0])
        finish(d_down, sems.at[1])


def feed_backward(base, first, me, piece, own, grads, at, vectors, grad, n2, inv2, n1, act, slope):
    tokens = n1.shape[0]
    weights = list(piece.arrays[own]) + list(piece.arrays[own + 1])
    act, slope, n2, inv2, n1, grad = (near_not(a) for a in (act, slope, n2, inv2, n1, grad))
    held = [vectors, grad, n2, inv2, n1]
    chunk_spec = pl.BlockSpec((1, tokens, 512), lambda i: (i, 0, 0))
    outs = [like(tokens, 512, F32), like(8, 512, F32), jax.ShapeDtypeStruct((4, 8, 512), F32)]
    got = pl.pallas_call(
        functools.partial(feed_backward_kernel, base, first, piece, own, grads, at),
        grid=(4,),
        in_specs=[SMEM]
        + [ANY] * len(weights)
        + [whole_spec(a) for a in held]
        + [chunk_spec, chunk_spec],
        out_specs=[ANY] * len(grads.out_shapes())
        + [whole_spec(outs[0]), whole_spec(outs[1]), pl.BlockSpec((1, 8, 512), lambda i: (i, 0, 0))],
        out_shape=[far(s) for s in grads.out_shapes()] + [far(outs[0])] + outs[1:],
        scratch_shapes=[
            pltpu.VMEM(piece.cut(own), BF),
            pltpu.VMEM(piece.cut(own + 1), BF),
            pltpu.VMEM(grads.cut(at), BF),
            pltpu.VMEM(grads.cut(at + 1), BF),
            pltpu.VMEM((512, tokens), BF),
            pltpu.VMEM((tokens, 512), BF),
            pltpu.SemaphoreType.DMA((2,)),
        ],
        compiler_params=params(32),
        cost_estimate=cost(tokens, 16 * 512 * 512),
        name="feed_backward",
    )(me, *weights, *held, act, slope)
    m = len(grads.out_shapes())
    return got[:m], got[m], got[m + 1], got[m + 2][:, 0, :]


def feed_both_kernel(base, first, piece, own, grads, at, tiles, *refs):
    refs = list(refs)
    me_ref = refs.pop(0)
    take = lambda k: [refs.pop(0) for _ in range(k)]
    up_refs, down_refs = take(piece.refs), take(piece.refs)
    vectors_ref, bias_ref, n1_ref, grad_ref = take(4)
    grad_outs = take(len(grads.out_shapes()))
    low_out, dx_out, sums_out, bias_out = take(4)
    up, down, d_up, d_down, acts, slopes, low_t, branches, sems = take(9)
    step = pl.program_id(0)
    vectors = vectors_ref[...]

    @pl.when(step == 0)
    def _():
        me = me_ref[0]
        piece.fetch(own, me, up_refs, up, sems.at[0])
        piece.fetch(own + 1, me, down_refs, down, sems.at[1])
        sums_out[...] = jnp.zeros_like(sums_out)
        finish(up, sems.at[0])
        finish(down, sems.at[1])

    @pl.when(step < tiles)
    def _():
        x = n1_ref[...] * vec(vectors, first) + vec(vectors, first + 1)
        low = x.astype(BF)
        rows = pl.ds(pl.multiple_of(step * ROW, ROW), ROW)
        branch = None
        for j in range(4):
            h = dot(low, square(up, j)) + bias_ref[j : j + 1, :]
            act, slope = gate(h)
            act = act.astype(BF)
            acts[j, rows], slopes[j, rows] = act, slope.astype(BF)
            part = dot(act, tall(down, j))
            branch = part if branch is None else branch + part
        n, inv = norm(x + branch + vec(vectors, base))
        gain = vec(vectors, base + 1)
        low_out[...] = (n * gain + vec(vectors, base + 2)).astype(BF)
        back, d_gain, d_shift = norm_back(grad_ref[...].astype(F32), n, inv, gain)
        dx_out[rows] = back
        back = back.astype(BF)
        branches[rows] = back
        sums_out[0:1] += jnp.sum(back.astype(F32), axis=0, keepdims=True)
        sums_out[1:2] += d_gain[None]
        sums_out[2:3] += d_shift[None]
        low_t[:, rows] = low.T

    @pl.when(step >= tiles)
    def _():
        j = step - tiles
        size = down.shape[0] // 4
        low = branches[...]
        hidden = dot_t(low, down[pl.ds(size * j, size)].reshape(512, 512))
        hidden = (hidden * slopes[j].astype(F32)).astype(BF)
        bias_out[0] = jnp.broadcast_to(
            jnp.sum(hidden.astype(F32), axis=0, keepdims=True), bias_out.shape[1:]
        )
        dx_out[...] += dot_t(hidden, up[j].reshape(512, 512))
        d_up[j] = dot(low_t[...], hidden).astype(BF).reshape(d_up.shape[1:])
        d_down[pl.ds(size * j, size)] = (
            t_dot(acts[j], low).astype(BF).reshape((size,) + d_down.shape[1:])
        )

    @pl.when(step == pl.num_programs(0) - 1)
    def _():
        me = me_ref[0]
        grads.store(at, me, d_up, grad_outs, sems.at[0])
        grads.store(at + 1, me, d_down, grad_outs, sems.at[1])
        finish(d_up, sems.at[0])
        finish(d_down, sems.at[1])


def feed_both(base, first, me, piece, own, grads, at, vectors, bias, n1, grad):
    tokens = n1.shape[0]
    tiles = tokens // ROW
    weights = list(piece.arrays[own]) + list(piece.arrays[own + 1])
    tile_spec = pl.BlockSpec((ROW, 512), lambda i: (jnp.minimum(i, tiles - 1), 0))
    outs = [
        like(tokens, 512, BF),
        like(tokens, 512, F32),
        like(8, 512, F32),
        jax.ShapeDtypeStruct((4, 8, 512), F32),
    ]
    got = pl.pallas_call(
        functools.partial(feed_both_kernel, base, first, piece, own, grads, at, tiles),
        grid=(tiles + 4,),
        in_specs=[SMEM]
        + [ANY] * len(weights)
        + [whole_spec(vectors), whole_spec(bias), tile_spec, tile_spec],
        out_specs=[ANY] * len(grads.out_shapes())
        + [
            tile_spec,
            whole_spec(outs[1]),
            whole_spec(outs[2]),
            pl.BlockSpec((1, 8, 512), lambda i: (jnp.maximum(i - tiles, 0), 0, 0)),
        ],
        out_shape=[far(s) for s in grads.out_shapes()] + outs,
        scratch_shapes=[
            pltpu.VMEM(piece.cut(own), BF),
            pltpu.VMEM(piece.cut(own + 1), BF),
            pltpu.VMEM(grads.cut(at), BF),
            pltpu.VMEM(grads.cut(at + 1), BF),
            pltpu.VMEM((4, tokens, 512), BF),
            pltpu.VMEM((4, tokens, 512), BF),
            pltpu.VMEM((512, tokens), BF),
            pltpu.VMEM((tokens, 512), BF),
            pltpu.SemaphoreType.DMA((2,)),
        ],
        compiler_params=params(44),
        cost_estimate=cost(tokens, 24 * 512 * 512),
        name="feed_both",
    )(me, *weights, vectors, bias, n1, grad)
    m = len(grads.out_shapes())
    return got[:m], got[m], got[m + 1], got[m + 2], got[m + 3][:, 0, :]


def attend_backward_kernel(mode, base, piece, grads, first, shared, *refs):
    refs = list(refs)
    me_ref = refs.pop(0)
    count = piece.refs
    take = lambda k: [refs.pop(0) for _ in range(k)]
    kinds = 3 if mode == "cross" else 2
    weight_refs = [take(count) for _ in range(kinds)]
    vectors_ref, grad_ref, n_ref, inv_ref, q_ref, k_ref, v_ref, o_ref, lse_ref = take(9)
    hot_ref, bar_ref, low_ref = take(3)
    memory_ref = refs.pop(0) if mode == "cross" else None
    lang_ref = refs.pop(0) if mode == "dec" else None
    sum_refs = take(5) if mode == "enc" else None
    cols_ref = refs.pop(0) if mode == "enc" else None
    if shared:
        refs.pop(0)
    grad_outs = take(len(grads.out_shapes()))
    dx_out, sums_out = take(2)
    dm_out = refs.pop(0) if mode == "cross" else None
    lang_out = refs.pop(0) if mode == "dec" else None
    staged_kinds = 2 if mode == "dec" else 3
    weights, staged = take(kinds), take(staged_kinds)
    low_t, o_t, gqs, gks, gvs, gbs, sems = take(7)
    memory_t = refs.pop(0) if mode == "cross" else None
    all_sums = refs.pop(0) if mode == "enc" else None
    step = pl.program_id(0)
    vectors = vectors_ref[...]

    @pl.when(step == 0)
    def _():
        me = me_ref[0]
        for k, (source, dst) in enumerate(zip(weight_refs, weights)):
            piece.fetch(k, me, source, dst, sems.at[k])
        sums_out[...] = jnp.zeros_like(sums_out)
        if mode == "dec":
            lang_out[...] = jnp.zeros_like(lang_out)

    back, gain, shift = norm_back(
        grad_ref[...], n_ref[...], inv_ref[...], vec(vectors, base + 3)
    )
    gb = back.astype(BF)

    @pl.when(step == 0)
    def _():
        for k, dst in enumerate(weights):
            finish(dst, sems.at[k])

    go = dot_t(gb, square(weights[-1], 0)).astype(BF)
    q, k, v, o = q_ref[...], k_ref[...], v_ref[...], o_ref[...]
    gq, gk, gv = heads_backward(go, q, k, v, o, lse_ref[...], hot_ref[...], bar_ref[...])
    if mode == "cross":
        wq, wk, wv = square(weights[0], 0), square(weights[1], 0), square(weights[1], 1)
    else:
        wq, wk, wv = (square(weights[0], j) for j in range(3))
    dx = back + dot_t(gq, wq)
    dm = dot_t(gk, wk) + dot_t(gv, wv)
    if mode == "cross":
        dx_out[...] = dx
        dm_out[...] = dm
    else:
        dx = dx + dm
        dx_out[...] = dx.astype(BF)
    if mode == "dec":
        high = dx.astype(BF)
        rest = (dx - high.astype(F32)).astype(BF)
        hot_lang = lang_ref[...].T
        lang_out[...] += dot(hot_lang, high) + dot(hot_lang, rest)
    sums_out[0:1] += jnp.sum(gq.astype(F32), axis=0, keepdims=True)
    sums_out[1:2] += jnp.sum(gv.astype(F32), axis=0, keepdims=True)
    sums_out[2:3] += jnp.sum(gb.astype(F32), axis=0, keepdims=True)
    sums_out[3:4] += gain[None]
    sums_out[4:5] += shift[None]
    part = pl.ds(pl.multiple_of(step * ROW, ROW), ROW)
    gqs[part], gks[part], gvs[part], gbs[part] = gq, gk, gv, gb
    low_t[:, part] = low_ref[...].T
    o_t[:, part] = o.astype(BF).T
    if mode == "cross":
        memory_t[:, part] = memory_ref[...].T

    @pl.when(step == pl.num_programs(0) - 1)
    def _():
        me = me_ref[0]
        shape = staged[0].shape[1:]
        out_grad = dot(o_t[...], gbs[...]).astype(BF).reshape(shape)
        gq_grad = dot(low_t[...], gqs[...]).astype(BF).reshape(shape)
        kv_t = (memory_t if mode == "cross" else low_t)[...]
        gk_grad = dot(kv_t, gks[...]).astype(BF).reshape(shape)
        gv_grad = dot(kv_t, gvs[...]).astype(BF).reshape(shape)
        if mode == "cross":
            staged[0][0] = gq_grad
            staged[1][0], staged[1][1] = gk_grad, gv_grad
        else:
            staged[0][0], staged[0][1], staged[0][2] = gq_grad, gk_grad, gv_grad
        staged[kinds - 1][0] = out_grad
        if mode == "enc":
            all_sums[...] = jnp.zeros_like(all_sums)
            row = 0
            counts = (8, 5, 3, 5, 5, 3)
            for ref, count in zip([sum_refs[0], sums_out] + sum_refs[1:], counts):
                all_sums[row : row + count] = ref[:count]
                row += count
            block = (all_sums[...].T + cols_ref[...]).astype(BF)
            block = jnp.concatenate([block, jnp.zeros((512, 384), BF)], axis=1)
            staged[2][0] = block.reshape(shape)
        for k, src in enumerate(staged):
            grads.store(first + k, me, src, grad_outs, sems.at[k])
        for k, src in enumerate(staged):
            finish(src, sems.at[k])


def attend_backward(
    mode, base, me, piece, grads, first, vectors, grad, saved, hot, bar, low, extra, fixed=(), into=None
):
    q, k, v, o, lse, n, inv = (near_not(a) for a in saved)
    low = near_not(low)
    extra = [near_not(a) for a in extra]
    grad = grad if mode == "cross" else near_not(grad)
    tokens = hot.shape[0]
    kinds = range(3 if mode == "cross" else 2)
    weights = [a for i in kinds for a in piece.arrays[i]]
    rows = [grad, n, inv, q, k, v, o, lse, hot, bar, low] + list(extra)
    outs = [like(tokens, 512, F32 if mode == "cross" else BF), like(8, 512, F32)]
    out_specs = [row_spec(outs[0]), whole_spec(outs[1])]
    if mode == "cross":
        outs.append(far(like(tokens, 512, F32)))
        out_specs.append(row_spec(like(tokens, 512, F32)))
    if mode == "dec":
        outs.append(like(128, 512, F32))
        out_specs.append(whole_spec(outs[-1]))
    grad_shapes = grads.out_shapes()
    scratch = [pltpu.VMEM(piece.cut(i), BF) for i in kinds]
    scratch += [pltpu.VMEM(grads.cut(first + i), BF) for i in range(2 if mode == "dec" else 3)]
    scratch += [pltpu.VMEM((512, tokens), BF)] * 2 + [pltpu.VMEM((tokens, 512), BF)] * 4
    scratch.append(pltpu.SemaphoreType.DMA((3,)))
    if mode == "cross":
        scratch.append(pltpu.VMEM((512, tokens), BF))
    if mode == "enc":
        scratch.append(pltpu.VMEM((128, 512), F32))
    args = [me, *weights, vectors, *rows, *fixed]
    shared = [] if into is None else [into]
    got = pl.pallas_call(
        functools.partial(attend_backward_kernel, mode, base, piece, grads, first, bool(shared)),
        grid=(tokens // ROW,),
        in_specs=[SMEM]
        + [ANY] * len(weights)
        + [whole_spec(vectors)]
        + [row_spec(a) for a in rows]
        + [whole_spec(a) for a in fixed]
        + [ANY] * len(shared),
        input_output_aliases={len(args): 0} if shared else {},
        out_specs=[ANY] * len(grad_shapes) + out_specs,
        out_shape=[far(s) for s in grad_shapes] + [far(outs[0])] + outs[1:],
        scratch_shapes=scratch,
        compiler_params=params(42),
        cost_estimate=cost(tokens, 8 * 512 * 512 + 5 * 8 * 512 * 256),
        name="attend_backward_" + mode,
    )(*args, *shared)
    m = len(grad_shapes)
    return got[:m], got[m:]


def segment_marks(segments):
    flat = segments.reshape(-1)
    hot = flat[:, None] == jnp.arange(128, dtype=jnp.int32)[None, :]
    bar = jnp.where(~hot & (jnp.arange(128) < 8)[None, :], -BIG, 0.0)
    return hot.astype(BF), bar.astype(BF)


def language_marks(segments, language):
    picked = jnp.zeros_like(segments)
    for s in range(language.shape[1]):
        picked = jnp.where(segments == s, language[:, s : s + 1], picked)
    flat = picked.reshape(-1)
    return (flat[:, None] == jnp.arange(128, dtype=jnp.int32)[None, :]).astype(BF)


def layers(
    grid,
    source,
    target,
    source_segments,
    target_segments,
    target_language,
    cotangent,
    enc_qkv,
    enc_out,
    enc_up,
    enc_down,
    enc_vecs,
    enc_bias_up,
    dec_qkv,
    dec_out,
    cross_q,
    cross_kv,
    cross_out,
    dec_up,
    dec_down,
    dec_vecs,
    dec_bias_up,
    lang_table,
):
    unit = enc_qkv.shape[0]
    feed_forms = [(4, True), (4, False)]
    self_forms = [(3, True), (1, True)]
    cross_forms = [(1, True), (2, True), (1, True)]
    enc_self = Piece(grid, self_forms + [(1, True)])
    dec_self = Piece(grid, self_forms)
    enc_feed = Piece(grid, feed_forms)
    late = Piece(grid, cross_forms + feed_forms, plain=True)
    rows01, rows2, rows3 = pack(
        grid,
        [lang_table, enc_vecs, dec_vecs, enc_bias_up, dec_bias_up],
        [enc_qkv, enc_out, dec_qkv, dec_out],
        [enc_up, enc_down],
        [cross_q, cross_kv, cross_out, dec_up, dec_down],
    )
    held = jnp.stack(z_gather(grid, rows01))
    held0, held1 = held[:, : 5 * unit], held[:, 5 * unit :]
    held2 = z_gather_halves(grid, after(rows2, held1))
    late.arrive(lax.all_gather(rows3, AXES, axis=0, tiled=False))
    held0 = jnp.concatenate(xy_gather(grid, held0), axis=0)
    held0, held2 = after((held0, held2), held1)
    enc_self.arrive(held0, grid.swap_dp(held0, 1))
    held1, held2 = after((held1, held2), held0[0])
    parts1 = xy_gather(grid, held1)
    parts2 = xy_gather_early(grid, held2)

    me = grid.me().astype(jnp.int32).reshape(1)
    source_hot, source_bar = segment_marks(source_segments)
    target_hot, target_bar = segment_marks(target_segments)
    lang = language_marks(target_segments, target_language)

    *enc_saved, vectors, columns = attend_forward(
        "enc", ENC, me, enc_self, 2, (source,), source_hot, source_bar, None
    )
    token = enc_saved[6]
    held1 = jnp.concatenate(after(parts1, token), axis=0)
    dec_self.arrive(held1, grid.swap_dp(held1, 1))
    parts2 = parts2 + xy_gather_rest(grid, after(held2, token))
    enc_bias = columns[:, ENC_UP:DEC_UP].astype(F32).reshape(4, 512)
    dec_bias = columns[:, DEC_UP : DEC_UP + 4].astype(F32).reshape(4, 512)
    *dec_saved, target_low = attend_forward(
        "dec", DEC, me, dec_self, None, (target, lang), target_hot, target_bar, vectors
    )
    held2 = jnp.concatenate(after(parts2, dec_saved[6]), axis=0)
    enc_feed.arrive(held2, grid.swap_dp(held2, 1))
    enc_act, enc_slope, enc_n, enc_inv, encoded = feed_forward(
        ENC + 5, ENC + 3, me, enc_feed, 0, vectors, enc_bias, enc_saved[5]
    )
    *cross_saved, first_low = attend_forward(
        "cross", DEC + 5, me, late, None, (dec_saved[5], encoded), target_hot, source_bar, vectors
    )
    late_back = Piece(grid, cross_forms + feed_forms, plain=True)
    enc_feed_back = Piece(grid, feed_forms)
    dec_back = Piece(grid, self_forms)
    enc_back = Piece(grid, self_forms + [(1, None)])
    outs, dec_output, grad_second, dec_feed_sums, dec_bias_grad = feed_both(
        DEC + 10, DEC + 8, me, late, 3, late_back, 3, vectors, dec_bias, cross_saved[5], cotangent
    )
    shared = outs[0] if grid.tiled else None
    late_outs, (grad_first, cross_sums, grad_encoded) = attend_backward(
        "cross", DEC + 5, me, late, late_back, 0, vectors, grad_second, cross_saved,
        target_hot, source_bar, first_low, (encoded,), into=shared,
    )
    if not grid.tiled:
        late_outs = list(late_outs[:3]) + list(outs[3:])
    late_total = scatter_plain(grid, *late_back.ready(late_outs))

    outs, grad_enc_first, enc_feed_sums, enc_bias_grad = feed_backward(
        ENC + 5, ENC + 3, me, enc_feed, 0, enc_feed_back, 0, vectors, grad_encoded, enc_n, enc_inv,
        enc_saved[5], enc_act, enc_slope,
    )
    keep2, send2 = enc_feed_back.ready(outs)
    got2 = grid.swap_dp(send2, 1)
    grad_first = after(grad_first, enc_feed_sums)
    outs, (target_grad, dec_sums, lang_grad) = attend_backward(
        "dec", DEC, me, dec_self, dec_back, 0, vectors, grad_first, dec_saved,
        target_hot, target_bar, target_low, (lang,),
    )
    keep3, send3 = dec_back.ready(outs)
    got3 = grid.swap_dp(send3, 1)
    got2 = after(got2, dec_sums)
    held2, sends = core_sum(grid, keep2, got2)
    parts2 = xy_scatter(grid, sends)
    cols = jnp.concatenate([enc_bias_grad.reshape(512, 4), dec_bias_grad.reshape(512, 4)], axis=1)
    cols = jnp.pad(cols, ((0, 0), (ENC_UP, 128 - ENC_UP - 8)))
    grad_enc_first = after(grad_enc_first, got2)
    outs, (source_grad, enc_sums) = attend_backward(
        "enc", ENC, me, enc_self, enc_back, 0, vectors, grad_enc_first, enc_saved,
        source_hot, source_bar, source, (), fixed=(lang_grad, enc_feed_sums, dec_sums, cross_sums, dec_feed_sums, cols),
    )
    keep4, send4 = enc_back.ready(outs)
    got3, parts2 = after((got3, parts2), enc_sums)
    got4 = grid.swap_dp(after(send4, (parts2, got3)), 1)
    held3, sends = core_sum(grid, keep3, got3)
    parts3 = xy_scatter(grid, sends)
    held4, sends = core_sum(grid, keep4, got4)
    parts3 = after(parts3, sends)
    parts4 = xy_scatter(grid, sends)

    def last_swaps(*pieces):
        kind = pieces[0][0].dtype
        sends = [
            jnp.concatenate([xy_sum(grid, p, z).astype(kind) for p in pieces])
            for z in range(1, grid.nf)
        ]
        return [grid.swap_fsdp(s, z) for z, s in zip(range(1, grid.nf), sends)]

    all2, all3, all4 = held2 + parts2, held3 + parts3, held4 + parts4
    enc_up_grad, enc_down_grad, dec_qkv_grad, dec_out_grad = shards(
        grid, [enc_feed_back, dec_back], [all2, all3], last_swaps(all2, all3)
    )
    cross_q_grad, cross_kv_grad, cross_out_grad, dec_up_grad, dec_down_grad = shards(
        grid, [late_back], [[late_total[None]]], []
    )
    all4 = after(all4, cross_q_grad)
    enc_qkv_grad, enc_out_grad, *rest = shards(grid, [enc_back], [all4], last_swaps(all4))

    return (
        dec_output,
        source_grad,
        target_grad,
        enc_qkv_grad,
        enc_out_grad,
        enc_up_grad,
        enc_down_grad,
        rest[1],
        rest[3].reshape(-1),
        dec_qkv_grad,
        dec_out_grad,
        cross_q_grad,
        cross_kv_grad,
        cross_out_grad,
        dec_up_grad,
        dec_down_grad,
        rest[2],
        rest[4].reshape(-1),
        rest[0],
    )


def solution(mesh):
    split = P(("dp", "fsdp"))
    return jax.shard_map(
        functools.partial(layers, Grid(mesh)),
        mesh=mesh,
        in_specs=(split,) * 22,
        out_specs=(split,) * 19,
        check_vma=False,
    )
```
